256 devices in a mesh: lat: 8 (over y, x_hi), lon: 32 (over x_lo, z, core).
Axes of the slice: x: 4 (x_hi: 2, x_lo: 2; x = x_hi * 2 + x_lo), y: 4, z: 8, core: 2. Of those that a mesh axis runs over, the one named last changes fastest.
Arguments:
- inputs: bfloat16 [4, 48, 384, 384], P(None, 'lat', 'lon'), may hold values from -60 to 60
- cotangent: bfloat16 [4, 48, 384, 384], P(None, 'lat', 'lon'), may hold values from -6 to 6
- land_sea: int32 [48, 384], P('lat', 'lon'), may hold values from 0 to 3
- rel_index: int32 [144, 144], replicated, may hold values from 0 to 758, as said below
- norm_gain: float32 [384], replicated, may hold values from 0.1 to 1.9
- norm_shift: float32 [384], replicated, may hold values from -3 to 3
- w_qkv: bfloat16 [384, 1152], replicated, may hold values from -0.3125 to 0.3125
- b_qkv: float32 [1152], replicated, may hold values from -3 to 3
- w_proj: bfloat16 [384, 384], replicated, may hold values from -0.3125 to 0.3125
- pos_bias: float32 [16, 12, 759], replicated, may hold values from -6 to 330
- surf_bias: float32 [12, 4, 4], replicated, may hold values from -4 to 4
Outputs:
- grad_inputs: bfloat16 [4, 48, 384, 384], P(None, 'lat', 'lon')
- grad_wqkv: float32 [384, 1152], replicated
- grad_bqkv: float32 [1152], replicated
- grad_wproj: float32 [384, 384], replicated
- grad_bproj: float32 [384], replicated
- grad_gain: float32 [384], replicated
- grad_shift: float32 [384], replicated
- grad_pos_bias: float32 [16, 12, 759], replicated
- grad_surf_bias: float32 [12, 4, 4], replicated
The draws below stay inside these ranges and needn't reach their ends.
Inputs may be any that keep to these rules, and one draw needn't show every extreme that they name: rel_index gives every pair of tokens of a window its relative offset in levels, rows and columns as a slot: pairs with the same offset share a slot and pairs with different offsets have different slots.
All inputs are finite; a program needn't handle non-finite values.
Results may differ from the reference program's by a relative error of at most 0.015.
Values may be sent and summed in bfloat16 or wider, within the bound.
A program may use at most 64 MiB of HBM per device.

```python
import jax
import jax.numpy as jnp
from jax import lax

C = 384
HEADS = 12
WLEV = 2
WLAT = 6
WLON = 12
SURF = 4
LEV = 4
WT = 144
NREL = 759
NLAT = 48
NLON = 384
TYPES = 16


def draw_inputs(key, part):
    key = jax.random.fold_in(key, 3)
    base_key = jax.random.fold_in(key, 0)
    full_shape = (LEV, NLAT, NLON, C)
    base = jax.random.normal(base_key, full_shape, jnp.float32)
    return jnp.clip(base, -60.0, 60.0).astype(jnp.bfloat16)


def draw_rel_index(key, part):
    key = jax.random.fold_in(key, 7)
    token_ids = jnp.arange(WT, dtype=jnp.int32)
    lev_pos = token_ids // (WLAT * WLON)
    lat_pos = token_ids // WLON % WLAT
    lon_pos = token_ids % WLON
    lev_off = lev_pos[:, None] - lev_pos[None, :] + WLEV - 1
    lat_off = lat_pos[:, None] - lat_pos[None, :] + WLAT - 1
    lon_off = lon_pos[:, None] - lon_pos[None, :] + WLON - 1
    geometry = (lev_off * (2 * WLAT - 1) + lat_off) * (2 * WLON - 1) + lon_off
    shuffle = jax.random.permutation(key, NREL).astype(jnp.int32)
    return jnp.take(shuffle, geometry).astype(jnp.int32)


def draw_pos_bias(key, part):
    key = jax.random.fold_in(key, 11)
    base_key = jax.random.fold_in(key, 0)
    base = jnp.clip(jax.random.normal(base_key, (TYPES, HEADS, NREL), jnp.float32), -6.0, 6.0)
    return base


def place_ends(values, stream_key, smallest, top_value):
    shape = values.shape
    place = [jax.random.randint(jax.random.fold_in(stream_key, axis), (), 0, shape[axis]) for axis in range(len(shape))]
    values = values.at[tuple(place)].set(smallest)
    longest = shape.index(max(shape))
    place[longest] = (place[longest] + 1) % shape[longest]
    return values.at[tuple(place)].set(top_value)


def shard_levels(own_key, extent, pieces, low, top_value):
    loudness, own = 1.0, jax.random.fold_in(own_key, 6)
    for dim, parts in pieces:
        steps = jnp.exp(jax.random.uniform(jax.random.fold_in(own, dim), (parts,), jnp.float32, low / len(pieces), top_value / len(pieces)))
        loudness = loudness * jnp.repeat(steps, extent[dim] // parts).reshape([-1 if axis == dim else 1 for axis in range(len(extent))])
    return loudness


def scatter_about(stream_key, extent, scale, limit, shards=(), held_as=jnp.bfloat16):
    values = scale * jax.random.normal(stream_key, extent, jnp.float32)
    if shards:
        values = values * shard_levels(stream_key, extent, shards, -0.22, 0.18)
    return jnp.clip(values, -limit, limit).astype(held_as)


def setup_inputs(seed: int = 0) -> dict:
    seeds = jax.random.split(jax.random.key(seed), 12)
    inputs = draw_inputs(jax.random.fold_in(seeds[11], 71), 0)
    cotangent = scatter_about(seeds[1], (LEV, NLAT, NLON, C), 1.0, 6.0, ((1, 8), (2, 32)))
    land_sea = place_ends(jax.random.randint(seeds[2], (NLAT, NLON), 0, SURF), jax.random.fold_in(seeds[2], 1), 0, SURF - 1).astype(jnp.int32)
    rel_index = draw_rel_index(jax.random.fold_in(seeds[11], 71), 0)
    norm_gain = jnp.clip(1.0 + 0.18 * jax.random.normal(seeds[4], (C,), jnp.float32), 0.1, 1.9)
    norm_shift = scatter_about(seeds[5], (C,), 0.5, 3.0, (), jnp.float32)
    w_qkv = scatter_about(seeds[6], (C, 3 * C), C ** -0.5, 0.3125)
    b_qkv = scatter_about(seeds[7], (3 * C,), 0.5, 3.0, (), jnp.float32)
    w_proj = scatter_about(seeds[8], (C, C), C ** -0.5, 0.3125)
    pos_bias = draw_pos_bias(jax.random.fold_in(seeds[11], 71), 0)
    surf_bias = scatter_about(seeds[10], (HEADS, SURF, SURF), 1.0, 4.0, (), jnp.float32)
    return {"inputs": inputs, "cotangent": cotangent, "land_sea": land_sea, "rel_index": rel_index, "norm_gain": norm_gain, "norm_shift": norm_shift, "w_qkv": w_qkv, "b_qkv": b_qkv, "w_proj": w_proj, "pos_bias": pos_bias, "surf_bias": surf_bias}


EPS = 1e-05
NEG_FILL = -1000000000.0

def layer_stats(block_data):
    as_float = block_data.astype(jnp.float32)
    centred = as_float - lax.optimization_barrier(jnp.mean(as_float, -1, keepdims=True))
    inv_std = lax.rsqrt(lax.optimization_barrier(jnp.mean(centred * centred, -1, keepdims=True)) + EPS)
    return (centred * inv_std, inv_std)

def to_windows(block_data):
    shape_in = block_data.shape
    tile_view = block_data.reshape(shape_in[0] // WLEV, WLEV, shape_in[1] // WLAT, WLAT, shape_in[2] // WLON, WLON, shape_in[3])
    tile_view = tile_view.transpose(0, 2, 4, 1, 3, 5, 6)
    return tile_view.reshape(-1, WT, shape_in[3])

def from_windows(windows, levels, lat_rows, lon_cols):
    channels = windows.shape[-1]
    tile_view = windows.reshape(levels // WLEV, lat_rows // WLAT, lon_cols // WLON, WLEV, WLAT, WLON, channels)
    return tile_view.transpose(0, 3, 1, 4, 2, 5, 6).reshape(levels, lat_rows, lon_cols, channels)

def token_labels(lev_label, lat_label):
    label_rows = lat_label.shape[0]
    joined = lev_label[None, :, None, None] * 2 + lat_label[:, None, :, None] + jnp.zeros((1, 1, 1, WLON), jnp.int32)
    return joined.reshape(label_rows, WT)

def surf_terms(onehot, surf_bias):
    side_terms = jnp.einsum('bqa,hac->bhqc', onehot, surf_bias, precision=lax.Precision.HIGHEST)
    return jnp.einsum('bhqc,bkc->bhqk', side_terms, onehot, precision=lax.Precision.HIGHEST)

def surf_grad(grad_scores, onehot):
    side_terms = jnp.einsum('bhqk,bkc->bhqc', grad_scores, onehot, precision=lax.Precision.HIGHEST)
    return jnp.einsum('bhqc,bqa->hac', side_terms, onehot, precision=lax.Precision.HIGHEST)

def table_grad(grad_sum, rel_index, slot_count):
    group_rows = grad_sum.shape[0]
    head_count = grad_sum.shape[1]
    flat_terms = grad_sum.reshape(group_rows * head_count, WT * WT).T
    summed = jax.ops.segment_sum(flat_terms, rel_index.reshape(-1), num_segments=slot_count)
    return summed.T.reshape(group_rows, head_count, slot_count)

def widen(values):
    return values.astype(jnp.float32)

def lower(values):
    return lax.optimization_barrier(values.astype(jnp.bfloat16))

def window_core(normed_win, grad_win, score_bias, allowed, w_qkv, b_qkv, w_proj):
    win_count, token_count, model_width = normed_win.shape
    head_count = score_bias.shape[-3]
    head_size = model_width // head_count
    score_scale = head_size ** (-0.5)
    flat_rows = normed_win.reshape(win_count * token_count, model_width)
    qkv_rows = lower(jnp.dot(flat_rows, w_qkv, preferred_element_type=jnp.float32) + b_qkv)
    qkv_rows = qkv_rows.reshape(win_count, token_count, 3, head_count, head_size)
    queries = widen(qkv_rows[:, :, 0])
    key_vecs = widen(qkv_rows[:, :, 1])
    value_vecs = widen(qkv_rows[:, :, 2])
    scores = jnp.einsum('bqhd,bkhd->bhqk', queries, key_vecs) * score_scale + score_bias
    scores = jnp.where(allowed, scores, NEG_FILL)
    top_score = lax.optimization_barrier(jnp.max(scores, -1, keepdims=True))
    exponent = jnp.exp(scores - top_score)
    attn_probs = exponent / lax.optimization_barrier(jnp.sum(exponent, -1, keepdims=True))
    probs_low = widen(lower(attn_probs))
    context = lower(jnp.einsum('bhqk,bkhd->bqhd', probs_low, value_vecs))
    context = context.reshape(win_count * token_count, model_width)
    grad_rows = grad_win.reshape(win_count * token_count, model_width)
    grad_context = lower(jnp.dot(grad_rows, w_proj.T, preferred_element_type=jnp.float32))
    grad_context = widen(grad_context).reshape(win_count, token_count, head_count, head_size)
    grad_wproj = jnp.dot(context.T, grad_rows, preferred_element_type=jnp.float32)
    grad_bproj = lax.optimization_barrier(jnp.sum(widen(grad_rows), 0))
    grad_probs = jnp.einsum('bqhd,bkhd->bhqk', grad_context, value_vecs)
    grad_values = jnp.einsum('bhqk,bqhd->bkhd', probs_low, grad_context)
    grad_scores = attn_probs * (grad_probs - lax.optimization_barrier(jnp.sum(grad_probs * attn_probs, -1, keepdims=True)))
    scores_low = widen(lower(grad_scores))
    grad_queries = jnp.einsum('bhqk,bkhd->bqhd', scores_low, key_vecs) * score_scale
    grad_keys = jnp.einsum('bhqk,bqhd->bkhd', scores_low, queries) * score_scale
    grad_qkv = jnp.stack([grad_queries, grad_keys, grad_values], 2).reshape(win_count * token_count, 3 * model_width)
    grad_bqkv = lax.optimization_barrier(jnp.sum(grad_qkv, 0))
    qkv_low = grad_qkv.astype(jnp.bfloat16)
    grad_wqkv = jnp.dot(flat_rows.T, qkv_low, preferred_element_type=jnp.float32)
    grad_normed = jnp.dot(qkv_low, w_qkv.T, preferred_element_type=jnp.float32).astype(jnp.bfloat16)
    grad_normed = grad_normed.reshape(win_count, token_count, model_width)
    return (grad_normed, grad_scores, grad_wqkv, grad_bqkv, grad_wproj, grad_bproj)

def reference(inputs, cotangent, land_sea, rel_index, norm_gain, norm_shift, w_qkv, b_qkv, w_proj, pos_bias, surf_bias):
    levels, lat_total, lon_total, model_width = inputs.shape
    head_count = surf_bias.shape[0]
    surf_kinds = surf_bias.shape[1]
    slot_count = pos_bias.shape[-1]
    lev_windows = levels // WLEV
    lat_windows = lat_total // WLAT
    offsets = (-(WLEV // 2), -(WLAT // 2), -(WLON // 2))
    rolled_x = jnp.roll(inputs, offsets, axis=(0, 1, 2))
    rolled_dy = jnp.roll(cotangent, offsets, axis=(0, 1, 2))
    rolled_ls = jnp.roll(land_sea, offsets[1:], axis=(0, 1))

    def group_step(totals, group_id):
        lat_w = group_id // lev_windows
        lev_w = group_id % lev_windows
        lev_start = (lev_w * WLEV).astype(jnp.int32)
        lat_start = (lat_w * WLAT).astype(jnp.int32)
        zero_index = jnp.zeros((), jnp.int32)
        x_block = lax.dynamic_slice(rolled_x, (lev_start, lat_start, zero_index, zero_index), (WLEV, WLAT, lon_total, model_width))
        dy_block = lax.dynamic_slice(rolled_dy, (lev_start, lat_start, zero_index, zero_index), (WLEV, WLAT, lon_total, model_width))
        ls_block = lax.dynamic_slice(rolled_ls, (lat_start, zero_index), (WLAT, lon_total))
        whitened, inv_std = layer_stats(x_block)
        normed = (whitened * norm_gain + norm_shift).astype(jnp.bfloat16)
        ls_windows = to_windows(jnp.broadcast_to(ls_block[None, :, :, None], (WLEV, WLAT, lon_total, 1)))[..., 0]
        onehot = (ls_windows[..., None] == jnp.arange(surf_kinds, dtype=jnp.int32)).astype(jnp.float32)
        lev_label = (lev_start + jnp.arange(WLEV, dtype=jnp.int32) == levels - 1).astype(jnp.int32)
        lat_orig = (lat_start + jnp.arange(WLAT, dtype=jnp.int32) + WLAT // 2) % lat_total
        lat_label = (lat_orig < WLAT // 2).astype(jnp.int32)[None]
        labels = token_labels(lev_label, lat_label)
        allowed = (labels[:, :, None] == labels[:, None, :])[:, None]
        pos_rows = lax.dynamic_slice_in_dim(pos_bias, group_id.astype(jnp.int32), 1, 0)
        pos_terms = jnp.take(pos_rows, rel_index, axis=2)
        score_bias = pos_terms + surf_terms(onehot, surf_bias)
        grad_norm_w, grad_scores, g_wqkv, g_bqkv, g_wproj, g_bproj = window_core(to_windows(normed), to_windows(dy_block), score_bias, allowed, w_qkv, b_qkv, w_proj)
        table_part = table_grad(lax.optimization_barrier(jnp.sum(grad_scores, 0, keepdims=True)), rel_index, slot_count)
        surf_part = surf_grad(grad_scores, onehot)
        grad_normed = from_windows(grad_norm_w, WLEV, WLAT, lon_total).astype(jnp.float32)
        gain_scaled = grad_normed * norm_gain
        first_mean = lax.optimization_barrier(jnp.mean(gain_scaled, -1, keepdims=True))
        second_mean = lax.optimization_barrier(jnp.mean(gain_scaled * whitened, -1, keepdims=True))
        grad_block = (dy_block.astype(jnp.float32) + inv_std * (gain_scaled - first_mean - whitened * second_mean)).astype(jnp.bfloat16)
        g_gain = lax.optimization_barrier(jnp.sum(grad_normed * whitened, (0, 1, 2)))
        g_shift = lax.optimization_barrier(jnp.sum(grad_normed, (0, 1, 2)))
        totals = (totals[0] + g_wqkv, totals[1] + g_bqkv, totals[2] + g_wproj, totals[3] + g_bproj, totals[4] + g_gain, totals[5] + g_shift, totals[6] + surf_part)
        return (totals, (grad_block, table_part[0]))
    start_totals = (jnp.zeros((model_width, 3 * model_width), jnp.float32), jnp.zeros((3 * model_width,), jnp.float32), jnp.zeros((model_width, model_width), jnp.float32), jnp.zeros((model_width,), jnp.float32), jnp.zeros((model_width,), jnp.float32), jnp.zeros((model_width,), jnp.float32), jnp.zeros((head_count, surf_kinds, surf_kinds), jnp.float32))
    group_ids = jnp.arange(lat_windows * lev_windows, dtype=jnp.int32)
    totals, outputs = lax.scan(group_step, start_totals, group_ids)
    grad_blocks, table_parts = outputs
    grad_blocks = grad_blocks.reshape(lat_windows, lev_windows, WLEV, WLAT, lon_total, model_width)
    grad_blocks = grad_blocks.transpose(1, 2, 0, 3, 4, 5).reshape(levels, lat_total, lon_total, model_width)
    grad_inputs = jnp.roll(grad_blocks, (WLEV // 2, WLAT // 2, WLON // 2), axis=(0, 1, 2))
    grad_scale = float(levels * lat_total * lon_total) ** (-0.5)
    return (grad_inputs, totals[0] * grad_scale, totals[1] * grad_scale, totals[2] * grad_scale, totals[3] * grad_scale, totals[4] * grad_scale, totals[5] * grad_scale, table_parts * grad_scale, totals[6] * grad_scale)
```

```python
import functools

import jax
import jax.numpy as jnp
import ml_dtypes
import numpy as np
from jax import lax
from jax.experimental import pallas as pl
from jax.experimental.pallas import tpu as pltpu
from jax.sharding import PartitionSpec as P

F32 = jnp.float32
BF16 = jnp.bfloat16
MESH = pl.DeviceIdType.MESH
EPS = 1e-05
LOG2E = 1.4426950408889634
BIG = 2.0**33
HEADS = 12
SLOTS = 759
WIDTH = 384
WT = 144
PITCH = 23
KEYS = 256
SCALE = 32.0**-0.5
NT = (((1,), (1,)), ((), ()))
TN = (((0,), (0,)), ((), ()))
NN = (((1,), (0,)), ((), ()))
PX, PY, PZ = 4, 4, 8
PLANE = PX * PY
VMEM = pl.BlockSpec(memory_space=pltpu.VMEM)


def dot(a, b, dims=NN):
    return lax.dot_general(a, b, dims, preferred_element_type=F32)


def quad_order():
    return [(li, q, r, c) for li in range(2) for q in range(4) for r in range(3) for c in range(6)]


def constants():
    order = quad_order()
    gather = np.zeros((576, 576), np.float32)
    back = np.zeros((320, 288), np.float32)
    for part in range(2):
        for w in range(2):
            for k, (li, q, r, c) in enumerate(order):
                row = part * 288 + w * 144 + k
                in_quad = (2 * w + li) * 18 + r * 6 + c
                gather[row, q * 144 + part * 72 + in_quad] = 1
                if part == 0:
                    back[q * 80 + in_quad, row] = 1
    spread = np.zeros((KEYS, WT), np.float32)
    cells = np.zeros((WT, 128), np.float32)
    for k, (li, q, r, c) in enumerate(order):
        spread[li * 128 + PITCH * (3 * (q // 2) + r) + 6 * (q % 2) + c, k] = 1
        cells[k, q * 32 + r * 6 + c] = 1
    spread_plain = np.zeros((KEYS, WT), np.float32)
    for k in range(WT):
        li, ri, ci = k // 72, k // 12 % 6, k % 12
        spread_plain[li * 128 + PITCH * ri + ci, k] = 1
    rows = np.array([[PITCH * (3 * (q // 2) + r) + 6 * (q % 2) + c] for li, q, r, c in order[:72]], np.int32)
    place = np.zeros((384, 320), np.float32)
    for l in range(4):
        for r in range(6):
            for c in range(12):
                q = (r // 3) * 2 + c // 6
                place[(l * 6 + r) * 16 + c, q * 80 + ((l - 1) % 4) * 18 + (r % 3) * 6 + c % 6] = 1
    low = lambda a: a.astype(ml_dtypes.bfloat16)
    return (low(gather), low(back), low(spread), low(spread_plain), low(cells), rows), low(place)


def halo_kernel(buf, cls, out, out_cls, send, recv, local):
    lat, lon = lax.axis_index("lat"), lax.axis_index("lon")
    n_lat, n_lon = lax.axis_size("lat"), lax.axis_size("lon")
    up, down = lax.rem(lat + 1, n_lat), lax.rem(lat + n_lat - 1, n_lat)
    east, west = lax.rem(lon + 1, n_lon), lax.rem(lon + n_lon - 1, n_lon)
    barrier = pltpu.get_barrier_semaphore()
    for device in ((lat, east), (up, lon), (up, east)):
        pl.semaphore_signal(barrier, inc=1, device_id=device, device_id_type=MESH)
    pl.semaphore_wait(barrier, 3)
    copies = []
    for k, (src, dst, device) in enumerate(((2, 1, (lat, west)), (1, 2, (down, lon)), (0, 3, (down, west)))):
        for m, (a, b) in enumerate(((buf, out), (cls, out_cls))):
            copies.append(
                pltpu.make_async_remote_copy(
                    src_ref=a.at[src],
                    dst_ref=b.at[dst],
                    send_sem=send.at[2 * k + m],
                    recv_sem=recv.at[2 * k + m],
                    device_id=device,
                    device_id_type=MESH,
                )
            )
    for copy in copies:
        copy.start()
    own = [
        pltpu.make_async_copy(buf.at[3], out.at[0], local.at[0]),
        pltpu.make_async_copy(cls.at[3], out_cls.at[0], local.at[1]),
    ]
    for copy in own:
        copy.start()
    for copy in own + copies:
        copy.wait()


def halo_forward(buf, cls):
    return pl.pallas_call(
        halo_kernel,
        out_shape=(jax.ShapeDtypeStruct(buf.shape, buf.dtype), jax.ShapeDtypeStruct(cls.shape, cls.dtype)),
        in_specs=[VMEM] * 2,
        out_specs=(VMEM, VMEM),
        scratch_shapes=[
            pltpu.SemaphoreType.DMA((6,)),
            pltpu.SemaphoreType.DMA((6,)),
            pltpu.SemaphoreType.DMA((2,)),
        ],
        compiler_params=pltpu.CompilerParams(collective_id=0, has_side_effects=True),
        name="halo",
    )(buf, cls)


def skew_parts(rows):
    lane = lax.broadcasted_iota(jnp.int32, (72, 128), 1)
    first = lane + rows >= PITCH * 5 + 11
    there = jnp.bitwise_and(lane - rows - 2, 127)
    back = jnp.bitwise_and(lane + rows + 2, 127)
    return first, there, back


def skew(table, first, there):
    mixed = jnp.where(first, table[:, :128], table[:, 128:])
    return jnp.take_along_axis(mixed, there, axis=1)


def split(values, count):
    pieces = []
    for _ in range(count):
        piece = values.astype(BF16)
        pieces.append(piece)
        values = values - piece.astype(F32)
    return pieces


def window_kernel(
    tok_in, cls_in, rel, gain, shift, w_qkv, b_qkv, w_proj, pos, surf,
    c_gather, c_back, c_spread, c_plain, c_cells, c_rows,
    out_w, out_t, out_gx,
    white, inv_std, normed, dy_low, qkv, dctx, turned, kv_pad, q_feat, k_feat,
    onehot, tables, d_tables, ctx_acc, dq_acc, f_acc, dkv_t, low, table_in,
):
    lat = lax.axis_index("lat")
    last_band = lat == lax.axis_size("lat") - 1

    tokens = dot(c_gather[...], tok_in[...])
    x = tokens[:288]
    dy = tokens[288:]
    dy_low[...] = dy.astype(BF16)
    centred = x - jnp.mean(x, -1, keepdims=True)
    inv = lax.rsqrt(jnp.mean(centred * centred, -1, keepdims=True) + EPS)
    inv_std[...] = inv
    whitened = centred * inv
    white[...] = whitened
    normed[...] = (whitened * gain[...] + shift[...]).astype(BF16)
    qkv[...] = (dot(normed[...], w_qkv[...]) + b_qkv[...]).astype(BF16)
    dctx[...] = dot(dy_low[...], w_proj[...], NT).astype(BF16)
    eye = (
        lax.broadcasted_iota(jnp.int32, (WIDTH, WIDTH), 0) == lax.broadcasted_iota(jnp.int32, (WIDTH, WIDTH), 1)
    ).astype(F32).astype(BF16)
    for w in range(2):
        rows = slice(w * WT, (w + 1) * WT)
        turned[w, 0] = dot(eye, qkv[rows, :WIDTH], NT).astype(BF16)
        turned[w, 1] = dot(eye, dctx[rows, :], NT).astype(BF16)
        kv_pad[w] = dot(c_spread[...], qkv[rows, WIDTH:]).astype(BF16)

    lane = lax.broadcasted_iota(jnp.int32, (WT, 128), 1)
    token = lax.broadcasted_iota(jnp.int32, (WT, 128), 0)
    kind = dot(c_cells[...], cls_in[...]).astype(jnp.int32)
    turned_over = jnp.logical_and(lax.rem(token, 72) >= 36, last_band).astype(F32)
    of_key = jnp.where(kind == jnp.bitwise_and(lane, 3), 1.0, 0.0)
    of_query = jnp.where(lane < 4, of_key, 0.0).astype(BF16)
    surf_over = surf[...] * (1.0 / SCALE)
    surf_lane = lax.broadcasted_iota(jnp.int32, (128, 128), 1)
    surf_hi, surf_lo = split(surf_over, 2)
    side = dot(of_query, jnp.where(surf_lane < 48, surf_hi.astype(F32), surf_lo.astype(F32)).astype(BF16))
    q_feat[...] = jnp.where(
        lane < 96, side, jnp.where(lane == 96, turned_over, jnp.where(lane == 97, 1.0 - turned_over, 0.0))
    ).astype(BF16)
    key_side = jnp.where(
        lane < 96,
        of_key,
        jnp.where(lane == 96, -BIG * (1.0 - turned_over), jnp.where(lane == 97, -BIG * turned_over, 0.0)),
    ).astype(BF16)
    key_lane = lax.broadcasted_iota(jnp.int32, (KEYS, 128), 1)
    key_row = jnp.bitwise_and(lax.broadcasted_iota(jnp.int32, (KEYS, 128), 0), 127)
    hidden = jnp.logical_and(lax.rem(key_row, PITCH) >= 12, jnp.logical_and(key_lane >= 96, key_lane < 98))
    k_feat[...] = jnp.where(hidden, -BIG, dot(c_spread[...], key_side)).astype(BF16)

    rel_now = rel[...]
    rel_low = jnp.bitwise_and(rel_now, 15)
    rel_wide = dot((rel_now - rel_low).astype(F32).astype(BF16), c_plain[...], NT) + dot(
        rel_low.astype(F32).astype(BF16), c_plain[...], NT
    )
    rel_lane = jnp.bitwise_and(lax.broadcasted_iota(jnp.int32, (WT, KEYS), 1), 127)
    rel_wide = jnp.where(lax.rem(rel_lane, PITCH) < 12, rel_wide, -1.0)
    plain = lax.broadcasted_iota(jnp.int32, (72, 128), 0)
    plain = plain + 11 * (plain // 12)
    first, _, back = skew_parts(plain)
    slot = lax.broadcasted_iota(jnp.int32, (768, 128), 0).astype(F32)
    for b, block in enumerate((rel_wide[:72, :128], rel_wide[:72, 128:], rel_wide[72:, :128])):
        turned_back = jnp.take_along_axis(block, back, axis=1)
        for half in range(2):
            kept = jnp.where(first, turned_back, -1.0) if half == 0 else jnp.where(first, -1.0, turned_back)
            slots = jnp.max(kept, 0, keepdims=True)
            lanes = slice(b * 256 + half * 128, b * 256 + half * 128 + 128)
            onehot[:, lanes] = jnp.where(slot == slots, 1.0, 0.0).astype(BF16)
    table_in[...] = jnp.zeros_like(table_in)
    for w in range(2):
        table_in[w, :HEADS, :SLOTS] = pos[2 * lat + w] * LOG2E
        tables[w] = functools.reduce(jnp.add, [dot(part, onehot[...]) for part in split(table_in[w], 3)])

    d_tables[...] = jnp.zeros_like(d_tables)
    f_acc[...] = jnp.zeros_like(f_acc)
    zero = jnp.zeros((72, 128), F32)

    def group_step(g, carry):
        first, there, back = skew_parts(jnp.broadcast_to(c_rows[...], (72, 128)))
        lanes = pl.ds(pl.multiple_of(g * 128, 128), 128)
        v_lanes = pl.ds(pl.multiple_of(WIDTH + g * 128, 128), 128)
        cat_lane = lax.broadcasted_iota(jnp.int32, (1, 256), 1)
        feat_lane = cat_lane - 128
        for w in range(2):
            rows = slice(w * WT, (w + 1) * WT)
            q_cat = jnp.concatenate([qkv[rows, lanes], q_feat[...]], 1)
            k_cat = jnp.concatenate([kv_pad[w, :, lanes], k_feat[...]], 1)
            v_now = kv_pad[w, :, v_lanes]
            dctx_now = dctx[rows, lanes]
            ctx_sum = jnp.zeros((WT, 128), F32)
            dq_sum = jnp.zeros((WT, 128), F32)
            feat_sum = jnp.zeros((WT, 128), F32)
            for hh in range(4):
                head = g * 4 + hh
                mine = cat_lane // 32 == hh
                feat_mine = jnp.logical_and(
                    cat_lane >= 128,
                    jnp.logical_or(feat_lane >= 96, lax.rem(feat_lane // 4 + 12, 12) == head),
                )
                keep = jnp.logical_or(mine, feat_mine).astype(F32).astype(BF16)
                k_head = k_cat * keep
                v_head = v_now * keep[:, :128]
                raw = dot(q_cat, k_head, NT)
                d_raw = dot(dctx_now, v_head, NT)
                table = tables[w, pl.ds(head, 1), :]
                same = skew(table[:, :256], first, there)
                if w == 0:
                    upper = jnp.concatenate([same, skew(table[:, 256:512], first, there)], 1)
                    lower = jnp.concatenate([skew(table[:, 512:], first, there), same], 1)
                    bias = jnp.concatenate([upper, lower], 0)
                else:
                    raw = jnp.concatenate([raw[:72, :128], raw[72:, 128:]], 0)
                    d_raw = jnp.concatenate([d_raw[:72, :128], d_raw[72:, 128:]], 0)
                    bias = jnp.concatenate([same, same], 0)
                score = raw * (SCALE * LOG2E) + bias
                power = jnp.exp2(score - jnp.max(score, -1, keepdims=True))
                probs = power * (1.0 / jnp.sum(power, -1, keepdims=True))
                dot_sum = jnp.sum(d_raw * probs, -1, keepdims=True)
                d_score = probs * (d_raw - dot_sum)
                if w == 0:
                    probs_low = probs.astype(BF16)
                    score_low = d_score.astype(BF16)
                    blocks = (d_score[:72, :128] + d_score[72:, 128:], d_score[:72, 128:], d_score[72:, :128])
                else:
                    def wide(a):
                        top = jnp.concatenate([a[:72], zero], 1)
                        return jnp.concatenate([top, jnp.concatenate([zero, a[72:]], 1)], 0).astype(BF16)

                    probs_low = wide(probs)
                    score_low = wide(d_score)
                    blocks = (d_score[:72] + d_score[72:],)
                for b, block in enumerate(blocks):
                    turned_back = jnp.take_along_axis(block, back, axis=1)
                    early = jnp.where(first, turned_back, 0.0)
                    late = turned_back - early
                    d_tables[w, head, :, b * 256 : b * 256 + 128] = jnp.sum(early.reshape(9, 8, 128), 0)
                    d_tables[w, head, :, b * 256 + 128 : b * 256 + 256] = jnp.sum(late.reshape(9, 8, 128), 0)
                ctx_sum += dot(probs_low, v_head)
                both = dot(score_low, k_head)
                dq_sum += both[:, :128]
                feat_sum += both[:, 128:]
                head_rows = pl.ds(pl.multiple_of(g * 128 + hh * 32, 32), 32)
                dkv_t[w, 0, head_rows, :] = dot(turned[w, 0, head_rows, :], score_low) * SCALE
                dkv_t[w, 1, head_rows, :] = dot(turned[w, 1, head_rows, :], probs_low)
            ctx_acc[rows, lanes] = ctx_sum.astype(BF16)
            dq_acc[rows, lanes] = dq_sum * SCALE
            f_acc[w] += feat_sum
        return carry

    lax.fori_loop(0, 3, group_step, 0)

    for w in range(2):
        table = functools.reduce(jnp.add, [dot(part, onehot[...], NT) for part in split(jnp.sum(d_tables[w], 1), 2)])
        for half in range(2):
            for k in range(3):
                at = 128 * (3 * half + k)
                out_t[w, half, 16 * k : 16 * k + 16, :] = table[:, at : at + 128].astype(BF16)

    low[:, :WIDTH] = dq_acc[...].astype(BF16)
    sums = [jnp.sum(dq_acc[...], 0, keepdims=True)]
    for part in range(2):
        total = jnp.zeros((1, WIDTH), F32)
        for w in range(2):
            plain_rows = dot(c_spread[...], dkv_t[w, part].astype(BF16), (((0,), (1,)), ((), ())))
            total += jnp.sum(plain_rows, 0, keepdims=True)
            low[w * WT : (w + 1) * WT, WIDTH * (part + 1) : WIDTH * (part + 2)] = plain_rows.astype(BF16)
        sums.append(total)
    d_normed = dot(low[...], w_qkv[...], NT).astype(BF16).astype(F32)
    scaled = d_normed * gain[...]
    first_mean = jnp.mean(scaled, -1, keepdims=True)
    second_mean = jnp.mean(scaled * white[...], -1, keepdims=True)
    d_inputs = dy_low[...].astype(F32) + inv_std[...] * (scaled - first_mean - white[...] * second_mean)
    moved = dot(c_back[...], d_inputs.astype(BF16)).astype(BF16)
    for q in range(4):
        out_gx[q] = moved[q * 80 : q * 80 + 80]
    sums.append(jnp.sum(dy_low[...].astype(F32), 0, keepdims=True))
    sums.append(jnp.sum(d_normed * white[...], 0, keepdims=True))
    sums.append(jnp.sum(d_normed, 0, keepdims=True))
    of_row = jnp.where(lane < 4, of_key, 0.0).astype(BF16)
    d_surf = functools.reduce(jnp.add, [dot(of_row, part, TN) for part in split(f_acc[0] + f_acc[1], 2)])

    for j in range(4):
        if j < 3:
            grad = dot(normed[...], low[:, j * WIDTH : (j + 1) * WIDTH], TN)
        else:
            grad = dot(ctx_acc[...], dy_low[...], TN)
        for i in range(8):
            n = i * 4 + j
            for m in range(3):
                out_w[n // PLANE, n % PLANE, 48 * m : 48 * m + 48, :] = grad[
                    48 * i : 48 * i + 48, 128 * m : 128 * m + 128
                ].astype(BF16)
    extra_row = lax.broadcasted_iota(jnp.int32, (16, 128), 0) == 12
    for n in range(2 * PLANE):
        if n < 18:
            row = sums[n // 3][:, 128 * (n % 3) : 128 * (n % 3) + 128]
        elif n < 22:
            row = d_surf[n - 18 : n - 17, :]
        else:
            row = jnp.zeros((1, 128), F32)
        out_w[n // PLANE, n % PLANE, 144:160, :] = jnp.where(extra_row, row, 0.0).astype(BF16)


def windows(tok, cls, rel, gain, shift, w_qkv, b_qkv, w_proj, pos, surf, consts):
    operands = (tok, cls, rel, gain, shift, w_qkv, b_qkv, w_proj, pos, surf, *consts)
    return pl.pallas_call(
        window_kernel,
        out_shape=(
            jax.ShapeDtypeStruct((2, PLANE, 160, 128), BF16),
            jax.ShapeDtypeStruct((2, 2, 48, 128), BF16),
            jax.ShapeDtypeStruct((4, 80, WIDTH), BF16),
        ),
        in_specs=[VMEM] * len(operands),
        out_specs=(VMEM,) * 3,
        scratch_shapes=[
            pltpu.VMEM((288, WIDTH), F32),
            pltpu.VMEM((288, 1), F32),
            pltpu.VMEM((288, WIDTH), BF16),
            pltpu.VMEM((288, WIDTH), BF16),
            pltpu.VMEM((288, 3 * WIDTH), BF16),
            pltpu.VMEM((288, WIDTH), BF16),
            pltpu.VMEM((2, 2, WIDTH, WT), BF16),
            pltpu.VMEM((2, KEYS, 2 * WIDTH), BF16),
            pltpu.VMEM((WT, 128), BF16),
            pltpu.VMEM((KEYS, 128), BF16),
            pltpu.VMEM((768, 768), BF16),
            pltpu.VMEM((2, 16, 768), F32),
            pltpu.VMEM((2, 16, 8, 768), F32),
            pltpu.VMEM((288, WIDTH), BF16),
            pltpu.VMEM((288, WIDTH), F32),
            pltpu.VMEM((2, WT, 128), F32),
            pltpu.VMEM((2, 2, WIDTH, KEYS), F32),
            pltpu.VMEM((288, 3 * WIDTH), BF16),
            pltpu.VMEM((2, 16, 768), F32),
        ],
        compiler_params=pltpu.CompilerParams(vmem_limit_bytes=56 * 1024 * 1024),
        name="windows",
    )(*operands)


def reduce_kernel(
    wp, tp, gx, full, gx_out,
    c_recv, tc_recv, t_send, t_recv, p_send, p_recv, z_own, z_send, z_recv, z_full,
    h_sems, c_sems, t_sems, p_sems, z_sems, a_sems, g_sems, k_sems, local,
):
    lat, lon = lax.axis_index("lat"), lax.axis_index("lon")
    n_lat, n_lon = lax.axis_size("lat"), lax.axis_size("lon")
    core = lax.rem(lon, 2)
    z = lax.rem(lon // 2, PZ)
    x = lax.rem(lat, 2) * 2 + lon // (2 * PZ)
    y = lat // 2
    here = y * PX + x

    def device(x_at, y_at, z_at, core_at):
        return (y_at * 2 + x_at // 2, (lax.rem(x_at, 2) * PZ + z_at) * 2 + core_at)

    def in_plane(step, sign):
        x_at = lax.rem(x + PX + sign * (step % PX), PX)
        y_at = lax.rem(y + PY + sign * (step // PX), PY)
        return x_at, y_at, y_at * PX + x_at

    up, down = lax.rem(lat + 1, n_lat), lax.rem(lat + n_lat - 1, n_lat)
    east, west = lax.rem(lon + 1, n_lon), lax.rem(lon + n_lon - 1, n_lon)
    sibling = (lat, lon + 1 - 2 * core)
    x_pair = device(x + 1 - 2 * lax.rem(x, 2), y, z, core)

    barrier = pltpu.get_barrier_semaphore()
    greeted = [(lat, west), (down, lon), (down, west), sibling]
    for step in range(1, PLANE):
        x_at, y_at, _ = in_plane(step, -1)
        greeted.append(device(x_at, y_at, z, core))
    for step in range(1, PZ):
        greeted.append(device(x, y, lax.rem(z + PZ - step, PZ), core))
    for other in greeted:
        pl.semaphore_signal(barrier, inc=1, device_id=other, device_id_type=MESH)
    pl.semaphore_wait(barrier, len(greeted))

    def send(src, dst, sems, k, to):
        copy = pltpu.make_async_remote_copy(
            src_ref=src,
            dst_ref=dst,
            send_sem=sems.at[0, k],
            recv_sem=sems.at[1, k],
            device_id=to,
            device_id_type=MESH,
        )
        copy.start()
        return copy

    order = list(range(1, PLANE)) + [0]
    core_copies = {}
    t_copy = send(tp.at[1 - core], tc_recv, t_sems, 0, sibling)
    for step in order:
        at = in_plane(step, 1)[2]
        core_copies[step] = send(wp.at[1 - core, at], c_recv.at[step], c_sems, step, sibling)

    halo = [
        send(gx.at[1], gx_out.at[2], h_sems, 0, (lat, east)),
        send(gx.at[2], gx_out.at[1], h_sems, 1, (up, lon)),
        send(gx.at[3], gx_out.at[0], h_sems, 2, (up, east)),
    ]
    own = pltpu.make_async_copy(gx.at[0], gx_out.at[3], local)
    own.start()

    t_copy.wait()
    t_mine = lax.rem(x, 2)
    t_send[...] = (tp[core, 1 - t_mine].astype(F32) + tc_recv[1 - t_mine].astype(F32)).astype(BF16)
    tx_copy = send(t_send, t_recv, t_sems, 1, x_pair)
    plane_copies = []
    for step in range(1, PLANE):
        x_at, y_at, at = in_plane(step, 1)
        core_copies[step].wait()
        p_send[step] = (wp[core, at].astype(F32) + c_recv[step].astype(F32)).astype(BF16)
        plane_copies.append(send(p_send.at[step], p_recv.at[step], p_sems, step, device(x_at, y_at, z, core)))
    core_copies[0].wait()
    total = wp[core, here].astype(F32) + c_recv[0].astype(F32)
    tx_copy.wait()
    t_total = tp[core, t_mine].astype(F32) + tc_recv[t_mine].astype(F32) + t_recv[...].astype(F32)
    for step in range(1, PLANE):
        plane_copies[step - 1].wait()
        total = total + p_recv[step].astype(F32)
    z_own[0:144, :] = total[:144]
    z_own[144:160, :] = total[144:] + t_total[:16]
    z_own[160:192, :] = t_total[16:]

    for k in range(PZ):
        z_send[k] = z_own[24 * k : 24 * k + 24, :].astype(BF16)
    z_copies = []
    for step in range(1, PZ):
        z_at = lax.rem(z + step, PZ)
        z_copies.append(send(z_send.at[z_at], z_recv.at[step], z_sems, step, device(x, y, z_at, core)))
    summed = z_own[pl.ds(pl.multiple_of(24 * z, 8), 24), :]
    for step in range(1, PZ):
        z_copies[step - 1].wait()
        summed = summed + z_recv[step].astype(F32)
    z_full[z] = summed.astype(BF16)
    a_copies = []
    for step in range(1, PZ):
        z_at = lax.rem(z + step, PZ)
        a_copies.append(send(z_full.at[z], z_full.at[z], a_sems, step, device(x, y, z_at, core)))
    for copy in a_copies:
        copy.wait()
    full[core, here] = jnp.concatenate([z_full[k].astype(F32) for k in range(PZ)], 0).astype(BF16)

    g_copies = []
    for step in range(1, PLANE):
        x_at, y_at, _ = in_plane(step, 1)
        g_copies.append(send(full.at[core, here], full.at[core, here], g_sems, step, device(x_at, y_at, z, core)))
    k_copies = [send(full.at[core, here], full.at[core, here], k_sems, 0, sibling)]
    for step in range(1, PLANE):
        at = in_plane(step, -1)[2]
        g_copies[step - 1].wait()
        k_copies.append(send(full.at[core, at], full.at[core, at], k_sems, step, sibling))
    for copy in k_copies + halo:
        copy.wait()
    own.wait()


def reduce_all(wp, tp, gx):
    sems = pltpu.SemaphoreType.DMA
    return pl.pallas_call(
        reduce_kernel,
        out_shape=(
            jax.ShapeDtypeStruct((2, PLANE, 192, 128), BF16),
            jax.ShapeDtypeStruct((4, 80, WIDTH), BF16),
        ),
        in_specs=[VMEM] * 3,
        out_specs=(VMEM, VMEM),
        scratch_shapes=[
            pltpu.VMEM((PLANE, 160, 128), BF16),
            pltpu.VMEM((2, 48, 128), BF16),
            pltpu.VMEM((48, 128), BF16),
            pltpu.VMEM((48, 128), BF16),
            pltpu.VMEM((PLANE, 160, 128), BF16),
            pltpu.VMEM((PLANE, 160, 128), BF16),
            pltpu.VMEM((192, 128), F32),
            pltpu.VMEM((PZ, 24, 128), BF16),
            pltpu.VMEM((PZ, 24, 128), BF16),
            pltpu.VMEM((PZ, 24, 128), BF16),
            sems((2, 3)),
            sems((2, PLANE)),
            sems((2, 2)),
            sems((2, PLANE)),
            sems((2, PZ)),
            sems((2, PZ)),
            sems((2, PLANE)),
            sems((2, PLANE)),
            sems(()),
        ],
        compiler_params=pltpu.CompilerParams(
            collective_id=1, has_side_effects=True, vmem_limit_bytes=32 * 1024 * 1024
        ),
        name="reduce",
    )(wp, tp, gx)


def finish_kernel(grad_scale, full, gx, place, o_gx, o_wqkv, o_bqkv, o_wproj, o_bproj, o_gain, o_shift, o_pos, o_surf):
    rows = jnp.concatenate([gx[q] for q in range(4)], 0)
    o_gx[...] = dot(place[...], rows).astype(BF16).reshape(4, 6, 16, WIDTH)[:, :, :12, :]
    for j in range(4):
        for i in range(8):
            n = i * 4 + j
            for m in range(3):
                part = full[n // PLANE, n % PLANE, 48 * m : 48 * m + 48, :].astype(F32) * grad_scale
                if j < 3:
                    o_wqkv[48 * i : 48 * i + 48, WIDTH * j + 128 * m : WIDTH * j + 128 * m + 128] = part
                else:
                    o_wproj[48 * i : 48 * i + 48, 128 * m : 128 * m + 128] = part
    for core in range(2):
        for at in range(PLANE):
            x, y = at % PX, at // PX
            kind = (y * 2 + x // 2) * 2 + core
            for k in range(3):
                part = full[core, at, 144 + 16 * k : 160 + 16 * k, :].astype(F32) * grad_scale
                lo = 128 * (3 * (x % 2) + k)
                width = min(128, SLOTS - lo)
                o_pos[kind, :, lo : lo + width] = part[:HEADS, :width]

    def extra(n):
        tile = full[n // PLANE, n % PLANE, 144:160, :].astype(F32) * grad_scale
        return tile[12:13, :]

    for n in range(9):
        o_bqkv[:, 128 * n : 128 * n + 128] = extra(n)
    for v, out in enumerate((o_bproj, o_gain, o_shift)):
        for m in range(3):
            out[:, 128 * m : 128 * m + 128] = extra(9 + 3 * v + m)
    sides = jnp.concatenate([extra(18 + a) for a in range(4)], 0)
    for h in range(HEADS):
        o_surf[h] = sides[:, 4 * h : 4 * h + 4]


def finish(full, gx, place, grad_scale):
    one = lambda *shape: jax.ShapeDtypeStruct(shape, F32)
    return pl.pallas_call(
        functools.partial(finish_kernel, grad_scale),
        out_shape=(
            jax.ShapeDtypeStruct((4, 6, 12, WIDTH), BF16),
            one(WIDTH, 3 * WIDTH),
            one(1, 3 * WIDTH),
            one(WIDTH, WIDTH),
            one(1, WIDTH),
            one(1, WIDTH),
            one(1, WIDTH),
            one(16, HEADS, SLOTS),
            one(HEADS, 4, 4),
        ),
        in_specs=[VMEM] * 3,
        out_specs=(VMEM,) * 9,
        compiler_params=pltpu.CompilerParams(vmem_limit_bytes=32 * 1024 * 1024),
        name="finish",
    )(full, gx, place)


def on_device(
    inputs, cotangent, land_sea, rel_index, norm_gain, norm_shift, w_qkv, b_qkv, w_proj, pos_bias, surf_bias
):
    levels, lat_rows, lon_cols, width = inputs.shape
    count = levels * lat_rows * lon_cols * lax.axis_size("lat") * lax.axis_size("lon")
    consts, place = constants()
    both = jnp.stack([inputs, cotangent])
    both = jnp.roll(both, -1, 1).reshape(2, 4, 2, 3, 2, 6, width)
    buf = both.transpose(2, 4, 0, 1, 3, 5, 6).reshape(4, 144, width)
    cells = land_sea.reshape(2, 3, 2, 6).transpose(0, 2, 1, 3).reshape(4, 18, 1).astype(BF16)
    cells = jnp.pad(jnp.broadcast_to(cells, (4, 18, 128)), ((0, 0), (0, 14), (0, 0)))
    side = surf_bias.transpose(1, 0, 2).reshape(4, 48)
    side = jnp.pad(jnp.concatenate([side, side], 1), ((0, 124), (0, 32)))
    tok, cls = halo_forward(buf, cells)
    wp, tp, gx = windows(
        tok.reshape(576, width),
        cls.reshape(128, 128),
        rel_index,
        norm_gain.reshape(1, width),
        norm_shift.reshape(1, width),
        w_qkv,
        b_qkv.reshape(1, 3 * width),
        w_proj,
        pos_bias,
        side,
        tuple(jnp.asarray(a) for a in consts),
    )
    full, gx = reduce_all(wp, tp, gx)
    outs = finish(full, gx, jnp.asarray(place), float(count) ** -0.5)
    g_x, g_wqkv, g_bqkv, g_wproj, g_bproj, g_gain, g_shift, g_pos, g_surf = outs
    return (
        g_x,
        g_wqkv,
        g_bqkv.reshape(-1),
        g_wproj,
        g_bproj.reshape(-1),
        g_gain.reshape(-1),
        g_shift.reshape(-1),
        g_pos,
        g_surf,
    )


def solution(mesh):
    in_specs = (P(None, "lat", "lon", None), P(None, "lat", "lon", None), P("lat", "lon")) + (P(),) * 8
    out_specs = (P(None, "lat", "lon", None),) + (P(),) * 8
    return jax.shard_map(on_device, mesh=mesh, in_specs=in_specs, out_specs=out_specs, check_vma=False)
```

```python
import functools

import jax
import jax.numpy as jnp
import ml_dtypes
import numpy as np
from jax import lax
from jax.experimental import pallas as pl
from jax.experimental.pallas import tpu as pltpu
from jax.sharding import PartitionSpec as P

F32 = jnp.float32
BF16 = jnp.bfloat16
MESH = pl.DeviceIdType.MESH
EPS = 1e-05
LOG2E = 1.4426950408889634
BIG = 2.0**33
HEADS = 12
SLOTS = 759
WIDTH = 384
WT = 144
PITCH = 23
KEYS = 256
SCALE = 32.0**-0.5
NT = (((1,), (1,)), ((), ()))
TN = (((0,), (0,)), ((), ()))
NN = (((1,), (0,)), ((), ()))
PX, PY, PZ = 4, 4, 8
PLANE = PX * PY
VMEM = pl.BlockSpec(memory_space=pltpu.VMEM)


def dot(a, b, dims=NN):
    return lax.dot_general(a, b, dims, preferred_element_type=F32)


def constants():
    spread = np.zeros((KEYS, WT), np.float32)
    of_row = np.zeros((WT, 32), np.float32)
    of_col = np.zeros((WT, 128), np.float32)
    for k in range(WT):
        li, ri, ci = k // 72, k // 12 % 6, k % 12
        spread[li * 128 + PITCH * ri + ci, k] = 1
        of_row[k, 8 * (2 * (ri // 3) + ci // 6) + ri % 3] = 1
        of_col[k, ci % 6] = 1
    return tuple(a.astype(ml_dtypes.bfloat16) for a in (spread, of_row, of_col))


class Place:
    def __init__(self):
        lat, lon = lax.axis_index("lat"), lax.axis_index("lon")
        n_lat, n_lon = lax.axis_size("lat"), lax.axis_size("lon")
        self.lat, self.n_lat = lat, n_lat
        self.core = lax.rem(lon, 2)
        self.z = lax.rem(lon // 2, PZ)
        self.x = lax.rem(lat, 2) * 2 + lon // (2 * PZ)
        self.y = lat // 2
        self.here = self.y * PX + self.x
        up, down = lax.rem(lat + 1, n_lat), lax.rem(lat + n_lat - 1, n_lat)
        right, left = lax.rem(lon + 1, n_lon), lax.rem(lon + n_lon - 1, n_lon)
        self.north, self.south = (up, lon), (down, lon)
        self.east, self.west = (lat, right), (lat, left)
        self.north_east, self.south_west = (up, right), (down, left)
        self.sibling = (lat, lon + 1 - 2 * self.core)
        self.x_pair = self.device(self.x + 1 - 2 * lax.rem(self.x, 2), self.y, self.z, self.core)

    def device(self, x, y, z, core):
        return (y * 2 + x // 2, (lax.rem(x, 2) * PZ + z) * 2 + core)

    def in_plane(self, step, sign):
        x = lax.rem(self.x + PX + sign * (step % PX), PX)
        y = lax.rem(self.y + PY + sign * (step // PX), PY)
        return x, y, y * PX + x

    def greet(self):
        others = [self.north, self.south, self.east, self.west, self.north_east, self.south_west, self.sibling]
        for step in range(1, PLANE):
            x, y, _ = self.in_plane(step, -1)
            others.append(self.device(x, y, self.z, self.core))
        for step in range(1, PZ):
            others.append(self.device(self.x, self.y, lax.rem(self.z + PZ - step, PZ), self.core))
        for other in others:
            pl.semaphore_signal(pltpu.get_barrier_semaphore(), inc=1, device_id=other, device_id_type=MESH)
        self.greeted = len(others)

    def meet(self):
        pl.semaphore_wait(pltpu.get_barrier_semaphore(), self.greeted)


def send(src, dst, sems, k, to):
    copy = pltpu.make_async_remote_copy(
        src_ref=src,
        dst_ref=dst,
        send_sem=sems.at[0, k],
        recv_sem=sems.at[1, k],
        device_id=to,
        device_id_type=MESH,
    )
    copy.start()
    return copy


def plain_rows():
    rows = lax.broadcasted_iota(jnp.int32, (72, 128), 0)
    return rows + (PITCH - 12) * (rows // 12)


def skew_parts(rows):
    lane = lax.broadcasted_iota(jnp.int32, (72, 128), 1)
    first = lane + rows >= PITCH * 5 + 11
    there = jnp.bitwise_and(lane - rows - 2, 127)
    back = jnp.bitwise_and(lane + rows + 2, 127)
    return first, there, back


def skew(table, first, there):
    mixed = jnp.where(first, table[:, :128], table[:, 128:])
    return jnp.take_along_axis(mixed, there, axis=1)


def split(values, count):
    pieces = []
    for _ in range(count):
        piece = values.astype(BF16)
        pieces.append(piece)
        values = values - piece.astype(F32)
    return pieces


def step_kernel(
    x_in, dy_in, land, rel, gain, shift, w_qkv, b_qkv, w_proj, pos, surf, c_spread, c_row, c_col,
    full, gx_out,
    tok_x, tok_dy, cls_out, cls_in, side_in, wp, tp, gx,
    mixed, white, inv_std, normed, dy_low, qkv, dctx, turned, kv_pad, q_feat, k_feat,
    onehot, tables, d_tables, ctx_acc, dq_acc, f_acc, dkv_t, low, table_in,
    c_recv, tc_recv, t_send, t_recv, p_send, p_recv, z_own, z_send, z_recv, z_full,
    f_sems, h_sems, c_sems, t_sems, p_sems, z_sems, a_sems, g_sems, k_sems, local,
):
    place = Place()
    place.greet()

    cls_out[...] = jnp.zeros_like(cls_out)
    for q in range(4):
        cls_out[q, :3, :6] = land[3 * (q // 2) : 3 * (q // 2) + 3, 6 * (q % 2) : 6 * (q % 2) + 6].astype(F32)

    def quadrant(ref, q):
        return ref.at[pl.ds(3 * (q // 2), 3), pl.ds(6 * (q % 2), 6)]

    place.meet()
    halo = []
    for k, (q, to) in enumerate(((2, place.west), (1, place.south), (0, place.south_west))):
        for m, (a, b) in enumerate(((x_in, tok_x), (dy_in, tok_dy))):
            halo.append(send(quadrant(a, q), quadrant(b, 3 - q), f_sems, 3 * k + m, to))
        halo.append(send(cls_out.at[q], cls_in.at[3 - q], f_sems, 3 * k + 2, to))
    own = [
        pltpu.make_async_copy(quadrant(x_in, 3), quadrant(tok_x, 0), local.at[0]),
        pltpu.make_async_copy(quadrant(dy_in, 3), quadrant(tok_dy, 0), local.at[1]),
        pltpu.make_async_copy(cls_out.at[3], cls_in.at[0], local.at[2]),
    ]
    for copy in own:
        copy.start()

    lat = place.lat
    last_band = lat == place.n_lat - 1
    rel_now = rel[...]
    rel_low = jnp.bitwise_and(rel_now, 15)
    rel_wide = dot((rel_now - rel_low).astype(F32).astype(BF16), c_spread[...], NT) + dot(
        rel_low.astype(F32).astype(BF16), c_spread[...], NT
    )
    rel_lane = jnp.bitwise_and(lax.broadcasted_iota(jnp.int32, (WT, KEYS), 1), 127)
    rel_wide = jnp.where(lax.rem(rel_lane, PITCH) < 12, rel_wide, -1.0)
    first, _, back = skew_parts(plain_rows())
    slot = lax.broadcasted_iota(jnp.int32, (768, 128), 0).astype(F32)
    for b, block in enumerate((rel_wide[:72, :128], rel_wide[:72, 128:], rel_wide[72:, :128])):
        turned_back = jnp.take_along_axis(block, back, axis=1)
        for half in range(2):
            kept = jnp.where(first, turned_back, -1.0) if half == 0 else jnp.where(first, -1.0, turned_back)
            slots = jnp.max(kept, 0, keepdims=True)
            lanes = slice(b * 256 + half * 128, b * 256 + half * 128 + 128)
            onehot[:, lanes] = jnp.where(slot == slots, 1.0, 0.0).astype(BF16)
    table_in[...] = jnp.zeros_like(table_in)
    for w in range(2):
        for h in range(HEADS):
            table_in[w, h : h + 1, :SLOTS] = pos[pl.ds(16 * h + 2 * lat + w, 1), :] * LOG2E
        tables[w] = functools.reduce(jnp.add, [dot(part, onehot[...]) for part in split(table_in[w], 3)])


    for copy in halo + own:
        copy.wait()
    for j in range(3):
        cols = slice(128 * j, 128 * j + 128)
        mixed[j, :, 0:4, :] = tok_x[:, :, :, cols].reshape(72, 4, 128).astype(F32)
        mixed[j, :, 4:8, :] = tok_dy[:, :, :, cols].reshape(72, 4, 128).astype(F32)
    strided = mixed.reshape(3 * 576, 128)
    for k in range(4):
        level = (1, 2, 3, 0)[k]
        rows = slice(72 * k, 72 * k + 72)
        for j in range(3):
            cols = slice(128 * j, 128 * j + 128)
            white[rows, cols] = strided[pl.ds(576 * j + level, 72, stride=8), :]
            dq_acc[rows, cols] = strided[pl.ds(576 * j + 4 + level, 72, stride=8), :]
    x = white[...]
    dy_low[...] = dq_acc[...].astype(BF16)
    centred = x - jnp.mean(x, -1, keepdims=True)
    inv = lax.rsqrt(jnp.mean(centred * centred, -1, keepdims=True) + EPS)
    inv_std[...] = inv
    whitened = centred * inv
    white[...] = whitened
    gain_row = gain[...].reshape(1, WIDTH)
    normed[...] = (whitened * gain_row + shift[...].reshape(1, WIDTH)).astype(BF16)
    qkv[...] = (dot(normed[...], w_qkv[...]) + b_qkv[...].reshape(1, 3 * WIDTH)).astype(BF16)
    dctx[...] = dot(dy_low[...], w_proj[...], NT).astype(BF16)
    eye = (
        lax.broadcasted_iota(jnp.int32, (WIDTH, WIDTH), 0) == lax.broadcasted_iota(jnp.int32, (WIDTH, WIDTH), 1)
    ).astype(F32).astype(BF16)
    for w in range(2):
        rows = slice(w * WT, (w + 1) * WT)
        turned[w, 0] = dot(eye, qkv[rows, :WIDTH], NT).astype(BF16)
        turned[w, 1] = dot(eye, dctx[rows, :], NT).astype(BF16)
        kv_pad[w] = dot(c_spread[...], qkv[rows, WIDTH:]).astype(BF16)

    lane = lax.broadcasted_iota(jnp.int32, (WT, 128), 1)
    token = lax.broadcasted_iota(jnp.int32, (WT, 128), 0)
    cells = dot(c_row[...], cls_in[...].reshape(32, 128).astype(BF16)) * c_col[...].astype(F32)
    kind = dot(cells.astype(BF16), jnp.ones((128, 128), BF16)).astype(jnp.int32)
    turned_over = jnp.logical_and(lax.rem(token, 72) >= 36, last_band).astype(F32)
    of_key = jnp.where(kind == lax.rem(lane, 48) // 12, 1.0, 0.0)
    of_query = jnp.where(kind == lane, 1.0, 0.0).astype(BF16)
    side_in[...] = jnp.zeros_like(side_in)
    for a in range(4):
        for b in range(4):
            side_in[a : a + 1, 12 * b : 12 * b + 12] = surf[a, b : b + 1, :]
            side_in[a : a + 1, 48 + 12 * b : 60 + 12 * b] = surf[a, b : b + 1, :]
    surf_lane = lax.broadcasted_iota(jnp.int32, (128, 128), 1)
    surf_hi, surf_lo = split(side_in[...] * (1.0 / SCALE), 2)
    side = dot(of_query, jnp.where(surf_lane < 48, surf_hi.astype(F32), surf_lo.astype(F32)).astype(BF16))
    q_feat[...] = jnp.where(
        lane < 96, side, jnp.where(lane == 96, turned_over, jnp.where(lane == 97, 1.0 - turned_over, 0.0))
    ).astype(BF16)
    key_side = jnp.where(
        lane < 96,
        of_key,
        jnp.where(lane == 96, -BIG * (1.0 - turned_over), jnp.where(lane == 97, -BIG * turned_over, 0.0)),
    ).astype(BF16)
    key_lane = lax.broadcasted_iota(jnp.int32, (KEYS, 128), 1)
    key_row = jnp.bitwise_and(lax.broadcasted_iota(jnp.int32, (KEYS, 128), 0), 127)
    hidden = jnp.logical_and(lax.rem(key_row, PITCH) >= 12, jnp.logical_and(key_lane >= 96, key_lane < 98))
    k_feat[...] = jnp.where(hidden, -BIG, dot(c_spread[...], key_side)).astype(BF16)

    d_tables[...] = jnp.zeros_like(d_tables)
    f_acc[...] = jnp.zeros_like(f_acc)
    zero = jnp.zeros((72, 128), F32)

    def group_step(g, carry):
        first, there, back = skew_parts(plain_rows())
        lanes = pl.ds(pl.multiple_of(g * 128, 128), 128)
        v_lanes = pl.ds(pl.multiple_of(WIDTH + g * 128, 128), 128)
        cat_lane = lax.broadcasted_iota(jnp.int32, (1, 256), 1)
        feat_lane = cat_lane - 128
        for w in range(2):
            rows = slice(w * WT, (w + 1) * WT)
            q_cat = jnp.concatenate([qkv[rows, lanes], q_feat[...]], 1)
            k_cat = jnp.concatenate([kv_pad[w, :, lanes], k_feat[...]], 1)
            v_now = kv_pad[w, :, v_lanes]
            dctx_now = dctx[rows, lanes]
            ctx_sum = jnp.zeros((WT, 128), F32)
            dq_sum = jnp.zeros((WT, 128), F32)
            feat_sum = jnp.zeros((WT, 128), F32)
            for hh in range(4):
                head = g * 4 + hh
                mine = cat_lane // 32 == hh
                feat_mine = jnp.logical_and(
                    cat_lane >= 128,
                    jnp.logical_or(feat_lane >= 96, lax.rem(feat_lane + 132, 12) == head),
                )
                keep = jnp.logical_or(mine, feat_mine).astype(F32).astype(BF16)
                k_head = k_cat * keep
                v_head = v_now * keep[:, :128]
                raw = dot(q_cat, k_head, NT)
                d_raw = dot(dctx_now, v_head, NT)
                table = tables[w, pl.ds(head, 1), :]
                same = skew(table[:, :256], first, there)
                if w == 0:
                    upper = jnp.concatenate([same, skew(table[:, 256:512], first, there)], 1)
                    lower = jnp.concatenate([skew(table[:, 512:], first, there), same], 1)
                    bias = jnp.concatenate([upper, lower], 0)
                else:
                    raw = jnp.concatenate([raw[:72, :128], raw[72:, 128:]], 0)
                    d_raw = jnp.concatenate([d_raw[:72, :128], d_raw[72:, 128:]], 0)
                    bias = jnp.concatenate([same, same], 0)
                score = raw * (SCALE * LOG2E) + bias
                power = jnp.exp2(score - jnp.max(score, -1, keepdims=True))
                probs = power * (1.0 / jnp.sum(power, -1, keepdims=True))
                dot_sum = jnp.sum(d_raw * probs, -1, keepdims=True)
                d_score = probs * (d_raw - dot_sum)
                if w == 0:
                    probs_low = probs.astype(BF16)
                    score_low = d_score.astype(BF16)
                    blocks = (d_score[:72, :128] + d_score[72:, 128:], d_score[:72, 128:], d_score[72:, :128])
                else:
                    def wide(a):
                        top = jnp.concatenate([a[:72], zero], 1)
                        return jnp.concatenate([top, jnp.concatenate([zero, a[72:]], 1)], 0).astype(BF16)

                    probs_low = wide(probs)
                    score_low = wide(d_score)
                    blocks = (d_score[:72] + d_score[72:],)
                for b, block in enumerate(blocks):
                    turned_back = jnp.take_along_axis(block, back, axis=1)
                    early = jnp.where(first, turned_back, 0.0)
                    late = turned_back - early
                    d_tables[w, head, :, b * 256 : b * 256 + 128] = jnp.sum(early.reshape(9, 8, 128), 0)
                    d_tables[w, head, :, b * 256 + 128 : b * 256 + 256] = jnp.sum(late.reshape(9, 8, 128), 0)
                ctx_sum += dot(probs_low, v_head)
                both = dot(score_low, k_head)
                dq_sum += both[:, :128]
                feat_sum += both[:, 128:]
                head_rows = pl.ds(pl.multiple_of(g * 128 + hh * 32, 32), 32)
                dkv_t[w, 0, head_rows, :] = dot(turned[w, 0, head_rows, :], score_low) * SCALE
                dkv_t[w, 1, head_rows, :] = dot(turned[w, 1, head_rows, :], probs_low)
            ctx_acc[rows, lanes] = ctx_sum.astype(BF16)
            dq_acc[rows, lanes] = dq_sum * SCALE
            f_acc[w] += feat_sum
        return carry

    lax.fori_loop(0, 3, group_step, 0)

    for w in range(2):
        table = functools.reduce(jnp.add, [dot(part, onehot[...], NT) for part in split(jnp.sum(d_tables[w], 1), 2)])
        for half in range(2):
            for k in range(3):
                at = 128 * (3 * half + k)
                tp[w, half, 16 * k : 16 * k + 16, :] = table[:, at : at + 128].astype(BF16)

    low[:, :WIDTH] = dq_acc[...].astype(BF16)
    sums = [jnp.sum(dq_acc[...], 0, keepdims=True)]
    for part in range(2):
        total = jnp.zeros((1, WIDTH), F32)
        for w in range(2):
            token_rows = dot(c_spread[...], dkv_t[w, part].astype(BF16), (((0,), (1,)), ((), ())))
            total += jnp.sum(token_rows, 0, keepdims=True)
            low[w * WT : (w + 1) * WT, WIDTH * (part + 1) : WIDTH * (part + 2)] = token_rows.astype(BF16)
        sums.append(total)
    d_normed = dot(low[...], w_qkv[...], NT).astype(BF16).astype(F32)
    scaled = d_normed * gain_row
    first_mean = jnp.mean(scaled, -1, keepdims=True)
    second_mean = jnp.mean(scaled * white[...], -1, keepdims=True)
    d_inputs = dy_low[...].astype(F32) + inv_std[...] * (scaled - first_mean - white[...] * second_mean)
    dq_acc[...] = d_inputs
    for j in range(3):
        cols = slice(128 * j, 128 * j + 128)
        for k in range(4):
            level = (1, 2, 3, 0)[k]
            strided[pl.ds(576 * j + level, 72, stride=8), :] = dq_acc[72 * k : 72 * k + 72, cols]
        gx[:, :, :, cols] = mixed[j, :, 0:4, :].astype(BF16).reshape(6, 12, 4, 128)
    sums.append(jnp.sum(dy_low[...].astype(F32), 0, keepdims=True))
    sums.append(jnp.sum(d_normed * white[...], 0, keepdims=True))
    sums.append(jnp.sum(d_normed, 0, keepdims=True))
    d_surf = functools.reduce(jnp.add, [dot(of_query, part, TN) for part in split(f_acc[0] + f_acc[1], 2)])

    for j in range(4):
        if j < 3:
            grad = dot(normed[...], low[:, j * WIDTH : (j + 1) * WIDTH], TN)
        else:
            grad = dot(ctx_acc[...], dy_low[...], TN)
        for i in range(8):
            n = i * 4 + j
            for m in range(3):
                wp[n // PLANE, n % PLANE, 48 * m : 48 * m + 48, :] = grad[
                    48 * i : 48 * i + 48, 128 * m : 128 * m + 128
                ].astype(BF16)
    extra_row = lax.broadcasted_iota(jnp.int32, (16, 128), 0) == 12
    for n in range(2 * PLANE):
        if n < 18:
            row = sums[n // 3][:, 128 * (n % 3) : 128 * (n % 3) + 128]
        elif n < 22:
            row = d_surf[n - 18 : n - 17, :]
        else:
            row = jnp.zeros((1, 128), F32)
        wp[n // PLANE, n % PLANE, 144:160, :] = jnp.where(extra_row, row, 0.0).astype(BF16)

    core, x, y, z, here = place.core, place.x, place.y, place.z, place.here

    order = list(range(1, PLANE)) + [0]
    core_copies = {}
    t_copy = send(tp.at[1 - core], tc_recv, t_sems, 0, place.sibling)
    for step in order:
        at = place.in_plane(step, 1)[2]
        core_copies[step] = send(wp.at[1 - core, at], c_recv.at[step], c_sems, step, place.sibling)

    halo = [
        send(quadrant(gx, q), quadrant(gx_out, 3 - q), h_sems, q - 1, to)
        for q, to in ((1, place.east), (2, place.north), (3, place.north_east))
    ]
    own = pltpu.make_async_copy(quadrant(gx, 0), quadrant(gx_out, 3), local.at[3])
    own.start()

    t_copy.wait()
    t_mine = lax.rem(x, 2)
    t_send[...] = (tp[core, 1 - t_mine].astype(F32) + tc_recv[1 - t_mine].astype(F32)).astype(BF16)
    tx_copy = send(t_send, t_recv, t_sems, 1, place.x_pair)
    plane_copies = []
    for step in range(1, PLANE):
        x_at, y_at, at = place.in_plane(step, 1)
        core_copies[step].wait()
        p_send[step] = (wp[core, at].astype(F32) + c_recv[step].astype(F32)).astype(BF16)
        plane_copies.append(send(p_send.at[step], p_recv.at[step], p_sems, step, place.device(x_at, y_at, z, core)))
    core_copies[0].wait()
    total = wp[core, here].astype(F32) + c_recv[0].astype(F32)
    tx_copy.wait()
    t_total = tp[core, t_mine].astype(F32) + tc_recv[t_mine].astype(F32) + t_recv[...].astype(F32)
    for step in range(1, PLANE):
        plane_copies[step - 1].wait()
        total = total + p_recv[step].astype(F32)
    z_own[0:144, :] = total[:144]
    z_own[144:160, :] = total[144:] + t_total[:16]
    z_own[160:192, :] = t_total[16:]

    for k in range(PZ):
        z_send[k] = z_own[24 * k : 24 * k + 24, :].astype(BF16)
    z_copies = []
    for step in range(1, PZ):
        z_at = lax.rem(z + step, PZ)
        z_copies.append(send(z_send.at[z_at], z_recv.at[step], z_sems, step, place.device(x, y, z_at, core)))
    summed = z_own[pl.ds(pl.multiple_of(24 * z, 8), 24), :]
    for step in range(1, PZ):
        z_copies[step - 1].wait()
        summed = summed + z_recv[step].astype(F32)
    z_full[z] = summed.astype(BF16)
    a_copies = []
    for step in range(1, PZ):
        z_at = lax.rem(z + step, PZ)
        a_copies.append(send(z_full.at[z], z_full.at[z], a_sems, step, place.device(x, y, z_at, core)))
    for copy in a_copies:
        copy.wait()
    full[core, here] = jnp.concatenate([z_full[k].astype(F32) for k in range(PZ)], 0).astype(BF16)

    g_copies = []
    for step in range(1, PLANE):
        x_at, y_at, _ = place.in_plane(step, 1)
        g_copies.append(send(full.at[core, here], full.at[core, here], g_sems, step, place.device(x_at, y_at, z, core)))
    k_copies = [send(full.at[core, here], full.at[core, here], k_sems, 0, place.sibling)]
    for step in range(1, PLANE):
        at = place.in_plane(step, -1)[2]
        g_copies[step - 1].wait()
        k_copies.append(send(full.at[core, at], full.at[core, at], k_sems, step, place.sibling))
    for copy in k_copies + halo:
        copy.wait()
    own.wait()


def step(*operands):
    sems = pltpu.SemaphoreType.DMA
    return pl.pallas_call(
        step_kernel,
        out_shape=(
            jax.ShapeDtypeStruct((2, PLANE, 192, 128), BF16),
            jax.ShapeDtypeStruct((6, 12, 4, WIDTH), BF16),
        ),
        in_specs=[VMEM] * len(operands),
        out_specs=(VMEM, VMEM),
        scratch_shapes=[
            pltpu.VMEM((6, 12, 4, WIDTH), BF16),
            pltpu.VMEM((6, 12, 4, WIDTH), BF16),
            pltpu.VMEM((4, 8, 128), F32),
            pltpu.VMEM((4, 8, 128), F32),
            pltpu.VMEM((128, 128), F32),
            pltpu.VMEM((2, PLANE, 160, 128), BF16),
            pltpu.VMEM((2, 2, 48, 128), BF16),
            pltpu.VMEM((6, 12, 4, WIDTH), BF16),
            pltpu.VMEM((3, 72, 8, 128), F32),
            pltpu.VMEM((288, WIDTH), F32),
            pltpu.VMEM((288, 1), F32),
            pltpu.VMEM((288, WIDTH), BF16),
            pltpu.VMEM((288, WIDTH), BF16),
            pltpu.VMEM((288, 3 * WIDTH), BF16),
            pltpu.VMEM((288, WIDTH), BF16),
            pltpu.VMEM((2, 2, WIDTH, WT), BF16),
            pltpu.VMEM((2, KEYS, 2 * WIDTH), BF16),
            pltpu.VMEM((WT, 128), BF16),
            pltpu.VMEM((KEYS, 128), BF16),
            pltpu.VMEM((768, 768), BF16),
            pltpu.VMEM((2, 16, 768), F32),
            pltpu.VMEM((2, 16, 8, 768), F32),
            pltpu.VMEM((288, WIDTH), BF16),
            pltpu.VMEM((288, WIDTH), F32),
            pltpu.VMEM((2, WT, 128), F32),
            pltpu.VMEM((2, 2, WIDTH, KEYS), F32),
            pltpu.VMEM((288, 3 * WIDTH), BF16),
            pltpu.VMEM((2, 16, 768), F32),
            pltpu.VMEM((PLANE, 160, 128), BF16),
            pltpu.VMEM((2, 48, 128), BF16),
            pltpu.VMEM((48, 128), BF16),
            pltpu.VMEM((48, 128), BF16),
            pltpu.VMEM((PLANE, 160, 128), BF16),
            pltpu.VMEM((PLANE, 160, 128), BF16),
            pltpu.VMEM((192, 128), F32),
            pltpu.VMEM((PZ, 24, 128), BF16),
            pltpu.VMEM((PZ, 24, 128), BF16),
            pltpu.VMEM((PZ, 24, 128), BF16),
            sems((2, 9)),
            sems((2, 3)),
            sems((2, PLANE)),
            sems((2, 2)),
            sems((2, PLANE)),
            sems((2, PZ)),
            sems((2, PZ)),
            sems((2, PLANE)),
            sems((2, PLANE)),
            sems((4,)),
        ],
        compiler_params=pltpu.CompilerParams(
            collective_id=0, has_side_effects=True, vmem_limit_bytes=56 * 1024 * 1024
        ),
        name="step",
    )(*operands)


def finish_kernel(grad_scale, full, gx, o_gx, o_wqkv, o_bqkv, o_wproj, o_bproj, o_gain, o_shift, o_pos, o_surf):
    o_gx[...] = gx[...]
    for j in range(4):
        for i in range(8):
            n = i * 4 + j
            for m in range(3):
                part = full[n // PLANE, n % PLANE, 48 * m : 48 * m + 48, :].astype(F32) * grad_scale
                if j < 3:
                    o_wqkv[48 * i : 48 * i + 48, WIDTH * j + 128 * m : WIDTH * j + 128 * m + 128] = part
                else:
                    o_wproj[48 * i : 48 * i + 48, 128 * m : 128 * m + 128] = part
    for core in range(2):
        for at in range(PLANE):
            x, y = at % PX, at // PX
            kind = (y * 2 + x // 2) * 2 + core
            for k in range(3):
                part = full[core, at, 144 + 16 * k : 160 + 16 * k, :].astype(F32) * grad_scale
                lo = 128 * (3 * (x % 2) + k)
                width = min(128, SLOTS - lo)
                for h in range(HEADS):
                    o_pos[16 * h + kind : 16 * h + kind + 1, lo : lo + width] = part[h : h + 1, :width]

    def extra(n):
        tile = full[n // PLANE, n % PLANE, 144:160, :].astype(F32) * grad_scale
        return tile[12:13, :]

    o_bqkv[...] = jnp.concatenate([extra(n) for n in range(9)], 1).reshape(3 * WIDTH)
    for v, out in enumerate((o_bproj, o_gain, o_shift)):
        out[...] = jnp.concatenate([extra(9 + 3 * v + m) for m in range(3)], 1).reshape(WIDTH)
    for a in range(4):
        side = extra(18 + a)
        for b in range(4):
            o_surf[a, b : b + 1, :] = side[:, 12 * b : 12 * b + 12]


def finish(full, gx, grad_scale):
    one = lambda *shape: jax.ShapeDtypeStruct(shape, F32)
    return pl.pallas_call(
        functools.partial(finish_kernel, grad_scale),
        out_shape=(
            jax.ShapeDtypeStruct((6, 12, 4, WIDTH), BF16),
            one(WIDTH, 3 * WIDTH),
            one(3 * WIDTH),
            one(WIDTH, WIDTH),
            one(WIDTH),
            one(WIDTH),
            one(WIDTH),
            one(HEADS * 16, SLOTS),
            one(4, 4, HEADS),
        ),
        in_specs=[VMEM] * 2,
        out_specs=(VMEM,) * 9,
        compiler_params=pltpu.CompilerParams(vmem_limit_bytes=32 * 1024 * 1024),
        name="finish",
    )(full, gx)


def on_device(
    inputs, cotangent, land_sea, rel_index, norm_gain, norm_shift, w_qkv, b_qkv, w_proj, pos_bias, surf_bias
):
    levels, lat_rows, lon_cols, width = inputs.shape
    count = levels * lat_rows * lon_cols * lax.axis_size("lat") * lax.axis_size("lon")
    full, gx = step(
        inputs.transpose(1, 2, 0, 3),
        cotangent.transpose(1, 2, 0, 3),
        land_sea,
        rel_index,
        norm_gain,
        norm_shift,
        w_qkv,
        b_qkv,
        w_proj,
        pos_bias.transpose(1, 0, 2).reshape(-1, SLOTS),
        surf_bias.transpose(1, 2, 0),
        *(jnp.asarray(a) for a in constants()),
    )
    outs = finish(full, gx, float(count) ** -0.5)
    g_x, g_wqkv, g_bqkv, g_wproj, g_bproj, g_gain, g_shift, g_pos, g_surf = outs
    return (
        g_x.transpose(2, 0, 1, 3),
        g_wqkv,
        g_bqkv,
        g_wproj,
        g_bproj,
        g_gain,
        g_shift,
        g_pos.reshape(HEADS, 16, SLOTS).transpose(1, 0, 2),
        g_surf.transpose(2, 0, 1),
    )


def solution(mesh):
    in_specs = (P(None, "lat", "lon", None), P(None, "lat", "lon", None), P("lat", "lon")) + (P(),) * 8
    out_specs = (P(None, "lat", "lon", None),) + (P(),) * 8
    return jax.shard_map(on_device, mesh=mesh, in_specs=in_specs, out_specs=out_specs, check_vma=False)
```

```python
import functools

import jax
import jax.numpy as jnp
import ml_dtypes
import numpy as np
from jax import lax
from jax.experimental import pallas as pl
from jax.experimental.pallas import tpu as pltpu
from jax.sharding import PartitionSpec as P

F32 = jnp.float32
BF16 = jnp.bfloat16
MESH = pl.DeviceIdType.MESH
EPS = 1e-05
LOG2E = 1.4426950408889634
BIG = 2.0**33
HEADS = 12
SLOTS = 759
WIDTH = 384
WT = 144
PITCH = 23
KEYS = 256
SCALE = 32.0**-0.5
NT = (((1,), (1,)), ((), ()))
TN = (((0,), (0,)), ((), ()))
NN = (((1,), (0,)), ((), ()))
PX, PY, PZ = 4, 4, 8
PLANE = PX * PY
VMEM = pl.BlockSpec(memory_space=pltpu.VMEM)


def dot(a, b, dims=NN):
    return lax.dot_general(a, b, dims, preferred_element_type=F32)


def constants():
    spread = np.zeros((KEYS, WT), np.float32)
    of_row = np.zeros((WT, 32), np.float32)
    of_col = np.zeros((WT, 128), np.float32)
    for k in range(WT):
        li, ri, ci = k // 72, k // 12 % 6, k % 12
        spread[li * 128 + PITCH * ri + ci, k] = 1
        of_row[k, 8 * (2 * (ri // 3) + ci // 6) + ri % 3] = 1
        of_col[k, ci % 6] = 1
    return tuple(a.astype(ml_dtypes.bfloat16) for a in (spread, of_row, of_col))


class Place:
    def __init__(self):
        lat, lon = lax.axis_index("lat"), lax.axis_index("lon")
        n_lat, n_lon = lax.axis_size("lat"), lax.axis_size("lon")
        self.lat, self.n_lat = lat, n_lat
        self.core = lax.rem(lon, 2)
        self.z = lax.rem(lon // 2, PZ)
        self.x = lax.rem(lat, 2) * 2 + lon // (2 * PZ)
        self.y = lat // 2
        self.here = self.y * PX + self.x
        up, down = lax.rem(lat + 1, n_lat), lax.rem(lat + n_lat - 1, n_lat)
        right, left = lax.rem(lon + 1, n_lon), lax.rem(lon + n_lon - 1, n_lon)
        self.north, self.south = (up, lon), (down, lon)
        self.east, self.west = (lat, right), (lat, left)
        self.north_east, self.south_west = (up, right), (down, left)
        self.sibling = (lat, lon + 1 - 2 * self.core)
        self.x_pair = self.device(self.x + 1 - 2 * lax.rem(self.x, 2), self.y, self.z, self.core)

    def device(self, x, y, z, core):
        return (y * 2 + x // 2, (lax.rem(x, 2) * PZ + z) * 2 + core)

    def in_plane(self, step, sign):
        x = lax.rem(self.x + PX + sign * (step % PX), PX)
        y = lax.rem(self.y + PY + sign * (step // PX), PY)
        return x, y, y * PX + x

    def greet(self):
        others = [self.north, self.south, self.east, self.west, self.north_east, self.south_west, self.sibling]
        for step in range(1, PLANE):
            x, y, _ = self.in_plane(step, -1)
            others.append(self.device(x, y, self.z, self.core))
        for step in range(1, PZ):
            others.append(self.device(self.x, self.y, lax.rem(self.z + PZ - step, PZ), self.core))
        for other in others:
            pl.semaphore_signal(pltpu.get_barrier_semaphore(), inc=1, device_id=other, device_id_type=MESH)
        self.greeted = len(others)

    def meet(self):
        pl.semaphore_wait(pltpu.get_barrier_semaphore(), self.greeted)


def send(src, dst, sems, k, to):
    copy = pltpu.make_async_remote_copy(
        src_ref=src,
        dst_ref=dst,
        send_sem=sems.at[0, k],
        recv_sem=sems.at[1, k],
        device_id=to,
        device_id_type=MESH,
    )
    copy.start()
    return copy


def plain_rows():
    rows = lax.broadcasted_iota(jnp.int32, (72, 128), 0)
    return rows + (PITCH - 12) * (rows // 12)


def skew_parts(rows):
    lane = lax.broadcasted_iota(jnp.int32, (72, 128), 1)
    first = lane + rows >= PITCH * 5 + 11
    there = jnp.bitwise_and(lane - rows - 2, 127)
    back = jnp.bitwise_and(lane + rows + 2, 127)
    return first, there, back


def skew(table, first, there):
    mixed = jnp.where(first, table[:, :128], table[:, 128:])
    return jnp.take_along_axis(mixed, there, axis=1)


def split(values, count):
    pieces = []
    for _ in range(count):
        piece = values.astype(BF16)
        pieces.append(piece)
        values = values - piece.astype(F32)
    return pieces


def step_kernel(
    x_in, dy_in, land, rel, gain, shift, w_qkv_in, b_qkv, w_proj_in, pos_in, surf, c_spread, c_row, c_col,
    full_b, full_c, gx_out,
    w_qkv, w_proj, pos,
    tok_x, tok_dy, cls_out, cls_in, side_in, tp, tp_low, gx,
    mixed, white, inv_std, normed, normed_t, dy_low, qkv, dctx, turned, kv_pad, q_feat, k_feat,
    onehot, tables, d_tables, ctx_acc, dq_acc, f_acc, dkv_t, low, table_in,
    wp, c_recv, p_send, p_recv, tc_recv, t_send, t_recv, z_own, z_send, z_recv, z_full,
    f_sems, h_sems, c_sems, t_sems, p_sems, z_sems, a_sems, bx_sems, by_sems, cx_sems, cy_sems, k_sems, local,
):
    place = Place()
    core, x, y, z, here = place.core, place.x, place.y, place.z, place.here
    place.greet()
    fetches = [
        pltpu.make_async_copy(a, b, local.at[4 + k])
        for k, (a, b) in enumerate(((pos_in, pos), (w_qkv_in, w_qkv), (w_proj_in, w_proj)))
    ]
    for copy in fetches:
        copy.start()

    cls_out[...] = jnp.zeros_like(cls_out)
    for q in range(4):
        cls_out[q, :3, :6] = land[3 * (q // 2) : 3 * (q // 2) + 3, 6 * (q % 2) : 6 * (q % 2) + 6].astype(F32)

    def quadrant(ref, q):
        return ref.at[pl.ds(3 * (q // 2), 3), pl.ds(6 * (q % 2), 6)]

    place.meet()
    routes = ((0, place.south_west), (1, place.south), (2, place.west))
    halo_x = [send(quadrant(x_in, q), quadrant(tok_x, 3 - q), f_sems, q, to) for q, to in routes]
    halo_x += [send(cls_out.at[q], cls_in.at[3 - q], f_sems, 3 + q, to) for q, to in routes]
    halo_dy = [send(quadrant(dy_in, q), quadrant(tok_dy, 3 - q), f_sems, 6 + q, to) for q, to in routes]
    own_x = pltpu.make_async_copy(quadrant(x_in, 3), quadrant(tok_x, 0), local.at[0])
    own_dy = pltpu.make_async_copy(quadrant(dy_in, 3), quadrant(tok_dy, 0), local.at[1])
    own_cls = pltpu.make_async_copy(cls_out.at[3], cls_in.at[0], local.at[2])
    for copy in (own_x, own_dy, own_cls):
        copy.start()

    lat = place.lat
    last_band = lat == place.n_lat - 1
    for copy in fetches:
        copy.wait()
    rel_now = rel[...]
    rel_low = jnp.bitwise_and(rel_now, 15)
    rel_wide = dot((rel_now - rel_low).astype(F32).astype(BF16), c_spread[...], NT) + dot(
        rel_low.astype(F32).astype(BF16), c_spread[...], NT
    )
    rel_lane = jnp.bitwise_and(lax.broadcasted_iota(jnp.int32, (WT, KEYS), 1), 127)
    rel_wide = jnp.where(lax.rem(rel_lane, PITCH) < 12, rel_wide, -1.0)
    first, _, back = skew_parts(plain_rows())
    slot = lax.broadcasted_iota(jnp.int32, (768, 128), 0).astype(F32)
    for b, block in enumerate((rel_wide[:72, :128], rel_wide[:72, 128:], rel_wide[72:, :128])):
        turned_back = jnp.take_along_axis(block, back, axis=1)
        for half in range(2):
            kept = jnp.where(first, turned_back, -1.0) if half == 0 else jnp.where(first, -1.0, turned_back)
            slots = jnp.max(kept, 0, keepdims=True)
            lanes = slice(b * 256 + half * 128, b * 256 + half * 128 + 128)
            onehot[:, lanes] = jnp.where(slot == slots, 1.0, 0.0).astype(BF16)
    table_in[...] = jnp.zeros_like(table_in)
    for w in range(2):
        for h in range(HEADS):
            table_in[w, h : h + 1, :SLOTS] = pos[pl.ds(16 * h + 2 * lat + w, 1), :] * LOG2E
        tables[w] = functools.reduce(jnp.add, [dot(part, onehot[...]) for part in split(table_in[w], 3)])

    eye = (
        lax.broadcasted_iota(jnp.int32, (WIDTH, WIDTH), 0) == lax.broadcasted_iota(jnp.int32, (WIDTH, WIDTH), 1)
    ).astype(F32).astype(BF16)
    strided = mixed.reshape(3 * 576, 128)

    def in_order(tok, first_row, out):
        for j in range(3):
            cols = slice(128 * j, 128 * j + 128)
            mixed[j, :, first_row : first_row + 4, :] = tok[:, :, :, cols].reshape(72, 4, 128).astype(F32)
        for k in range(4):
            level = (1, 2, 3, 0)[k]
            for j in range(3):
                out[72 * k : 72 * k + 72, 128 * j : 128 * j + 128] = strided[
                    pl.ds(576 * j + first_row + level, 72, stride=8), :
                ]

    for copy in halo_x + [own_x, own_cls]:
        copy.wait()
    in_order(tok_x, 0, white)
    tokens = white[...]
    centred = tokens - jnp.mean(tokens, -1, keepdims=True)
    inv = lax.rsqrt(jnp.mean(centred * centred, -1, keepdims=True) + EPS)
    inv_std[...] = inv
    whitened = centred * inv
    white[...] = whitened
    gain_row = gain[...].reshape(1, WIDTH)
    normed[...] = (whitened * gain_row + shift[...].reshape(1, WIDTH)).astype(BF16)
    qkv[...] = (dot(normed[...], w_qkv[...]) + b_qkv[...].reshape(1, 3 * WIDTH)).astype(BF16)
    normed_t[...] = dot(eye, normed[...], NT).astype(BF16)
    for w in range(2):
        rows = slice(w * WT, (w + 1) * WT)
        turned[w, 0] = dot(eye, qkv[rows, :WIDTH], NT).astype(BF16)
        kv_pad[w] = dot(c_spread[...], qkv[rows, WIDTH:]).astype(BF16)

    lane = lax.broadcasted_iota(jnp.int32, (WT, 128), 1)
    token = lax.broadcasted_iota(jnp.int32, (WT, 128), 0)
    cells = dot(c_row[...], cls_in[...].reshape(32, 128).astype(BF16)) * c_col[...].astype(F32)
    kind = dot(cells.astype(BF16), jnp.ones((128, 128), BF16)).astype(jnp.int32)
    turned_over = jnp.logical_and(lax.rem(token, 72) >= 36, last_band).astype(F32)
    of_key = jnp.where(kind == lax.rem(lane, 48) // 12, 1.0, 0.0)
    of_query = jnp.where(kind == lane, 1.0, 0.0).astype(BF16)
    side_in[...] = jnp.zeros_like(side_in)
    for a in range(4):
        for b in range(4):
            side_in[a : a + 1, 12 * b : 12 * b + 12] = surf[a, b : b + 1, :]
            side_in[a : a + 1, 48 + 12 * b : 60 + 12 * b] = surf[a, b : b + 1, :]
    surf_lane = lax.broadcasted_iota(jnp.int32, (128, 128), 1)
    surf_hi, surf_lo = split(side_in[...] * (1.0 / SCALE), 2)
    side = dot(of_query, jnp.where(surf_lane < 48, surf_hi.astype(F32), surf_lo.astype(F32)).astype(BF16))
    q_feat[...] = jnp.where(
        lane < 96, side, jnp.where(lane == 96, turned_over, jnp.where(lane == 97, 1.0 - turned_over, 0.0))
    ).astype(BF16)
    key_side = jnp.where(
        lane < 96,
        of_key,
        jnp.where(lane == 96, -BIG * (1.0 - turned_over), jnp.where(lane == 97, -BIG * turned_over, 0.0)),
    ).astype(BF16)
    key_lane = lax.broadcasted_iota(jnp.int32, (KEYS, 128), 1)
    key_row = jnp.bitwise_and(lax.broadcasted_iota(jnp.int32, (KEYS, 128), 0), 127)
    hidden = jnp.logical_and(lax.rem(key_row, PITCH) >= 12, jnp.logical_and(key_lane >= 96, key_lane < 98))
    k_feat[...] = jnp.where(hidden, -BIG, dot(c_spread[...], key_side)).astype(BF16)

    for copy in halo_dy + [own_dy]:
        copy.wait()
    in_order(tok_dy, 4, dq_acc)
    dy_low[...] = dq_acc[...].astype(BF16)
    dctx[...] = dot(dy_low[...], w_proj[...], NT).astype(BF16)
    for w in range(2):
        turned[w, 1] = dot(eye, dctx[w * WT : (w + 1) * WT, :], NT).astype(BF16)

    zero = jnp.zeros((72, 128), F32)

    def group_step(g):
        first, there, back = skew_parts(plain_rows())
        lanes = slice(g * 128, g * 128 + 128)
        v_lanes = slice(WIDTH + g * 128, WIDTH + g * 128 + 128)
        cat_lane = lax.broadcasted_iota(jnp.int32, (1, 256), 1)
        feat_lane = cat_lane - 128
        for w in range(2):
            rows = slice(w * WT, (w + 1) * WT)
            q_cat = jnp.concatenate([qkv[rows, lanes], q_feat[...]], 1)
            k_cat = jnp.concatenate([kv_pad[w, :, lanes], k_feat[...]], 1)
            v_now = kv_pad[w, :, v_lanes]
            dctx_now = dctx[rows, lanes]
            ctx_sum = jnp.zeros((WT, 128), F32)
            dq_sum = jnp.zeros((WT, 128), F32)
            feat_sum = jnp.zeros((WT, 128), F32)
            for hh in range(4):
                head = g * 4 + hh
                mine = cat_lane // 32 == hh
                feat_mine = jnp.logical_and(
                    cat_lane >= 128,
                    jnp.logical_or(feat_lane >= 96, lax.rem(feat_lane + 132, 12) == head),
                )
                keep = jnp.logical_or(mine, feat_mine).astype(F32).astype(BF16)
                k_head = k_cat * keep
                v_head = v_now * keep[:, :128]
                raw = dot(q_cat, k_head, NT)
                d_raw = dot(dctx_now, v_head, NT)
                table = tables[w, head : head + 1, :]
                same = skew(table[:, :256], first, there)
                if w == 0:
                    upper = jnp.concatenate([same, skew(table[:, 256:512], first, there)], 1)
                    lower = jnp.concatenate([skew(table[:, 512:], first, there), same], 1)
                    bias = jnp.concatenate([upper, lower], 0)
                else:
                    raw = jnp.concatenate([raw[:72, :128], raw[72:, 128:]], 0)
                    d_raw = jnp.concatenate([d_raw[:72, :128], d_raw[72:, 128:]], 0)
                    bias = jnp.concatenate([same, same], 0)
                score = raw * (SCALE * LOG2E) + bias
                power = jnp.exp2(score - jnp.max(score, -1, keepdims=True))
                probs = power * (1.0 / jnp.sum(power, -1, keepdims=True))
                dot_sum = jnp.sum(d_raw * probs, -1, keepdims=True)
                d_score = probs * (d_raw - dot_sum)
                if w == 0:
                    probs_low = probs.astype(BF16)
                    score_low = d_score.astype(BF16)
                    blocks = (d_score[:72, :128] + d_score[72:, 128:], d_score[:72, 128:], d_score[72:, :128])
                else:
                    def wide(a):
                        top = jnp.concatenate([a[:72], zero], 1)
                        return jnp.concatenate([top, jnp.concatenate([zero, a[72:]], 1)], 0).astype(BF16)

                    probs_low = wide(probs)
                    score_low = wide(d_score)
                    blocks = (d_score[:72] + d_score[72:],)
                for b, block in enumerate(blocks):
                    turned_back = jnp.take_along_axis(block, back, axis=1)
                    early = jnp.where(first, turned_back, 0.0)
                    late = turned_back - early
                    d_tables[w, head, :, b * 256 : b * 256 + 128] = jnp.sum(early.reshape(9, 8, 128), 0)
                    d_tables[w, head, :, b * 256 + 128 : b * 256 + 256] = jnp.sum(late.reshape(9, 8, 128), 0)
                ctx_sum += dot(probs_low, v_head)
                both = dot(score_low, k_head)
                dq_sum += both[:, :128]
                feat_sum += both[:, 128:]
                head_rows = slice(head * 32, head * 32 + 32)
                dkv_t[w, 0, head_rows, :] = dot(turned[w, 0, head_rows, :], score_low) * SCALE
                dkv_t[w, 1, head_rows, :] = dot(turned[w, 1, head_rows, :], probs_low)
            ctx_acc[rows, lanes] = ctx_sum.astype(BF16)
            dq_acc[rows, lanes] = dq_sum * SCALE
            f_acc[w] += feat_sum

    sums = {}

    def weight_grads(g):
        lanes = slice(128 * g, 128 * g + 128)
        dq = dq_acc[:, lanes]
        low[:, lanes] = dq.astype(BF16)
        sums[0, g] = jnp.sum(dq, 0, keepdims=True)
        for part in range(2):
            total = jnp.zeros((1, 128), F32)
            for w in range(2):
                rows_now = dot(c_spread[...], dkv_t[w, part, lanes, :].astype(BF16), (((0,), (1,)), ((), ())))
                total += jnp.sum(rows_now, 0, keepdims=True)
                at = WIDTH * (part + 1) + 128 * g
                low[w * WT : (w + 1) * WT, at : at + 128] = rows_now.astype(BF16)
            sums[part + 1, g] = total
        for part in range(3):
            at = WIDTH * part + 128 * g
            grad = dot(normed_t[...], low[:, at : at + 128])
            for i in range(8):
                n = 3 * i + part
                wp[g, n // PLANE, n % PLANE] = grad[48 * i : 48 * i + 48, :].astype(BF16)
        grad = dot(ctx_acc[:, lanes], dy_low[...], TN)
        for u in range(8):
            n = 24 + u
            for m in range(3):
                wp[g, n // PLANE, n % PLANE, 16 * m : 16 * m + 16, :] = grad[
                    16 * u : 16 * u + 16, 128 * m : 128 * m + 128
                ].astype(BF16)
        return send(wp.at[g, 1 - core], c_recv.at[g], c_sems, g, place.sibling)

    def plane_sends(g, core_copy):
        core_copy.wait()
        copies = []
        for step in range(1, PLANE):
            x_at, y_at, at = place.in_plane(step, 1)
            p_send[g, step] = (wp[g, core, at].astype(F32) + c_recv[g, at].astype(F32)).astype(BF16)
            copies.append(
                send(
                    p_send.at[g, step], p_recv.at[g, step], p_sems, g * PLANE + step, place.device(x_at, y_at, z, core)
                )
            )
        return copies

    d_tables[...] = jnp.zeros_like(d_tables)
    f_acc[...] = jnp.zeros_like(f_acc)
    group_step(0)
    core_copies = [weight_grads(0)]
    group_step(1)
    plane_copies = [plane_sends(0, core_copies[0])]
    core_copies.append(weight_grads(1))
    group_step(2)
    plane_copies.append(plane_sends(1, core_copies[1]))
    core_copies.append(weight_grads(2))

    d_normed = dot(low[...], w_qkv[...], NT).astype(BF16).astype(F32)
    scaled = d_normed * gain_row
    first_mean = jnp.mean(scaled, -1, keepdims=True)
    second_mean = jnp.mean(scaled * white[...], -1, keepdims=True)
    dq_acc[...] = dy_low[...].astype(F32) + inv_std[...] * (scaled - first_mean - white[...] * second_mean)
    plane_copies.append(plane_sends(2, core_copies[2]))
    for j in range(3):
        cols = slice(128 * j, 128 * j + 128)
        for k in range(4):
            level = (1, 2, 3, 0)[k]
            strided[pl.ds(576 * j + level, 72, stride=8), :] = dq_acc[72 * k : 72 * k + 72, cols]
        gx[:, :, :, cols] = mixed[j, :, 0:4, :].astype(BF16).reshape(6, 12, 4, 128)
    home = [
        send(quadrant(gx, q), quadrant(gx_out, 3 - q), h_sems, q - 1, to)
        for q, to in ((1, place.east), (2, place.north), (3, place.north_east))
    ]
    own_gx = pltpu.make_async_copy(quadrant(gx, 0), quadrant(gx_out, 3), local.at[3])
    own_gx.start()

    for w in range(2):
        table = functools.reduce(jnp.add, [dot(part, onehot[...], NT) for part in split(jnp.sum(d_tables[w], 1), 2)])
        for half in range(2):
            for k in range(3):
                at = 128 * (3 * half + k)
                tp[w, half, 16 * k : 16 * k + 16, :] = table[:, at : at + 128]
    small = [sums[part, g] for part in range(3) for g in range(3)]
    for total in (
        jnp.sum(dy_low[...].astype(F32), 0, keepdims=True),
        jnp.sum(d_normed * white[...], 0, keepdims=True),
        jnp.sum(d_normed, 0, keepdims=True),
    ):
        small += [total[:, 128 * m : 128 * m + 128] for m in range(3)]
    d_surf = functools.reduce(jnp.add, [dot(of_query, part, TN) for part in split(f_acc[0] + f_acc[1], 2)])
    small += [d_surf[a : a + 1, :] for a in range(4)]
    for e, row in enumerate(small):
        w, half, at = small_row(e)
        tp[w, half, at : at + 1, :] = row
    tp_low[...] = tp[...].astype(BF16)
    t_copy = send(tp_low.at[1 - core], tc_recv, t_sems, 0, place.sibling)

    t_mine = lax.rem(x, 2)
    total = [wp[g, core, here].astype(F32) + c_recv[g, here].astype(F32) for g in range(3)]
    t_copy.wait()
    t_send[...] = (tp[core, 1 - t_mine] + tc_recv[1 - t_mine].astype(F32)).astype(BF16)
    tx_copy = send(t_send, t_recv, t_sems, 1, place.x_pair)
    t_total = tp[core, t_mine] + tc_recv[t_mine].astype(F32)
    for g in range(3):
        for step in range(1, PLANE):
            plane_copies[g][step - 1].wait()
            total[g] = total[g] + p_recv[g, step].astype(F32)
        z_own[48 * g : 48 * g + 48, :] = total[g]
    tx_copy.wait()
    z_own[144:192, :] = t_total + t_recv[...].astype(F32)

    for k in range(PZ):
        z_send[k] = z_own[24 * k : 24 * k + 24, :].astype(BF16)
    z_copies = []
    for step in (4, 3, 5, 2, 6, 1, 7):
        z_at = lax.rem(z + step, PZ)
        z_copies.append(send(z_send.at[z_at], z_recv.at[step], z_sems, step, place.device(x, y, z_at, core)))
    summed = z_own[pl.ds(pl.multiple_of(24 * z, 8), 24), :]
    for copy in z_copies:
        copy.wait()
    for step in range(1, PZ):
        summed = summed + z_recv[step].astype(F32)
    z_full[z] = summed.astype(BF16)
    a_copies = []
    for step in (4, 3, 5, 2, 6, 1, 7):
        z_at = lax.rem(z + step, PZ)
        a_copies.append(send(z_full.at[z], z_full.at[z], a_sems, step, place.device(x, y, z_at, core)))
    for copy in a_copies:
        copy.wait()
    full_b[core, y, x] = jnp.concatenate([z_full[k].astype(F32) for k in range(4)], 0).astype(BF16)
    full_c[core, x, y] = jnp.concatenate([z_full[k].astype(F32) for k in range(4, 8)], 0).astype(BF16)

    def x_away(step):
        return place.device(lax.rem(x + step, PX), y, z, core)

    def y_away(step):
        return place.device(x, lax.rem(y + step, PY), z, core)

    b_first, c_first, b_then, c_then, last = {}, {}, {}, {}, []
    for d in (2, 1, 3):
        b_first[d] = send(full_b.at[core, y, x], full_b.at[core, y, x], bx_sems, d, x_away(d))
        c_first[d] = send(full_c.at[core, x, y], full_c.at[core, x, y], cy_sems, d, y_away(d))
    for d in (2, 1, 3):
        b_then[0, d] = send(full_b.at[core, y, x], full_b.at[core, y, x], by_sems, d, y_away(d))
        c_then[0, d] = send(full_c.at[core, x, y], full_c.at[core, x, y], cx_sems, d, x_away(d))
    for e in (1, 3, 2):
        x_from, y_from = lax.rem(x + PX - e, PX), lax.rem(y + PY - e, PY)
        b_first[e].wait()
        for d in (2, 1, 3):
            b_then[e, d] = send(full_b.at[core, y, x_from], full_b.at[core, y, x_from], by_sems, 4 * e + d, y_away(d))
        c_first[e].wait()
        for d in (2, 1, 3):
            c_then[e, d] = send(full_c.at[core, x, y_from], full_c.at[core, x, y_from], cx_sems, 4 * e + d, x_away(d))
    last.append(send(full_b.at[core, y], full_b.at[core, y], k_sems, 0, place.sibling))
    last.append(send(full_c.at[core, x], full_c.at[core, x], k_sems, 4, place.sibling))
    for d in (1, 3, 2):
        x_from, y_from = lax.rem(x + PX - d, PX), lax.rem(y + PY - d, PY)
        for e in range(4):
            b_then[e, d].wait()
        last.append(send(full_b.at[core, y_from], full_b.at[core, y_from], k_sems, d, place.sibling))
        for e in range(4):
            c_then[e, d].wait()
        last.append(send(full_c.at[core, x_from], full_c.at[core, x_from], k_sems, 4 + d, place.sibling))
    for copy in last + home:
        copy.wait()
    own_gx.wait()


def step(*operands):
    sems = pltpu.SemaphoreType.DMA
    anywhere = pl.BlockSpec(memory_space=pl.ANY)
    in_specs = [VMEM] * len(operands)
    for k in (0, 1, 6, 8, 9):
        in_specs[k] = anywhere
    return pl.pallas_call(
        step_kernel,
        out_shape=(
            jax.ShapeDtypeStruct((2, PY, PX, 96, 128), BF16),
            jax.ShapeDtypeStruct((2, PX, PY, 96, 128), BF16),
            jax.ShapeDtypeStruct((6, 12, 4, WIDTH), BF16),
        ),
        in_specs=in_specs,
        out_specs=(VMEM, VMEM, VMEM),
        scratch_shapes=[
            pltpu.VMEM((WIDTH, 3 * WIDTH), BF16),
            pltpu.VMEM((WIDTH, WIDTH), BF16),
            pltpu.VMEM((HEADS * 16, SLOTS), F32),
            pltpu.VMEM((6, 12, 4, WIDTH), BF16),
            pltpu.VMEM((6, 12, 4, WIDTH), BF16),
            pltpu.VMEM((4, 8, 128), F32),
            pltpu.VMEM((4, 8, 128), F32),
            pltpu.VMEM((128, 128), F32),
            pltpu.VMEM((2, 2, 48, 128), F32),
            pltpu.VMEM((2, 2, 48, 128), BF16),
            pltpu.VMEM((6, 12, 4, WIDTH), BF16),
            pltpu.VMEM((3, 72, 8, 128), F32),
            pltpu.VMEM((288, WIDTH), F32),
            pltpu.VMEM((288, 1), F32),
            pltpu.VMEM((288, WIDTH), BF16),
            pltpu.VMEM((WIDTH, 288), BF16),
            pltpu.VMEM((288, WIDTH), BF16),
            pltpu.VMEM((288, 3 * WIDTH), BF16),
            pltpu.VMEM((288, WIDTH), BF16),
            pltpu.VMEM((2, 2, WIDTH, WT), BF16),
            pltpu.VMEM((2, KEYS, 2 * WIDTH), BF16),
            pltpu.VMEM((WT, 128), BF16),
            pltpu.VMEM((KEYS, 128), BF16),
            pltpu.VMEM((768, 768), BF16),
            pltpu.VMEM((2, 16, 768), F32),
            pltpu.VMEM((2, 16, 8, 768), F32),
            pltpu.VMEM((288, WIDTH), BF16),
            pltpu.VMEM((288, WIDTH), F32),
            pltpu.VMEM((2, WT, 128), F32),
            pltpu.VMEM((2, 2, WIDTH, KEYS), F32),
            pltpu.VMEM((288, 3 * WIDTH), BF16),
            pltpu.VMEM((2, 16, 768), F32),
            pltpu.VMEM((3, 2, PLANE, 48, 128), BF16),
            pltpu.VMEM((3, PLANE, 48, 128), BF16),
            pltpu.VMEM((3, PLANE, 48, 128), BF16),
            pltpu.VMEM((3, PLANE, 48, 128), BF16),
            pltpu.VMEM((2, 48, 128), BF16),
            pltpu.VMEM((48, 128), BF16),
            pltpu.VMEM((48, 128), BF16),
            pltpu.VMEM((192, 128), F32),
            pltpu.VMEM((PZ, 24, 128), BF16),
            pltpu.VMEM((PZ, 24, 128), BF16),
            pltpu.VMEM((PZ, 24, 128), BF16),
            sems((2, 9)),
            sems((2, 3)),
            sems((2, 3)),
            sems((2, 2)),
            sems((2, 3 * PLANE)),
            sems((2, PZ)),
            sems((2, PZ)),
            sems((2, 4)),
            sems((2, 16)),
            sems((2, 16)),
            sems((2, 4)),
            sems((2, 8)),
            sems((7,)),
        ],
        compiler_params=pltpu.CompilerParams(
            collective_id=0, has_side_effects=True, vmem_limit_bytes=60 * 1024 * 1024
        ),
        name="step",
    )(*operands)


def small_row(e):
    quarter, k = e // 6, e % 6
    return quarter // 2, quarter % 2, 16 * (k // 4) + 12 + k % 4


def finish_kernel(
    grad_scale, full_b, full_c, gx, o_gx, o_wqkv, o_bqkv, o_wproj, o_bproj, o_gain, o_shift, o_pos, o_surf
):
    o_gx[...] = gx[...]

    def chunk(core, at):
        x, y = at % PX, at // PX
        return full_b.at[core, y, x], full_c.at[core, x, y]

    for n in range(2 * PLANE):
        b, c = chunk(n // PLANE, n % PLANE)
        for g in range(3):
            source = (b, b, c)[g]
            rows = (0, 48, 0)[g]
            part = source[rows : rows + 48, :].astype(F32) * grad_scale
            if n < 24:
                i, at = n // 3, WIDTH * (n % 3) + 128 * g
                o_wqkv[48 * i : 48 * i + 48, at : at + 128] = part
            else:
                at = 128 * g + 16 * (n - 24)
                for m in range(3):
                    o_wproj[at : at + 16, 128 * m : 128 * m + 128] = part[16 * m : 16 * m + 16, :]

    quarters = {}
    for core in range(2):
        for at in range(PLANE):
            x, y = at % PX, at // PX
            kind = (y * 2 + x // 2) * 2 + core
            rows = chunk(core, at)[1][48:96, :].astype(F32) * grad_scale
            key = core, x % 2
            quarters[key] = rows if key not in quarters else quarters[key] + rows
            for k in range(3):
                lo = 128 * (3 * (x % 2) + k)
                width = min(128, SLOTS - lo)
                for h in range(HEADS):
                    o_pos[16 * h + kind : 16 * h + kind + 1, lo : lo + width] = rows[
                        16 * k + h : 16 * k + h + 1, :width
                    ]

    def small(e):
        w, half, at = small_row(e)
        return quarters[w, half][at : at + 1, :]

    o_bqkv[...] = jnp.concatenate([small(n) for n in range(9)], 1).reshape(3 * WIDTH)
    for v, out in enumerate((o_bproj, o_gain, o_shift)):
        out[...] = jnp.concatenate([small(9 + 3 * v + m) for m in range(3)], 1).reshape(WIDTH)
    for a in range(4):
        side = small(18 + a)
        for b in range(4):
            o_surf[a, b : b + 1, :] = side[:, 12 * b : 12 * b + 12]


def finish(full_b, full_c, gx, grad_scale):
    one = lambda *shape: jax.ShapeDtypeStruct(shape, F32)
    return pl.pallas_call(
        functools.partial(finish_kernel, grad_scale),
        out_shape=(
            jax.ShapeDtypeStruct((6, 12, 4, WIDTH), BF16),
            one(WIDTH, 3 * WIDTH),
            one(3 * WIDTH),
            one(WIDTH, WIDTH),
            one(WIDTH),
            one(WIDTH),
            one(WIDTH),
            one(HEADS * 16, SLOTS),
            one(4, 4, HEADS),
        ),
        in_specs=[VMEM] * 3,
        out_specs=(VMEM,) * 9,
        compiler_params=pltpu.CompilerParams(vmem_limit_bytes=60 * 1024 * 1024),
        name="finish",
    )(full_b, full_c, gx)


def on_device(
    inputs, cotangent, land_sea, rel_index, norm_gain, norm_shift, w_qkv, b_qkv, w_proj, pos_bias, surf_bias
):
    levels, lat_rows, lon_cols, width = inputs.shape
    count = levels * lat_rows * lon_cols * lax.axis_size("lat") * lax.axis_size("lon")
    full_b, full_c, gx = step(
        inputs.transpose(1, 2, 0, 3),
        cotangent.transpose(1, 2, 0, 3),
        land_sea,
        rel_index,
        norm_gain,
        norm_shift,
        w_qkv,
        b_qkv,
        w_proj,
        pos_bias.transpose(1, 0, 2).reshape(-1, SLOTS),
        surf_bias.transpose(1, 2, 0),
        *(jnp.asarray(a) for a in constants()),
    )
    outs = finish(full_b, full_c, gx, float(count) ** -0.5)
    g_x, g_wqkv, g_bqkv, g_wproj, g_bproj, g_gain, g_shift, g_pos, g_surf = outs
    return (
        g_x.transpose(2, 0, 1, 3),
        g_wqkv,
        g_bqkv,
        g_wproj,
        g_bproj,
        g_gain,
        g_shift,
        g_pos.reshape(HEADS, 16, SLOTS).transpose(1, 0, 2),
        g_surf.transpose(2, 0, 1),
    )


def solution(mesh):
    in_specs = (P(None, "lat", "lon", None), P(None, "lat", "lon", None), P("lat", "lon")) + (P(),) * 8
    out_specs = (P(None, "lat", "lon", None),) + (P(),) * 8
    return jax.shard_map(on_device, mesh=mesh, in_specs=in_specs, out_specs=out_specs, check_vma=False)
```

```python
import functools

import jax
import jax.numpy as jnp
import ml_dtypes
import numpy as np
from jax import lax
from jax.experimental import pallas as pl
from jax.experimental.pallas import tpu as pltpu
from jax.sharding import PartitionSpec as P

F32 = jnp.float32
BF16 = jnp.bfloat16
MESH = pl.DeviceIdType.MESH
EPS = 1e-05
LOG2E = 1.4426950408889634
BIG = 2.0**33
HEADS = 12
SLOTS = 759
WIDTH = 384
WT = 144
PITCH = 23
KEYS = 256
SCALE = 32.0**-0.5
NT = (((1,), (1,)), ((), ()))
TN = (((0,), (0,)), ((), ()))
NN = (((1,), (0,)), ((), ()))
PX, PY, PZ = 4, 4, 8
PLANE = PX * PY
VMEM = pl.BlockSpec(memory_space=pltpu.VMEM)


def dot(a, b, dims=NN):
    return lax.dot_general(a, b, dims, preferred_element_type=F32)


def constants():
    spread = np.zeros((KEYS, WT), np.float32)
    of_row = np.zeros((WT, 32), np.float32)
    of_col = np.zeros((WT, 128), np.float32)
    for k in range(WT):
        li, ri, ci = k // 72, k // 12 % 6, k % 12
        spread[li * 128 + PITCH * ri + ci, k] = 1
        of_row[k, 8 * (2 * (ri // 3) + ci // 6) + ri % 3] = 1
        of_col[k, ci % 6] = 1
    return tuple(a.astype(ml_dtypes.bfloat16) for a in (spread, spread.T, of_row, of_col))


class Place:
    def __init__(self):
        lat, lon = lax.axis_index("lat"), lax.axis_index("lon")
        n_lat, n_lon = lax.axis_size("lat"), lax.axis_size("lon")
        self.lat, self.n_lat = lat, n_lat
        self.core = lax.rem(lon, 2)
        self.z = lax.rem(lon // 2, PZ)
        self.x = lax.rem(lat, 2) * 2 + lon // (2 * PZ)
        self.y = lat // 2
        self.here = self.y * PX + self.x
        up, down = lax.rem(lat + 1, n_lat), lax.rem(lat + n_lat - 1, n_lat)
        right, left = lax.rem(lon + 1, n_lon), lax.rem(lon + n_lon - 1, n_lon)
        self.north, self.south = (up, lon), (down, lon)
        self.east, self.west = (lat, right), (lat, left)
        self.north_east, self.south_west = (up, right), (down, left)
        self.sibling = (lat, lon + 1 - 2 * self.core)
        self.x_pair = self.device(self.x + 1 - 2 * lax.rem(self.x, 2), self.y, self.z, self.core)

    def device(self, x, y, z, core):
        return (y * 2 + x // 2, (lax.rem(x, 2) * PZ + z) * 2 + core)

    def in_plane(self, step, sign):
        x = lax.rem(self.x + PX + sign * (step % PX), PX)
        y = lax.rem(self.y + PY + sign * (step // PX), PY)
        return x, y, y * PX + x

    def greet(self):
        others = [self.north, self.south, self.east, self.west, self.north_east, self.south_west, self.sibling]
        for step in range(1, PLANE):
            x, y, _ = self.in_plane(step, -1)
            others.append(self.device(x, y, self.z, self.core))
        for step in range(1, PZ):
            others.append(self.device(self.x, self.y, lax.rem(self.z + PZ - step, PZ), self.core))
        for other in others:
            pl.semaphore_signal(pltpu.get_barrier_semaphore(), inc=1, device_id=other, device_id_type=MESH)
        self.greeted = len(others)

    def meet(self):
        pl.semaphore_wait(pltpu.get_barrier_semaphore(), self.greeted)


def send(src, dst, sems, k, to):
    copy = pltpu.make_async_remote_copy(
        src_ref=src,
        dst_ref=dst,
        send_sem=sems.at[0, k],
        recv_sem=sems.at[1, k],
        device_id=to,
        device_id_type=MESH,
    )
    copy.start()
    return copy


def plain_rows():
    rows = lax.broadcasted_iota(jnp.int32, (72, 128), 0)
    return rows + (PITCH - 12) * (rows // 12)


def skew_parts(rows):
    lane = lax.broadcasted_iota(jnp.int32, (72, 128), 1)
    first = lane + rows >= PITCH * 5 + 11
    there = jnp.bitwise_and(lane - rows - 2, 127)
    back = jnp.bitwise_and(lane + rows + 2, 127)
    return first, there, back


def skew(table, first, there):
    mixed = jnp.where(first, table[:, :128], table[:, 128:])
    return jnp.take_along_axis(mixed, there, axis=1)


def split(values, count):
    pieces = []
    for _ in range(count):
        piece = values.astype(BF16)
        pieces.append(piece)
        values = values - piece.astype(F32)
    return pieces


def step_kernel(
    x_in, dy_in, land, rel, gain, shift, w_qkv_in, b_qkv, w_proj_in, pos_in, surf, c_spread, c_back, c_row, c_col,
    full_b, full_c, gx_out,
    w_qkv, w_proj, pos,
    tok_x, tok_dy, cls_out, cls_in, side_in, tp, tp_low, gx,
    mixed, white, inv_std, normed, normed_t, dy_low, qkv, dctx, turned, k_cat, k_cat_t, v_cat, v_turned, q_feat,
    onehot, tables, d_tables, ctx_acc, dq_acc, f_acc, dkv_t, low, table_in,
    wp, c_recv, p_send, p_recv, tc_recv, t_send, t_recv, z_own, z_send, z_recv, z_full,
    f_sems, h_sems, c_sems, t_sems, p_sems, z_sems, a_sems, bx_sems, by_sems, cx_sems, cy_sems, k_sems, local,
):
    place = Place()
    core, x, y, z, here = place.core, place.x, place.y, place.z, place.here
    place.greet()
    fetches = [
        pltpu.make_async_copy(a, b, local.at[4 + k])
        for k, (a, b) in enumerate(((pos_in, pos), (w_qkv_in, w_qkv), (w_proj_in, w_proj)))
    ]
    for copy in fetches:
        copy.start()

    cls_out[...] = jnp.zeros_like(cls_out)
    for q in range(4):
        cls_out[q, :3, :6] = land[3 * (q // 2) : 3 * (q // 2) + 3, 6 * (q % 2) : 6 * (q % 2) + 6].astype(F32)

    def quadrant(ref, q):
        return ref.at[pl.ds(3 * (q // 2), 3), pl.ds(6 * (q % 2), 6)]

    place.meet()
    routes = ((0, place.south_west), (1, place.south), (2, place.west))
    halo_x = [send(quadrant(x_in, q), quadrant(tok_x, 3 - q), f_sems, q, to) for q, to in routes]
    halo_x += [send(cls_out.at[q], cls_in.at[3 - q], f_sems, 3 + q, to) for q, to in routes]
    halo_dy = [send(quadrant(dy_in, q), quadrant(tok_dy, 3 - q), f_sems, 6 + q, to) for q, to in routes]
    own_x = pltpu.make_async_copy(quadrant(x_in, 3), quadrant(tok_x, 0), local.at[0])
    own_dy = pltpu.make_async_copy(quadrant(dy_in, 3), quadrant(tok_dy, 0), local.at[1])
    own_cls = pltpu.make_async_copy(cls_out.at[3], cls_in.at[0], local.at[2])
    for copy in (own_x, own_dy, own_cls):
        copy.start()

    lat = place.lat
    last_band = lat == place.n_lat - 1
    for copy in fetches:
        copy.wait()
    rel_now = rel[...]
    rel_low = jnp.bitwise_and(rel_now, 15)
    rel_wide = dot((rel_now - rel_low).astype(F32).astype(BF16), c_spread[...], NT) + dot(
        rel_low.astype(F32).astype(BF16), c_spread[...], NT
    )
    rel_lane = jnp.bitwise_and(lax.broadcasted_iota(jnp.int32, (WT, KEYS), 1), 127)
    rel_wide = jnp.where(lax.rem(rel_lane, PITCH) < 12, rel_wide, -1.0)
    first, _, back = skew_parts(plain_rows())
    slot = lax.broadcasted_iota(jnp.int32, (768, 128), 0).astype(F32)
    for b, block in enumerate((rel_wide[:72, :128], rel_wide[:72, 128:], rel_wide[72:, :128])):
        turned_back = jnp.take_along_axis(block, back, axis=1)
        for half in range(2):
            kept = jnp.where(first, turned_back, -1.0) if half == 0 else jnp.where(first, -1.0, turned_back)
            slots = jnp.max(kept, 0, keepdims=True)
            lanes = slice(b * 256 + half * 128, b * 256 + half * 128 + 128)
            onehot[:, lanes] = jnp.where(slot == slots, 1.0, 0.0).astype(BF16)
    table_in[...] = jnp.zeros_like(table_in)
    for w in range(2):
        for h in range(HEADS):
            table_in[w, h : h + 1, :SLOTS] = pos[pl.ds(16 * h + 2 * lat + w, 1), :] * LOG2E
        tables[w] = functools.reduce(jnp.add, [dot(part, onehot[...]) for part in split(table_in[w], 3)])

    eye = (
        lax.broadcasted_iota(jnp.int32, (WIDTH, WIDTH), 0) == lax.broadcasted_iota(jnp.int32, (WIDTH, WIDTH), 1)
    ).astype(F32).astype(BF16)
    strided = mixed.reshape(3 * 576, 128)

    def in_order(tok, first_row, out):
        for j in range(3):
            cols = slice(128 * j, 128 * j + 128)
            mixed[j, :, first_row : first_row + 4, :] = tok[:, :, :, cols].reshape(72, 4, 128).astype(F32)
        for k in range(4):
            level = (1, 2, 3, 0)[k]
            for j in range(3):
                out[72 * k : 72 * k + 72, 128 * j : 128 * j + 128] = strided[
                    pl.ds(576 * j + first_row + level, 72, stride=8), :
                ]

    for copy in halo_x + [own_x, own_cls]:
        copy.wait()
    in_order(tok_x, 0, white)
    tokens = white[...]
    centred = tokens - jnp.mean(tokens, -1, keepdims=True)
    inv = lax.rsqrt(jnp.mean(centred * centred, -1, keepdims=True) + EPS)
    inv_std[...] = inv
    whitened = centred * inv
    white[...] = whitened
    gain_row = gain[...].reshape(1, WIDTH)
    normed[...] = (whitened * gain_row + shift[...].reshape(1, WIDTH)).astype(BF16)
    qkv[...] = (dot(normed[...], w_qkv[...]) + b_qkv[...].reshape(1, 3 * WIDTH)).astype(BF16)
    normed_t[...] = dot(eye, normed[...], NT).astype(BF16)
    for w in range(2):
        rows = slice(w * WT, (w + 1) * WT)
        turned[w, 0] = dot(eye, qkv[rows, :WIDTH], NT).astype(BF16)
        padded = dot(c_spread[...], qkv[rows, WIDTH:]).astype(BF16)
        k_turned = dot(eye, padded[:, :WIDTH], NT).astype(BF16)
        v_turned[w] = dot(eye, padded[:, WIDTH:], NT).astype(BF16)
        for g in range(3):
            lanes = slice(128 * g, 128 * g + 128)
            k_cat[w, g, :, :128] = padded[:, lanes]
            k_cat_t[w, g, :128, :] = k_turned[lanes, :]
            v_cat[w, g, :, :128] = padded[:, WIDTH + 128 * g : WIDTH + 128 * g + 128]
            v_cat[w, g, :, 128:] = jnp.ones((KEYS, 128), BF16)

    lane = lax.broadcasted_iota(jnp.int32, (WT, 128), 1)
    token = lax.broadcasted_iota(jnp.int32, (WT, 128), 0)
    cells = dot(c_row[...], cls_in[...].reshape(32, 128).astype(BF16)) * c_col[...].astype(F32)
    kind = dot(cells.astype(BF16), jnp.ones((128, 128), BF16)).astype(jnp.int32)
    turned_over = jnp.logical_and(lax.rem(token, 72) >= 36, last_band).astype(F32)
    of_key = jnp.where(kind == lax.rem(lane, 48) // 12, 1.0, 0.0)
    of_query = jnp.where(kind == lane, 1.0, 0.0).astype(BF16)
    side_in[...] = jnp.zeros_like(side_in)
    for a in range(4):
        for b in range(4):
            side_in[a : a + 1, 12 * b : 12 * b + 12] = surf[a, b : b + 1, :]
            side_in[a : a + 1, 48 + 12 * b : 60 + 12 * b] = surf[a, b : b + 1, :]
    surf_lane = lax.broadcasted_iota(jnp.int32, (128, 128), 1)
    surf_hi, surf_lo = split(side_in[...] * (1.0 / SCALE), 2)
    side = dot(of_query, jnp.where(surf_lane < 48, surf_hi.astype(F32), surf_lo.astype(F32)).astype(BF16))
    q_feat[...] = jnp.where(
        lane < 96, side, jnp.where(lane == 96, turned_over, jnp.where(lane == 97, 1.0 - turned_over, 0.0))
    ).astype(BF16)
    key_side = jnp.where(
        lane < 96,
        of_key,
        jnp.where(lane == 96, -BIG * (1.0 - turned_over), jnp.where(lane == 97, -BIG * turned_over, 0.0)),
    ).astype(BF16)
    key_lane = lax.broadcasted_iota(jnp.int32, (KEYS, 128), 1)
    key_row = jnp.bitwise_and(lax.broadcasted_iota(jnp.int32, (KEYS, 128), 0), 127)
    hidden = jnp.logical_and(lax.rem(key_row, PITCH) >= 12, jnp.logical_and(key_lane >= 96, key_lane < 98))
    k_feat = jnp.where(hidden, -BIG, dot(c_spread[...], key_side)).astype(BF16)
    k_feat_t = dot(eye[:128, :128], k_feat, NT).astype(BF16)
    for w in range(2):
        for g in range(3):
            k_cat[w, g, :, 128:] = k_feat
            k_cat_t[w, g, 128:, :] = k_feat_t

    for copy in halo_dy + [own_dy]:
        copy.wait()
    in_order(tok_dy, 4, dq_acc)
    dy_low[...] = dq_acc[...].astype(BF16)
    dctx[...] = dot(dy_low[...], w_proj[...], NT).astype(BF16)
    for w in range(2):
        turned[w, 1] = dot(eye, dctx[w * WT : (w + 1) * WT, :], NT).astype(BF16)

    zero = jnp.zeros((72, 128), F32)
    cat_lane = lax.broadcasted_iota(jnp.int32, (1, 256), 1)
    half_lane = lax.broadcasted_iota(jnp.int32, (1, 128), 1)
    block_row = jnp.bitwise_and(lax.broadcasted_iota(jnp.int32, (256, 512), 0), 127)
    block_lane = lax.broadcasted_iota(jnp.int32, (256, 512), 1)
    blocks_of_ones = jnp.where(block_row // 32 == block_lane // 128, 1.0, 0.0).astype(BF16)
    first, there, back = skew_parts(plain_rows())

    def own_level(a):
        return jnp.concatenate([a[:72, :128], a[72:, 128:]], 0)

    def both_levels(a):
        top = jnp.concatenate([a[:72], zero], 1)
        return jnp.concatenate([top, jnp.concatenate([zero, a[72:]], 1)], 0)

    def group_step(g):
        lanes = slice(g * 128, g * 128 + 128)
        for w in range(2):
            rows = slice(w * WT, (w + 1) * WT)
            part = [slice(WT * hh, WT * hh + WT) for hh in range(4)]
            q_cat = jnp.concatenate([qkv[rows, lanes], q_feat[...]], 1)
            dctx_now = dctx[rows, lanes]
            q_all, dctx_all = [], []
            for hh in range(4):
                mine = cat_lane // 32 == hh
                feat_mine = jnp.logical_and(
                    cat_lane >= 128, jnp.logical_or(cat_lane >= 224, lax.rem(cat_lane + 4, 12) == g * 4 + hh)
                )
                keep = jnp.logical_or(mine, feat_mine).astype(F32).astype(BF16)
                q_all.append(q_cat * keep)
                dctx_all.append(dctx_now * keep[:, :128])
            raw_all = dot(jnp.concatenate(q_all, 0), k_cat_t[w, g])
            d_raw_all = dot(jnp.concatenate(dctx_all, 0), v_turned[w, lanes, :])
            powers = []
            for hh in range(4):
                head = g * 4 + hh
                raw = raw_all[part[hh]]
                table = tables[w, head : head + 1, :]
                same = skew(table[:, :256], first, there)
                if w == 0:
                    upper = jnp.concatenate([same, skew(table[:, 256:512], first, there)], 1)
                    lower = jnp.concatenate([skew(table[:, 512:], first, there), same], 1)
                    bias = jnp.concatenate([upper, lower], 0)
                else:
                    raw = own_level(raw)
                    bias = jnp.concatenate([same, same], 0)
                score = raw * (SCALE * LOG2E) + bias
                powers.append(jnp.exp2(score - jnp.max(score, -1, keepdims=True)))
            wide = [a if w == 0 else both_levels(a) for a in powers]
            mixed_all = dot(jnp.concatenate([a.astype(BF16) for a in wide], 0), v_cat[w, g])
            inverse, context = [], jnp.zeros((WT, 128), F32)
            for hh in range(4):
                inverse.append(1.0 / mixed_all[part[hh], 128:])
                context = jnp.where(half_lane // 32 == hh, mixed_all[part[hh], :128] * inverse[hh], context)
            ctx_acc[rows, lanes] = context.astype(BF16)
            shares = jnp.concatenate(split(dctx_now.astype(F32) * context, 2), 1)
            deltas = dot(shares, blocks_of_ones)
            score_lows = []
            for hh in range(4):
                head = g * 4 + hh
                d_raw, delta = d_raw_all[part[hh]], deltas[:, 128 * hh : 128 * hh + 128]
                if w == 0:
                    double = lambda a: jnp.concatenate([a, a], 1)
                    probs = powers[hh] * double(inverse[hh])
                    d_score = probs * (d_raw - double(delta))
                    blocks = (d_score[:72, :128] + d_score[72:, 128:], d_score[:72, 128:], d_score[72:, :128])
                    probs_low, score_low = probs.astype(BF16), d_score.astype(BF16)
                else:
                    probs = powers[hh] * inverse[hh]
                    d_score = probs * (own_level(d_raw) - delta)
                    blocks = (d_score[:72] + d_score[72:],)
                    probs_low, score_low = both_levels(probs).astype(BF16), both_levels(d_score).astype(BF16)
                score_lows.append(score_low)
                head_rows = slice(head * 32, head * 32 + 32)
                dkv_t[w, 0, head_rows, :] = dot(turned[w, 0, head_rows, :], score_low) * SCALE
                dkv_t[w, 1, head_rows, :] = dot(turned[w, 1, head_rows, :], probs_low)
                for b, block in enumerate(blocks):
                    turned_back = jnp.take_along_axis(block, back, axis=1)
                    early = jnp.where(first, turned_back, 0.0)
                    late = turned_back - early
                    d_tables[w, head, :, b * 256 : b * 256 + 128] = jnp.sum(early.reshape(9, 8, 128), 0)
                    d_tables[w, head, :, b * 256 + 128 : b * 256 + 256] = jnp.sum(late.reshape(9, 8, 128), 0)
            both_all = dot(jnp.concatenate(score_lows, 0), k_cat[w, g])
            dq, feats = jnp.zeros((WT, 128), F32), f_acc[w]
            for hh in range(4):
                dq = jnp.where(half_lane // 32 == hh, both_all[part[hh], :128], dq)
                feats = jnp.where(lax.rem(half_lane, 12) == g * 4 + hh, both_all[part[hh], 128:], feats)
            dq_acc[rows, lanes] = dq * SCALE
            f_acc[w] = feats

    sums = {}

    def weight_grads(g):
        lanes = slice(128 * g, 128 * g + 128)
        dq = dq_acc[:, lanes]
        low[:, lanes] = dq.astype(BF16)
        sums[0, g] = jnp.sum(dq, 0, keepdims=True)
        for part in range(2):
            total = jnp.zeros((1, 128), F32)
            for w in range(2):
                rows_now = dot(c_back[...], dkv_t[w, part, lanes, :].astype(BF16), NT)
                total += jnp.sum(rows_now, 0, keepdims=True)
                at = WIDTH * (part + 1) + 128 * g
                low[w * WT : (w + 1) * WT, at : at + 128] = rows_now.astype(BF16)
            sums[part + 1, g] = total
        for part in range(3):
            at = WIDTH * part + 128 * g
            grad = dot(normed_t[...], low[:, at : at + 128])
            for i in range(8):
                n = 3 * i + part
                wp[g, n // PLANE, n % PLANE] = grad[48 * i : 48 * i + 48, :].astype(BF16)
        grad = dot(ctx_acc[:, lanes], dy_low[...], TN)
        for u in range(8):
            n = 24 + u
            for m in range(3):
                wp[g, n // PLANE, n % PLANE, 16 * m : 16 * m + 16, :] = grad[
                    16 * u : 16 * u + 16, 128 * m : 128 * m + 128
                ].astype(BF16)
        return send(wp.at[g, 1 - core], c_recv.at[g], c_sems, g, place.sibling)

    def plane_sends(g, core_copy):
        core_copy.wait()
        copies = []
        for step in range(1, PLANE):
            x_at, y_at, at = place.in_plane(step, 1)
            p_send[g, step] = (wp[g, core, at].astype(F32) + c_recv[g, at].astype(F32)).astype(BF16)
            copies.append(
                send(
                    p_send.at[g, step], p_recv.at[g, step], p_sems, g * PLANE + step, place.device(x_at, y_at, z, core)
                )
            )
        return copies

    d_tables[...] = jnp.zeros_like(d_tables)
    f_acc[...] = jnp.zeros_like(f_acc)
    group_step(0)
    core_copies = [weight_grads(0)]
    group_step(1)
    plane_copies = [plane_sends(0, core_copies[0])]
    core_copies.append(weight_grads(1))
    group_step(2)
    plane_copies.append(plane_sends(1, core_copies[1]))
    core_copies.append(weight_grads(2))

    d_normed = dot(low[...], w_qkv[...], NT).astype(BF16).astype(F32)
    scaled = d_normed * gain_row
    first_mean = jnp.mean(scaled, -1, keepdims=True)
    second_mean = jnp.mean(scaled * white[...], -1, keepdims=True)
    dq_acc[...] = dy_low[...].astype(F32) + inv_std[...] * (scaled - first_mean - white[...] * second_mean)
    plane_copies.append(plane_sends(2, core_copies[2]))
    for j in range(3):
        cols = slice(128 * j, 128 * j + 128)
        for k in range(4):
            level = (1, 2, 3, 0)[k]
            strided[pl.ds(576 * j + level, 72, stride=8), :] = dq_acc[72 * k : 72 * k + 72, cols]
        gx[:, :, :, cols] = mixed[j, :, 0:4, :].astype(BF16).reshape(6, 12, 4, 128)
    home = [
        send(quadrant(gx, q), quadrant(gx_out, 3 - q), h_sems, q - 1, to)
        for q, to in ((1, place.east), (2, place.north), (3, place.north_east))
    ]
    own_gx = pltpu.make_async_copy(quadrant(gx, 0), quadrant(gx_out, 3), local.at[3])
    own_gx.start()

    for w in range(2):
        table = functools.reduce(jnp.add, [dot(part, onehot[...], NT) for part in split(jnp.sum(d_tables[w], 1), 2)])
        for half in range(2):
            for k in range(3):
                at = 128 * (3 * half + k)
                tp[w, half, 16 * k : 16 * k + 16, :] = table[:, at : at + 128]
    small = [sums[part, g] for part in range(3) for g in range(3)]
    for total in (
        jnp.sum(dy_low[...].astype(F32), 0, keepdims=True),
        jnp.sum(d_normed * white[...], 0, keepdims=True),
        jnp.sum(d_normed, 0, keepdims=True),
    ):
        small += [total[:, 128 * m : 128 * m + 128] for m in range(3)]
    d_surf = functools.reduce(jnp.add, [dot(of_query, part, TN) for part in split(f_acc[0] + f_acc[1], 2)])
    small += [d_surf[a : a + 1, :] for a in range(4)]
    for e, row in enumerate(small):
        w, half, at = small_row(e)
        tp[w, half, at : at + 1, :] = row
    tp_low[...] = tp[...].astype(BF16)
    t_copy = send(tp_low.at[1 - core], tc_recv, t_sems, 0, place.sibling)

    t_mine = lax.rem(x, 2)
    total = [wp[g, core, here].astype(F32) + c_recv[g, here].astype(F32) for g in range(3)]
    t_copy.wait()
    t_send[...] = (tp[core, 1 - t_mine] + tc_recv[1 - t_mine].astype(F32)).astype(BF16)
    tx_copy = send(t_send, t_recv, t_sems, 1, place.x_pair)
    t_total = tp[core, t_mine] + tc_recv[t_mine].astype(F32)
    for g in range(3):
        for step in range(1, PLANE):
            plane_copies[g][step - 1].wait()
            total[g] = total[g] + p_recv[g, step].astype(F32)
        z_own[48 * g : 48 * g + 48, :] = total[g]
    tx_copy.wait()
    z_own[144:192, :] = t_total + t_recv[...].astype(F32)

    for k in range(PZ):
        z_send[k] = z_own[24 * k : 24 * k + 24, :].astype(BF16)
    z_copies = []
    for step in (4, 3, 5, 2, 6, 1, 7):
        z_at = lax.rem(z + step, PZ)
        z_copies.append(send(z_send.at[z_at], z_recv.at[step], z_sems, step, place.device(x, y, z_at, core)))
    summed = z_own[pl.ds(pl.multiple_of(24 * z, 8), 24), :]
    for copy in z_copies:
        copy.wait()
    for step in range(1, PZ):
        summed = summed + z_recv[step].astype(F32)
    z_full[z] = summed.astype(BF16)
    a_copies = []
    for step in (4, 3, 5, 2, 6, 1, 7):
        z_at = lax.rem(z + step, PZ)
        a_copies.append(send(z_full.at[z], z_full.at[z], a_sems, step, place.device(x, y, z_at, core)))
    for copy in a_copies:
        copy.wait()
    full_b[core, y, x] = jnp.concatenate([z_full[k].astype(F32) for k in range(4)], 0).astype(BF16)
    full_c[core, x, y] = jnp.concatenate([z_full[k].astype(F32) for k in range(4, 8)], 0).astype(BF16)

    def x_away(step):
        return place.device(lax.rem(x + step, PX), y, z, core)

    def y_away(step):
        return place.device(x, lax.rem(y + step, PY), z, core)

    b_first, c_first, b_then, c_then, last = {}, {}, {}, {}, []
    for d in (2, 1, 3):
        b_first[d] = send(full_b.at[core, y, x], full_b.at[core, y, x], bx_sems, d, x_away(d))
        c_first[d] = send(full_c.at[core, x, y], full_c.at[core, x, y], cy_sems, d, y_away(d))
    for d in (2, 1, 3):
        b_then[0, d] = send(full_b.at[core, y, x], full_b.at[core, y, x], by_sems, d, y_away(d))
        c_then[0, d] = send(full_c.at[core, x, y], full_c.at[core, x, y], cx_sems, d, x_away(d))
    for e in (1, 3, 2):
        x_from, y_from = lax.rem(x + PX - e, PX), lax.rem(y + PY - e, PY)
        b_first[e].wait()
        for d in (2, 1, 3):
            b_then[e, d] = send(full_b.at[core, y, x_from], full_b.at[core, y, x_from], by_sems, 4 * e + d, y_away(d))
        c_first[e].wait()
        for d in (2, 1, 3):
            c_then[e, d] = send(full_c.at[core, x, y_from], full_c.at[core, x, y_from], cx_sems, 4 * e + d, x_away(d))
    last.append(send(full_b.at[core, y], full_b.at[core, y], k_sems, 0, place.sibling))
    last.append(send(full_c.at[core, x], full_c.at[core, x], k_sems, 4, place.sibling))
    for d in (1, 3, 2):
        x_from, y_from = lax.rem(x + PX - d, PX), lax.rem(y + PY - d, PY)
        for e in range(4):
            b_then[e, d].wait()
        last.append(send(full_b.at[core, y_from], full_b.at[core, y_from], k_sems, d, place.sibling))
        for e in range(4):
            c_then[e, d].wait()
        last.append(send(full_c.at[core, x_from], full_c.at[core, x_from], k_sems, 4 + d, place.sibling))
    for copy in last + home:
        copy.wait()
    own_gx.wait()


def step(*operands):
    sems = pltpu.SemaphoreType.DMA
    anywhere = pl.BlockSpec(memory_space=pl.ANY)
    in_specs = [VMEM] * len(operands)
    for k in (0, 1, 6, 8, 9):
        in_specs[k] = anywhere
    return pl.pallas_call(
        step_kernel,
        out_shape=(
            jax.ShapeDtypeStruct((2, PY, PX, 96, 128), BF16),
            jax.ShapeDtypeStruct((2, PX, PY, 96, 128), BF16),
            jax.ShapeDtypeStruct((6, 12, 4, WIDTH), BF16),
        ),
        in_specs=in_specs,
        out_specs=(VMEM, VMEM, VMEM),
        scratch_shapes=[
            pltpu.VMEM((WIDTH, 3 * WIDTH), BF16),
            pltpu.VMEM((WIDTH, WIDTH), BF16),
            pltpu.VMEM((HEADS * 16, SLOTS), F32),
            pltpu.VMEM((6, 12, 4, WIDTH), BF16),
            pltpu.VMEM((6, 12, 4, WIDTH), BF16),
            pltpu.VMEM((4, 8, 128), F32),
            pltpu.VMEM((4, 8, 128), F32),
            pltpu.VMEM((128, 128), F32),
            pltpu.VMEM((2, 2, 48, 128), F32),
            pltpu.VMEM((2, 2, 48, 128), BF16),
            pltpu.VMEM((6, 12, 4, WIDTH), BF16),
            pltpu.VMEM((3, 72, 8, 128), F32),
            pltpu.VMEM((288, WIDTH), F32),
            pltpu.VMEM((288, 1), F32),
            pltpu.VMEM((288, WIDTH), BF16),
            pltpu.VMEM((WIDTH, 288), BF16),
            pltpu.VMEM((288, WIDTH), BF16),
            pltpu.VMEM((288, 3 * WIDTH), BF16),
            pltpu.VMEM((288, WIDTH), BF16),
            pltpu.VMEM((2, 2, WIDTH, WT), BF16),
            pltpu.VMEM((2, 3, KEYS, 256), BF16),
            pltpu.VMEM((2, 3, 256, KEYS), BF16),
            pltpu.VMEM((2, 3, KEYS, 256), BF16),
            pltpu.VMEM((2, WIDTH, KEYS), BF16),
            pltpu.VMEM((WT, 128), BF16),
            pltpu.VMEM((768, 768), BF16),
            pltpu.VMEM((2, 16, 768), F32),
            pltpu.VMEM((2, 16, 8, 768), F32),
            pltpu.VMEM((288, WIDTH), BF16),
            pltpu.VMEM((288, WIDTH), F32),
            pltpu.VMEM((2, WT, 128), F32),
            pltpu.VMEM((2, 2, WIDTH, KEYS), F32),
            pltpu.VMEM((288, 3 * WIDTH), BF16),
            pltpu.VMEM((2, 16, 768), F32),
            pltpu.VMEM((3, 2, PLANE, 48, 128), BF16),
            pltpu.VMEM((3, PLANE, 48, 128), BF16),
            pltpu.VMEM((3, PLANE, 48, 128), BF16),
            pltpu.VMEM((3, PLANE, 48, 128), BF16),
            pltpu.VMEM((2, 48, 128), BF16),
            pltpu.VMEM((48, 128), BF16),
            pltpu.VMEM((48, 128), BF16),
            pltpu.VMEM((192, 128), F32),
            pltpu.VMEM((PZ, 24, 128), BF16),
            pltpu.VMEM((PZ, 24, 128), BF16),
            pltpu.VMEM((PZ, 24, 128), BF16),
            sems((2, 9)),
            sems((2, 3)),
            sems((2, 3)),
            sems((2, 2)),
            sems((2, 3 * PLANE)),
            sems((2, PZ)),
            sems((2, PZ)),
            sems((2, 4)),
            sems((2, 16)),
            sems((2, 16)),
            sems((2, 4)),
            sems((2, 8)),
            sems((7,)),
        ],
        compiler_params=pltpu.CompilerParams(
            collective_id=0, has_side_effects=True, vmem_limit_bytes=60 * 1024 * 1024
        ),
        name="step",
    )(*operands)


def small_row(e):
    quarter, k = e // 6, e % 6
    return quarter // 2, quarter % 2, 16 * (k // 4) + 12 + k % 4


def finish_kernel(
    grad_scale, full_b, full_c, gx, o_gx, o_wqkv, o_bqkv, o_wproj, o_bproj, o_gain, o_shift, o_pos, o_surf
):
    o_gx[...] = gx[...]

    def chunk(core, at):
        x, y = at % PX, at // PX
        return full_b.at[core, y, x], full_c.at[core, x, y]

    for n in range(2 * PLANE):
        b, c = chunk(n // PLANE, n % PLANE)
        for g in range(3):
            source = (b, b, c)[g]
            rows = (0, 48, 0)[g]
            part = source[rows : rows + 48, :].astype(F32) * grad_scale
            if n < 24:
                i, at = n // 3, WIDTH * (n % 3) + 128 * g
                o_wqkv[48 * i : 48 * i + 48, at : at + 128] = part
            else:
                at = 128 * g + 16 * (n - 24)
                for m in range(3):
                    o_wproj[at : at + 16, 128 * m : 128 * m + 128] = part[16 * m : 16 * m + 16, :]

    quarters = {}
    for core in range(2):
        for at in range(PLANE):
            x, y = at % PX, at // PX
            kind = (y * 2 + x // 2) * 2 + core
            rows = chunk(core, at)[1][48:96, :].astype(F32) * grad_scale
            key = core, x % 2
            quarters[key] = rows if key not in quarters else quarters[key] + rows
            for k in range(3):
                lo = 128 * (3 * (x % 2) + k)
                width = min(128, SLOTS - lo)
                for h in range(HEADS):
                    o_pos[16 * h + kind : 16 * h + kind + 1, lo : lo + width] = rows[
                        16 * k + h : 16 * k + h + 1, :width
                    ]

    def small(e):
        w, half, at = small_row(e)
        return quarters[w, half][at : at + 1, :]

    o_bqkv[...] = jnp.concatenate([small(n) for n in range(9)], 1).reshape(3 * WIDTH)
    for v, out in enumerate((o_bproj, o_gain, o_shift)):
        out[...] = jnp.concatenate([small(9 + 3 * v + m) for m in range(3)], 1).reshape(WIDTH)
    for a in range(4):
        side = small(18 + a)
        for b in range(4):
            o_surf[a, b : b + 1, :] = side[:, 12 * b : 12 * b + 12]


def finish(full_b, full_c, gx, grad_scale):
    one = lambda *shape: jax.ShapeDtypeStruct(shape, F32)
    return pl.pallas_call(
        functools.partial(finish_kernel, grad_scale),
        out_shape=(
            jax.ShapeDtypeStruct((6, 12, 4, WIDTH), BF16),
            one(WIDTH, 3 * WIDTH),
            one(3 * WIDTH),
            one(WIDTH, WIDTH),
            one(WIDTH),
            one(WIDTH),
            one(WIDTH),
            one(HEADS * 16, SLOTS),
            one(4, 4, HEADS),
        ),
        in_specs=[VMEM] * 3,
        out_specs=(VMEM,) * 9,
        compiler_params=pltpu.CompilerParams(vmem_limit_bytes=60 * 1024 * 1024),
        name="finish",
    )(full_b, full_c, gx)


def on_device(
    inputs, cotangent, land_sea, rel_index, norm_gain, norm_shift, w_qkv, b_qkv, w_proj, pos_bias, surf_bias
):
    levels, lat_rows, lon_cols, width = inputs.shape
    count = levels * lat_rows * lon_cols * lax.axis_size("lat") * lax.axis_size("lon")
    full_b, full_c, gx = step(
        inputs.transpose(1, 2, 0, 3),
        cotangent.transpose(1, 2, 0, 3),
        land_sea,
        rel_index,
        norm_gain,
        norm_shift,
        w_qkv,
        b_qkv,
        w_proj,
        pos_bias.transpose(1, 0, 2).reshape(-1, SLOTS),
        surf_bias.transpose(1, 2, 0),
        *(jnp.asarray(a) for a in constants()),
    )
    outs = finish(full_b, full_c, gx, float(count) ** -0.5)
    g_x, g_wqkv, g_bqkv, g_wproj, g_bproj, g_gain, g_shift, g_pos, g_surf = outs
    return (
        g_x.transpose(2, 0, 1, 3),
        g_wqkv,
        g_bqkv,
        g_wproj,
        g_bproj,
        g_gain,
        g_shift,
        g_pos.reshape(HEADS, 16, SLOTS).transpose(1, 0, 2),
        g_surf.transpose(2, 0, 1),
    )


def solution(mesh):
    in_specs = (P(None, "lat", "lon", None), P(None, "lat", "lon", None), P("lat", "lon")) + (P(),) * 8
    out_specs = (P(None, "lat", "lon", None),) + (P(),) * 8
    return jax.shard_map(on_device, mesh=mesh, in_specs=in_specs, out_specs=out_specs, check_vma=False)
```

```python
import functools

import jax
import jax.numpy as jnp
from jax import lax
from jax.experimental import pallas as pl
from jax.experimental.pallas import tpu as pltpu
from jax.sharding import PartitionSpec as P

F32 = jnp.float32
BF16 = jnp.bfloat16
MESH = pl.DeviceIdType.MESH
EPS = 1e-05
LOG2E = 1.4426950408889634
BIG = 2.0**33
HEADS = 12
SLOTS = 759
WIDTH = 384
WT = 144
PITCH = 23
KEYS = 256
SCALE = 32.0**-0.5
NT = (((1,), (1,)), ((), ()))
TN = (((0,), (0,)), ((), ()))
NN = (((1,), (0,)), ((), ()))
PX, PY, PZ = 4, 4, 8
PLANE = PX * PY
VMEM = pl.BlockSpec(memory_space=pltpu.VMEM)


def dot(a, b, dims=NN):
    return lax.dot_general(a, b, dims, preferred_element_type=F32)


class Place:
    def __init__(self):
        lat, lon = lax.axis_index("lat"), lax.axis_index("lon")
        n_lat, n_lon = lax.axis_size("lat"), lax.axis_size("lon")
        self.lat, self.n_lat = lat, n_lat
        self.core = lax.rem(lon, 2)
        self.z = lax.rem(lon // 2, PZ)
        self.x = lax.rem(lat, 2) * 2 + lon // (2 * PZ)
        self.y = lat // 2
        self.here = self.y * PX + self.x
        up, down = lax.rem(lat + 1, n_lat), lax.rem(lat + n_lat - 1, n_lat)
        right, left = lax.rem(lon + 1, n_lon), lax.rem(lon + n_lon - 1, n_lon)
        self.north, self.south = (up, lon), (down, lon)
        self.east, self.west = (lat, right), (lat, left)
        self.north_east, self.south_west = (up, right), (down, left)
        self.sibling = (lat, lon + 1 - 2 * self.core)
        self.x_pair = self.device(self.x + 1 - 2 * lax.rem(self.x, 2), self.y, self.z, self.core)

    def device(self, x, y, z, core):
        return (y * 2 + x // 2, (lax.rem(x, 2) * PZ + z) * 2 + core)

    def in_plane(self, step, sign):
        x = lax.rem(self.x + PX + sign * (step % PX), PX)
        y = lax.rem(self.y + PY + sign * (step // PX), PY)
        return x, y, y * PX + x

    def greet(self):
        others = [self.north, self.south, self.east, self.west, self.north_east, self.south_west, self.sibling]
        for step in range(1, PLANE):
            x, y, _ = self.in_plane(step, -1)
            others.append(self.device(x, y, self.z, self.core))
        for step in range(1, PZ):
            others.append(self.device(self.x, self.y, lax.rem(self.z + PZ - step, PZ), self.core))
        for other in others:
            pl.semaphore_signal(pltpu.get_barrier_semaphore(), inc=1, device_id=other, device_id_type=MESH)
        self.greeted = len(others)

    def meet(self):
        pl.semaphore_wait(pltpu.get_barrier_semaphore(), self.greeted)


def send(src, dst, sems, k, to):
    copy = pltpu.make_async_remote_copy(
        src_ref=src,
        dst_ref=dst,
        send_sem=sems.at[0, k],
        recv_sem=sems.at[1, k],
        device_id=to,
        device_id_type=MESH,
    )
    copy.start()
    return copy


def key_of(token):
    level, cell = token // 72, lax.rem(token, 72)
    return 128 * level + cell + (PITCH - 12) * (cell // 12)


def plain_rows():
    rows = lax.broadcasted_iota(jnp.int32, (72, 128), 0)
    return rows + (PITCH - 12) * (rows // 12)


def skew_parts(rows):
    lane = lax.broadcasted_iota(jnp.int32, (72, 128), 1)
    first = lane + rows >= PITCH * 5 + 11
    there = jnp.bitwise_and(lane - rows - 2, 127)
    back = jnp.bitwise_and(lane + rows + 2, 127)
    return first, there, back


def skew(table, first, there):
    mixed = jnp.where(first, table[:, :128], table[:, 128:])
    return jnp.take_along_axis(mixed, there, axis=1)


def split(values, count):
    pieces = []
    for _ in range(count):
        piece = values.astype(BF16)
        pieces.append(piece)
        values = values - piece.astype(F32)
    return pieces


def step_kernel(
    x_in, dy_in, land_in, rel_in, gain_in, shift_in, w_qkv_in, b_qkv_in, w_proj_in, pos_in, surf_in,
    full_b, full_c, gx_out,
    land, rel, gain, shift, w_qkv, b_qkv, w_proj, pos, surf, c_spread, c_back, w_qkv_t, w_proj_t, onehot_t,
    tok_x, tok_dy, cls_out, cls_in, side_in, tp, tp_low, gx,
    mixed, white, inv_std, normed, normed_t, dy_low, qkv, dctx, turned, k_cat, k_cat_t, v_cat, v_turned, q_feat,
    onehot, tables, d_tables, ctx_acc, dq_acc, f_acc, dkv_t, low, table_in,
    wp, c_recv, p_send, p_recv, tc_recv, t_send, t_recv, z_own, z_send, z_recv, z_full,
    f_sems, h_sems, c_sems, t_sems, p_sems, z_sems, a_sems, bx_sems, by_sems, cx_sems, cy_sems, k_sems, local,
):
    place = Place()
    core, x, y, z, here = place.core, place.x, place.y, place.z, place.here
    place.greet()
    fetches = [
        pltpu.make_async_copy(a, b, local.at[4 + k])
        for k, (a, b) in enumerate(
            (
                (land_in, land), (pos_in, pos), (rel_in, rel), (w_qkv_in, w_qkv), (w_proj_in, w_proj),
                (gain_in, gain), (shift_in, shift), (b_qkv_in, b_qkv), (surf_in, surf),
            )
        )
    ]
    for copy in fetches:
        copy.start()

    cls_out[...] = jnp.zeros_like(cls_out)
    fetches[0].wait()
    for q in range(4):
        cls_out[q, :3, :6] = land[3 * (q // 2) : 3 * (q // 2) + 3, 6 * (q % 2) : 6 * (q % 2) + 6].astype(F32)

    def quadrant(ref, q):
        return ref.at[pl.ds(3 * (q // 2), 3), pl.ds(6 * (q % 2), 6)]

    place.meet()
    routes = ((0, place.south_west), (1, place.south), (2, place.west))
    halo_x = [send(quadrant(x_in, q), quadrant(tok_x, 3 - q), f_sems, q, to) for q, to in routes]
    halo_x += [send(cls_out.at[q], cls_in.at[3 - q], f_sems, 3 + q, to) for q, to in routes]
    halo_dy = [send(quadrant(dy_in, q), quadrant(tok_dy, 3 - q), f_sems, 6 + q, to) for q, to in routes]
    own_x = pltpu.make_async_copy(quadrant(x_in, 3), quadrant(tok_x, 0), local.at[0])
    own_dy = pltpu.make_async_copy(quadrant(dy_in, 3), quadrant(tok_dy, 0), local.at[1])
    own_cls = pltpu.make_async_copy(cls_out.at[3], cls_in.at[0], local.at[2])
    for copy in (own_x, own_dy, own_cls):
        copy.start()

    lat = place.lat
    last_band = lat == place.n_lat - 1
    for copy in fetches[1:]:
        copy.wait()
    key_at = lax.broadcasted_iota(jnp.int32, (KEYS, WT), 0)
    c_spread[...] = jnp.where(key_at == key_of(lax.broadcasted_iota(jnp.int32, (KEYS, WT), 1)), 1.0, 0.0).astype(BF16)
    key_at = lax.broadcasted_iota(jnp.int32, (WT, KEYS), 1)
    c_back[...] = jnp.where(key_at == key_of(lax.broadcasted_iota(jnp.int32, (WT, KEYS), 0)), 1.0, 0.0).astype(BF16)
    rel_now = rel[...]
    rel_low = jnp.bitwise_and(rel_now, 15)
    rel_wide = dot((rel_now - rel_low).astype(F32).astype(BF16), c_spread[...], NT) + dot(
        rel_low.astype(F32).astype(BF16), c_spread[...], NT
    )
    rel_lane = jnp.bitwise_and(lax.broadcasted_iota(jnp.int32, (WT, KEYS), 1), 127)
    rel_wide = jnp.where(lax.rem(rel_lane, PITCH) < 12, rel_wide, -1.0)
    first, _, back = skew_parts(plain_rows())
    slot = lax.broadcasted_iota(jnp.int32, (768, 128), 0).astype(F32)
    for b, block in enumerate((rel_wide[:72, :128], rel_wide[:72, 128:], rel_wide[72:, :128])):
        turned_back = jnp.take_along_axis(block, back, axis=1)
        for half in range(2):
            kept = jnp.where(first, turned_back, -1.0) if half == 0 else jnp.where(first, -1.0, turned_back)
            slots = jnp.max(kept, 0, keepdims=True)
            lanes = slice(b * 256 + half * 128, b * 256 + half * 128 + 128)
            onehot[:, lanes] = jnp.where(slot == slots, 1.0, 0.0).astype(BF16)
    table_in[...] = jnp.zeros_like(table_in)
    for w in range(2):
        for h in range(HEADS):
            table_in[w, h : h + 1, :SLOTS] = pos[pl.ds(16 * h + 2 * lat + w, 1), :] * LOG2E
        tables[w] = functools.reduce(jnp.add, [dot(part, onehot[...]) for part in split(table_in[w], 3)])

    onehot_t[...] = onehot[...].T
    w_qkv_t[...] = w_qkv[...].T
    w_proj_t[...] = w_proj[...].T

    eye = (
        lax.broadcasted_iota(jnp.int32, (WIDTH, WIDTH), 0) == lax.broadcasted_iota(jnp.int32, (WIDTH, WIDTH), 1)
    ).astype(F32).astype(BF16)
    strided = mixed.reshape(3 * 576, 128)

    def in_order(tok, first_row, out):
        for j in range(3):
            cols = slice(128 * j, 128 * j + 128)
            mixed[j, :, first_row : first_row + 4, :] = tok[:, :, :, cols].reshape(72, 4, 128).astype(F32)
        for k in range(4):
            level = (1, 2, 3, 0)[k]
            for j in range(3):
                out[72 * k : 72 * k + 72, 128 * j : 128 * j + 128] = strided[
                    pl.ds(576 * j + first_row + level, 72, stride=8), :
                ]

    for copy in halo_x + [own_x, own_cls]:
        copy.wait()
    in_order(tok_x, 0, white)
    tokens = white[...]
    centred = tokens - jnp.mean(tokens, -1, keepdims=True)
    inv = lax.rsqrt(jnp.mean(centred * centred, -1, keepdims=True) + EPS)
    inv_std[...] = inv
    whitened = centred * inv
    white[...] = whitened
    gain_row = gain[...].reshape(1, WIDTH)
    normed[...] = (whitened * gain_row + shift[...].reshape(1, WIDTH)).astype(BF16)
    qkv[...] = (dot(normed[...], w_qkv[...]) + b_qkv[...].reshape(1, 3 * WIDTH)).astype(BF16)
    normed_t[...] = dot(eye, normed[...], NT).astype(BF16)
    for w in range(2):
        rows = slice(w * WT, (w + 1) * WT)
        turned[w, 0] = dot(eye, qkv[rows, :WIDTH], NT).astype(BF16)
        padded = dot(c_spread[...], qkv[rows, WIDTH:]).astype(BF16)
        k_turned = dot(eye, padded[:, :WIDTH], NT).astype(BF16)
        v_turned[w] = dot(eye, padded[:, WIDTH:], NT).astype(BF16)
        for g in range(3):
            lanes = slice(128 * g, 128 * g + 128)
            k_cat[w, g, :, :128] = padded[:, lanes]
            k_cat_t[w, g, :128, :] = k_turned[lanes, :]
            v_cat[w, g, :, :128] = padded[:, WIDTH + 128 * g : WIDTH + 128 * g + 128]
            v_cat[w, g, :, 128:] = jnp.ones((KEYS, 128), BF16)

    lane = lax.broadcasted_iota(jnp.int32, (WT, 128), 1)
    token = lax.broadcasted_iota(jnp.int32, (WT, 128), 0)
    cell = lax.rem(token, 72)
    cell_row, cell_col = cell // 12, lax.rem(cell, 12)
    in_quad = 8 * (2 * (cell_row // 3) + cell_col // 6) + lax.rem(cell_row, 3)
    pick_row = jnp.where(lane == in_quad, 1.0, 0.0).astype(BF16)[:, :32]
    pick_col = jnp.where(lane == lax.rem(cell_col, 6), 1.0, 0.0)
    cells = dot(pick_row, cls_in[...].reshape(32, 128).astype(BF16)) * pick_col
    kind = dot(cells.astype(BF16), jnp.ones((128, 128), BF16)).astype(jnp.int32)
    turned_over = jnp.logical_and(lax.rem(token, 72) >= 36, last_band).astype(F32)
    of_key = jnp.where(kind == lax.rem(lane, 48) // 12, 1.0, 0.0)
    of_query = jnp.where(kind == lane, 1.0, 0.0).astype(BF16)
    side_in[...] = jnp.zeros_like(side_in)
    for a in range(4):
        for b in range(4):
            side_in[a : a + 1, 12 * b : 12 * b + 12] = surf[a, b : b + 1, :]
            side_in[a : a + 1, 48 + 12 * b : 60 + 12 * b] = surf[a, b : b + 1, :]
    surf_lane = lax.broadcasted_iota(jnp.int32, (128, 128), 1)
    surf_hi, surf_lo = split(side_in[...] * (1.0 / SCALE), 2)
    side = dot(of_query, jnp.where(surf_lane < 48, surf_hi.astype(F32), surf_lo.astype(F32)).astype(BF16))
    q_feat[...] = jnp.where(
        lane < 96, side, jnp.where(lane == 96, turned_over, jnp.where(lane == 97, 1.0 - turned_over, 0.0))
    ).astype(BF16)
    key_side = jnp.where(
        lane < 96,
        of_key,
        jnp.where(lane == 96, -BIG * (1.0 - turned_over), jnp.where(lane == 97, -BIG * turned_over, 0.0)),
    ).astype(BF16)
    key_lane = lax.broadcasted_iota(jnp.int32, (KEYS, 128), 1)
    key_row = jnp.bitwise_and(lax.broadcasted_iota(jnp.int32, (KEYS, 128), 0), 127)
    hidden = jnp.logical_and(lax.rem(key_row, PITCH) >= 12, jnp.logical_and(key_lane >= 96, key_lane < 98))
    k_feat = jnp.where(hidden, -BIG, dot(c_spread[...], key_side)).astype(BF16)
    k_feat_t = dot(eye[:128, :128], k_feat, NT).astype(BF16)
    for w in range(2):
        for g in range(3):
            k_cat[w, g, :, 128:] = k_feat
            k_cat_t[w, g, 128:, :] = k_feat_t

    for copy in halo_dy + [own_dy]:
        copy.wait()
    in_order(tok_dy, 4, dq_acc)
    dy_low[...] = dq_acc[...].astype(BF16)
    dctx[...] = dot(dy_low[...], w_proj_t[...]).astype(BF16)
    for w in range(2):
        turned[w, 1] = dot(eye, dctx[w * WT : (w + 1) * WT, :], NT).astype(BF16)

    zero = jnp.zeros((72, 128), F32)
    cat_lane = lax.broadcasted_iota(jnp.int32, (1, 256), 1)
    half_lane = lax.broadcasted_iota(jnp.int32, (1, 128), 1)
    block_row = jnp.bitwise_and(lax.broadcasted_iota(jnp.int32, (256, 512), 0), 127)
    block_lane = lax.broadcasted_iota(jnp.int32, (256, 512), 1)
    blocks_of_ones = jnp.where(block_row // 32 == block_lane // 128, 1.0, 0.0).astype(BF16)
    first, there, back = skew_parts(plain_rows())

    def own_level(a):
        return jnp.concatenate([a[:72, :128], a[72:, 128:]], 0)

    def both_levels(a):
        top = jnp.concatenate([a[:72], zero], 1)
        return jnp.concatenate([top, jnp.concatenate([zero, a[72:]], 1)], 0)

    def group_step(g):
        lanes = slice(g * 128, g * 128 + 128)
        for w in range(2):
            rows = slice(w * WT, (w + 1) * WT)
            part = [slice(WT * hh, WT * hh + WT) for hh in range(4)]
            q_cat = jnp.concatenate([qkv[rows, lanes], q_feat[...]], 1)
            dctx_now = dctx[rows, lanes]
            q_all, dctx_all = [], []
            for hh in range(4):
                mine = cat_lane // 32 == hh
                feat_mine = jnp.logical_and(
                    cat_lane >= 128, jnp.logical_or(cat_lane >= 224, lax.rem(cat_lane + 4, 12) == g * 4 + hh)
                )
                keep = jnp.logical_or(mine, feat_mine).astype(F32).astype(BF16)
                q_all.append(q_cat * keep)
                dctx_all.append(dctx_now * keep[:, :128])
            raw_all = dot(jnp.concatenate(q_all, 0), k_cat_t[w, g])
            d_raw_all = dot(jnp.concatenate(dctx_all, 0), v_turned[w, lanes, :])
            powers = []
            for hh in range(4):
                head = g * 4 + hh
                raw = raw_all[part[hh]]
                table = tables[w, head : head + 1, :]
                same = skew(table[:, :256], first, there)
                if w == 0:
                    upper = jnp.concatenate([same, skew(table[:, 256:512], first, there)], 1)
                    lower = jnp.concatenate([skew(table[:, 512:], first, there), same], 1)
                    bias = jnp.concatenate([upper, lower], 0)
                else:
                    raw = own_level(raw)
                    bias = jnp.concatenate([same, same], 0)
                score = raw * (SCALE * LOG2E) + bias
                powers.append(jnp.exp2(score - jnp.max(score, -1, keepdims=True)))
            wide = [a if w == 0 else both_levels(a) for a in powers]
            mixed_all = dot(jnp.concatenate([a.astype(BF16) for a in wide], 0), v_cat[w, g])
            inverse, context = [], jnp.zeros((WT, 128), F32)
            for hh in range(4):
                inverse.append(1.0 / mixed_all[part[hh], 128:])
                context = jnp.where(half_lane // 32 == hh, mixed_all[part[hh], :128] * inverse[hh], context)
            ctx_acc[rows, lanes] = context.astype(BF16)
            shares = jnp.concatenate(split(dctx_now.astype(F32) * context, 2), 1)
            deltas = dot(shares, blocks_of_ones)
            score_lows = []
            for hh in range(4):
                head = g * 4 + hh
                d_raw, delta = d_raw_all[part[hh]], deltas[:, 128 * hh : 128 * hh + 128]
                if w == 0:
                    double = lambda a: jnp.concatenate([a, a], 1)
                    probs = powers[hh] * double(inverse[hh])
                    d_score = probs * (d_raw - double(delta))
                    blocks = (d_score[:72, :128] + d_score[72:, 128:], d_score[:72, 128:], d_score[72:, :128])
                    probs_low, score_low = probs.astype(BF16), d_score.astype(BF16)
                else:
                    probs = powers[hh] * inverse[hh]
                    d_score = probs * (own_level(d_raw) - delta)
                    blocks = (d_score[:72] + d_score[72:],)
                    probs_low, score_low = both_levels(probs).astype(BF16), both_levels(d_score).astype(BF16)
                score_lows.append(score_low)
                head_rows = slice(head * 32, head * 32 + 32)
                dkv_t[w, 0, head_rows, :] = dot(turned[w, 0, head_rows, :], score_low) * SCALE
                dkv_t[w, 1, head_rows, :] = dot(turned[w, 1, head_rows, :], probs_low)
                for b, block in enumerate(blocks):
                    turned_back = jnp.take_along_axis(block, back, axis=1)
                    early = jnp.where(first, turned_back, 0.0)
                    late = turned_back - early
                    d_tables[w, head, :, b * 256 : b * 256 + 128] = jnp.sum(early.reshape(9, 8, 128), 0)
                    d_tables[w, head, :, b * 256 + 128 : b * 256 + 256] = jnp.sum(late.reshape(9, 8, 128), 0)
            both_all = dot(jnp.concatenate(score_lows, 0), k_cat[w, g])
            dq, feats = jnp.zeros((WT, 128), F32), f_acc[w]
            for hh in range(4):
                dq = jnp.where(half_lane // 32 == hh, both_all[part[hh], :128], dq)
                feats = jnp.where(lax.rem(half_lane, 12) == g * 4 + hh, both_all[part[hh], 128:], feats)
            dq_acc[rows, lanes] = dq * SCALE
            f_acc[w] = feats

    sums = {}

    def weight_grads(g):
        lanes = slice(128 * g, 128 * g + 128)
        dq = dq_acc[:, lanes]
        low[:, lanes] = dq.astype(BF16)
        sums[0, g] = jnp.sum(dq, 0, keepdims=True)
        for part in range(2):
            total = jnp.zeros((1, 128), F32)
            for w in range(2):
                rows_now = dot(c_back[...], dkv_t[w, part, lanes, :].astype(BF16), NT)
                total += jnp.sum(rows_now, 0, keepdims=True)
                at = WIDTH * (part + 1) + 128 * g
                low[w * WT : (w + 1) * WT, at : at + 128] = rows_now.astype(BF16)
            sums[part + 1, g] = total
        for part in range(3):
            at = WIDTH * part + 128 * g
            grad = dot(normed_t[...], low[:, at : at + 128])
            for i in range(8):
                n = 3 * i + part
                wp[g, n // PLANE, n % PLANE] = grad[48 * i : 48 * i + 48, :].astype(BF16)
        grad = dot(ctx_acc[:, lanes], dy_low[...], TN)
        for u in range(8):
            n = 24 + u
            for m in range(3):
                wp[g, n // PLANE, n % PLANE, 16 * m : 16 * m + 16, :] = grad[
                    16 * u : 16 * u + 16, 128 * m : 128 * m + 128
                ].astype(BF16)
        return send(wp.at[g, 1 - core], c_recv.at[g], c_sems, g, place.sibling)

    def plane_sends(g, core_copy):
        core_copy.wait()
        copies = []
        for step in range(1, PLANE):
            x_at, y_at, at = place.in_plane(step, 1)
            p_send[g, step] = (wp[g, core, at].astype(F32) + c_recv[g, at].astype(F32)).astype(BF16)
            copies.append(
                send(
                    p_send.at[g, step], p_recv.at[g, step], p_sems, g * PLANE + step, place.device(x_at, y_at, z, core)
                )
            )
        return copies

    d_tables[...] = jnp.zeros_like(d_tables)
    f_acc[...] = jnp.zeros_like(f_acc)
    group_step(0)
    core_copies = [weight_grads(0)]
    group_step(1)
    plane_copies = [plane_sends(0, core_copies[0])]
    core_copies.append(weight_grads(1))
    group_step(2)
    plane_copies.append(plane_sends(1, core_copies[1]))
    core_copies.append(weight_grads(2))

    d_normed = dot(low[...], w_qkv_t[...]).astype(BF16).astype(F32)
    scaled = d_normed * gain_row
    first_mean = jnp.mean(scaled, -1, keepdims=True)
    second_mean = jnp.mean(scaled * white[...], -1, keepdims=True)
    dq_acc[...] = dy_low[...].astype(F32) + inv_std[...] * (scaled - first_mean - white[...] * second_mean)
    plane_copies.append(plane_sends(2, core_copies[2]))
    for j in range(3):
        cols = slice(128 * j, 128 * j + 128)
        for k in range(4):
            level = (1, 2, 3, 0)[k]
            strided[pl.ds(576 * j + level, 72, stride=8), :] = dq_acc[72 * k : 72 * k + 72, cols]
        gx[:, :, :, cols] = mixed[j, :, 0:4, :].astype(BF16).reshape(6, 12, 4, 128)
    home = [
        send(quadrant(gx, q), quadrant(gx_out, 3 - q), h_sems, q - 1, to)
        for q, to in ((1, place.east), (2, place.north), (3, place.north_east))
    ]
    own_gx = pltpu.make_async_copy(quadrant(gx, 0), quadrant(gx_out, 3), local.at[3])
    own_gx.start()

    for w in range(2):
        table = functools.reduce(jnp.add, [dot(part, onehot_t[...]) for part in split(jnp.sum(d_tables[w], 1), 2)])
        for half in range(2):
            for k in range(3):
                at = 128 * (3 * half + k)
                tp[w, half, 16 * k : 16 * k + 16, :] = table[:, at : at + 128]
    small = [sums[part, g] for part in range(3) for g in range(3)]
    for total in (
        jnp.sum(dy_low[...].astype(F32), 0, keepdims=True),
        jnp.sum(d_normed * white[...], 0, keepdims=True),
        jnp.sum(d_normed, 0, keepdims=True),
    ):
        small += [total[:, 128 * m : 128 * m + 128] for m in range(3)]
    d_surf = functools.reduce(jnp.add, [dot(of_query, part, TN) for part in split(f_acc[0] + f_acc[1], 2)])
    small += [d_surf[a : a + 1, :] for a in range(4)]
    for e, row in enumerate(small):
        w, half, at = small_row(e)
        tp[w, half, at : at + 1, :] = row
    tp_low[...] = tp[...].astype(BF16)
    t_copy = send(tp_low.at[1 - core], tc_recv, t_sems, 0, place.sibling)

    t_mine = lax.rem(x, 2)
    total = [wp[g, core, here].astype(F32) + c_recv[g, here].astype(F32) for g in range(3)]
    t_copy.wait()
    t_send[...] = (tp[core, 1 - t_mine] + tc_recv[1 - t_mine].astype(F32)).astype(BF16)
    tx_copy = send(t_send, t_recv, t_sems, 1, place.x_pair)
    t_total = tp[core, t_mine] + tc_recv[t_mine].astype(F32)
    for g in range(3):
        for step in range(1, PLANE):
            plane_copies[g][step - 1].wait()
            total[g] = total[g] + p_recv[g, step].astype(F32)
        z_own[48 * g : 48 * g + 48, :] = total[g]
    tx_copy.wait()
    z_own[144:192, :] = t_total + t_recv[...].astype(F32)

    for k in range(PZ):
        z_send[k] = z_own[24 * k : 24 * k + 24, :].astype(BF16)
    z_copies = []
    for step in (4, 3, 5, 2, 6, 1, 7):
        z_at = lax.rem(z + step, PZ)
        z_copies.append(send(z_send.at[z_at], z_recv.at[step], z_sems, step, place.device(x, y, z_at, core)))
    summed = z_own[pl.ds(pl.multiple_of(24 * z, 8), 24), :]
    for copy in z_copies:
        copy.wait()
    for step in range(1, PZ):
        summed = summed + z_recv[step].astype(F32)
    z_full[z] = summed.astype(BF16)
    a_copies = []
    for step in (4, 3, 5, 2, 6, 1, 7):
        z_at = lax.rem(z + step, PZ)
        a_copies.append(send(z_full.at[z], z_full.at[z], a_sems, step, place.device(x, y, z_at, core)))
    for copy in a_copies:
        copy.wait()
    full_b[core, y, x] = jnp.concatenate([z_full[k].astype(F32) for k in range(4)], 0).astype(BF16)
    full_c[core, x, y] = jnp.concatenate([z_full[k].astype(F32) for k in range(4, 8)], 0).astype(BF16)

    def x_away(step):
        return place.device(lax.rem(x + step, PX), y, z, core)

    def y_away(step):
        return place.device(x, lax.rem(y + step, PY), z, core)

    b_first, c_first, b_then, c_then, last = {}, {}, {}, {}, []
    for d in (2, 1, 3):
        b_first[d] = send(full_b.at[core, y, x], full_b.at[core, y, x], bx_sems, d, x_away(d))
        c_first[d] = send(full_c.at[core, x, y], full_c.at[core, x, y], cy_sems, d, y_away(d))
    for d in (2, 1, 3):
        b_then[0, d] = send(full_b.at[core, y, x], full_b.at[core, y, x], by_sems, d, y_away(d))
        c_then[0, d] = send(full_c.at[core, x, y], full_c.at[core, x, y], cx_sems, d, x_away(d))
    for e in (1, 3, 2):
        x_from, y_from = lax.rem(x + PX - e, PX), lax.rem(y + PY - e, PY)
        b_first[e].wait()
        for d in (2, 1, 3):
            b_then[e, d] = send(full_b.at[core, y, x_from], full_b.at[core, y, x_from], by_sems, 4 * e + d, y_away(d))
        c_first[e].wait()
        for d in (2, 1, 3):
            c_then[e, d] = send(full_c.at[core, x, y_from], full_c.at[core, x, y_from], cx_sems, 4 * e + d, x_away(d))
    last.append(send(full_b.at[core, y], full_b.at[core, y], k_sems, 0, place.sibling))
    last.append(send(full_c.at[core, x], full_c.at[core, x], k_sems, 4, place.sibling))
    for d in (1, 3, 2):
        x_from, y_from = lax.rem(x + PX - d, PX), lax.rem(y + PY - d, PY)
        for e in range(4):
            b_then[e, d].wait()
        last.append(send(full_b.at[core, y_from], full_b.at[core, y_from], k_sems, d, place.sibling))
        for e in range(4):
            c_then[e, d].wait()
        last.append(send(full_c.at[core, x_from], full_c.at[core, x_from], k_sems, 4 + d, place.sibling))
    for copy in last + home:
        copy.wait()
    own_gx.wait()


def step(*operands):
    sems = pltpu.SemaphoreType.DMA
    anywhere = pl.BlockSpec(memory_space=pl.ANY)
    in_specs = [anywhere] * len(operands)
    return pl.pallas_call(
        step_kernel,
        out_shape=(
            pltpu.VMEM((2, PY, PX, 96, 128), BF16),
            pltpu.VMEM((2, PX, PY, 96, 128), BF16),
            pltpu.VMEM((6, 12, 4, WIDTH), BF16),
        ),
        in_specs=in_specs,
        out_specs=(VMEM, VMEM, VMEM),
        scratch_shapes=[
            pltpu.VMEM((6, 12), jnp.int32),
            pltpu.VMEM((WT, WT), jnp.int32),
            pltpu.VMEM((WIDTH,), F32),
            pltpu.VMEM((WIDTH,), F32),
            pltpu.VMEM((WIDTH, 3 * WIDTH), BF16),
            pltpu.VMEM((3 * WIDTH,), F32),
            pltpu.VMEM((WIDTH, WIDTH), BF16),
            pltpu.VMEM((HEADS * 16, SLOTS), F32),
            pltpu.VMEM((4, 4, HEADS), F32),
            pltpu.VMEM((KEYS, WT), BF16),
            pltpu.VMEM((WT, KEYS), BF16),
            pltpu.VMEM((3 * WIDTH, WIDTH), BF16),
            pltpu.VMEM((WIDTH, WIDTH), BF16),
            pltpu.VMEM((768, 768), BF16),
            pltpu.VMEM((6, 12, 4, WIDTH), BF16),
            pltpu.VMEM((6, 12, 4, WIDTH), BF16),
            pltpu.VMEM((4, 8, 128), F32),
            pltpu.VMEM((4, 8, 128), F32),
            pltpu.VMEM((128, 128), F32),
            pltpu.VMEM((2, 2, 48, 128), F32),
            pltpu.VMEM((2, 2, 48, 128), BF16),
            pltpu.VMEM((6, 12, 4, WIDTH), BF16),
            pltpu.VMEM((3, 72, 8, 128), F32),
            pltpu.VMEM((288, WIDTH), F32),
            pltpu.VMEM((288, 1), F32),
            pltpu.VMEM((288, WIDTH), BF16),
            pltpu.VMEM((WIDTH, 288), BF16),
            pltpu.VMEM((288, WIDTH), BF16),
            pltpu.VMEM((288, 3 * WIDTH), BF16),
            pltpu.VMEM((288, WIDTH), BF16),
            pltpu.VMEM((2, 2, WIDTH, WT), BF16),
            pltpu.VMEM((2, 3, KEYS, 256), BF16),
            pltpu.VMEM((2, 3, 256, KEYS), BF16),
            pltpu.VMEM((2, 3, KEYS, 256), BF16),
            pltpu.VMEM((2, WIDTH, KEYS), BF16),
            pltpu.VMEM((WT, 128), BF16),
            pltpu.VMEM((768, 768), BF16),
            pltpu.VMEM((2, 16, 768), F32),
            pltpu.VMEM((2, 16, 8, 768), F32),
            pltpu.VMEM((288, WIDTH), BF16),
            pltpu.VMEM((288, WIDTH), F32),
            pltpu.VMEM((2, WT, 128), F32),
            pltpu.VMEM((2, 2, WIDTH, KEYS), F32),
            pltpu.VMEM((288, 3 * WIDTH), BF16),
            pltpu.VMEM((2, 16, 768), F32),
            pltpu.VMEM((3, 2, PLANE, 48, 128), BF16),
            pltpu.VMEM((3, PLANE, 48, 128), BF16),
            pltpu.VMEM((3, PLANE, 48, 128), BF16),
            pltpu.VMEM((3, PLANE, 48, 128), BF16),
            pltpu.VMEM((2, 48, 128), BF16),
            pltpu.VMEM((48, 128), BF16),
            pltpu.VMEM((48, 128), BF16),
            pltpu.VMEM((192, 128), F32),
            pltpu.VMEM((PZ, 24, 128), BF16),
            pltpu.VMEM((PZ, 24, 128), BF16),
            pltpu.VMEM((PZ, 24, 128), BF16),
            sems((2, 9)),
            sems((2, 3)),
            sems((2, 3)),
            sems((2, 2)),
            sems((2, 3 * PLANE)),
            sems((2, PZ)),
            sems((2, PZ)),
            sems((2, 4)),
            sems((2, 16)),
            sems((2, 16)),
            sems((2, 4)),
            sems((2, 8)),
            sems((13,)),
        ],
        compiler_params=pltpu.CompilerParams(
            collective_id=0, has_side_effects=True, vmem_limit_bytes=60 * 1024 * 1024
        ),
        name="step",
    )(*operands)


def small_row(e):
    quarter, k = e // 6, e % 6
    return quarter // 2, quarter % 2, 16 * (k // 4) + 12 + k % 4


def finish_kernel(
    grad_scale, full_b, full_c, gx, o_gx, o_wqkv, o_bqkv, o_wproj, o_bproj, o_gain, o_shift, o_pos, o_surf
):
    o_gx[...] = gx[...]

    def chunk(core, at):
        x, y = at % PX, at // PX
        return full_b.at[core, y, x], full_c.at[core, x, y]

    for n in range(2 * PLANE):
        b, c = chunk(n // PLANE, n % PLANE)
        for g in range(3):
            source = (b, b, c)[g]
            rows = (0, 48, 0)[g]
            part = source[rows : rows + 48, :].astype(F32) * grad_scale
            if n < 24:
                i, at = n // 3, WIDTH * (n % 3) + 128 * g
                o_wqkv[48 * i : 48 * i + 48, at : at + 128] = part
            else:
                at = 128 * g + 16 * (n - 24)
                for m in range(3):
                    o_wproj[at : at + 16, 128 * m : 128 * m + 128] = part[16 * m : 16 * m + 16, :]

    quarters = {}
    for core in range(2):
        for at in range(PLANE):
            x, y = at % PX, at // PX
            kind = (y * 2 + x // 2) * 2 + core
            rows = chunk(core, at)[1][48:96, :].astype(F32) * grad_scale
            key = core, x % 2
            quarters[key] = rows if key not in quarters else quarters[key] + rows
            for k in range(3):
                lo = 128 * (3 * (x % 2) + k)
                width = min(128, SLOTS - lo)
                for h in range(HEADS):
                    o_pos[16 * h + kind : 16 * h + kind + 1, lo : lo + width] = rows[
                        16 * k + h : 16 * k + h + 1, :width
                    ]

    def small(e):
        w, half, at = small_row(e)
        return quarters[w, half][at : at + 1, :]

    o_bqkv[...] = jnp.concatenate([small(n) for n in range(9)], 1).reshape(3 * WIDTH)
    for v, out in enumerate((o_bproj, o_gain, o_shift)):
        out[...] = jnp.concatenate([small(9 + 3 * v + m) for m in range(3)], 1).reshape(WIDTH)
    for a in range(4):
        side = small(18 + a)
        for b in range(4):
            o_surf[a, b : b + 1, :] = side[:, 12 * b : 12 * b + 12]


def finish(full_b, full_c, gx, grad_scale):
    one = lambda *shape: jax.ShapeDtypeStruct(shape, F32)
    return pl.pallas_call(
        functools.partial(finish_kernel, grad_scale),
        out_shape=(
            jax.ShapeDtypeStruct((6, 12, 4, WIDTH), BF16),
            one(WIDTH, 3 * WIDTH),
            one(3 * WIDTH),
            one(WIDTH, WIDTH),
            one(WIDTH),
            one(WIDTH),
            one(WIDTH),
            one(HEADS * 16, SLOTS),
            one(4, 4, HEADS),
        ),
        in_specs=[VMEM] * 3,
        out_specs=(VMEM,) * 9,
        compiler_params=pltpu.CompilerParams(vmem_limit_bytes=32 * 1024 * 1024),
        name="finish",
    )(full_b, full_c, gx)


def on_device(
    inputs, cotangent, land_sea, rel_index, norm_gain, norm_shift, w_qkv, b_qkv, w_proj, pos_bias, surf_bias
):
    levels, lat_rows, lon_cols, width = inputs.shape
    count = levels * lat_rows * lon_cols * lax.axis_size("lat") * lax.axis_size("lon")
    full_b, full_c, gx = step(
        inputs.transpose(1, 2, 0, 3),
        cotangent.transpose(1, 2, 0, 3),
        land_sea,
        rel_index,
        norm_gain,
        norm_shift,
        w_qkv,
        b_qkv,
        w_proj,
        pos_bias.transpose(1, 0, 2).reshape(-1, SLOTS),
        surf_bias.transpose(1, 2, 0),
    )
    outs = finish(full_b, full_c, gx, float(count) ** -0.5)
    g_x, g_wqkv, g_bqkv, g_wproj, g_bproj, g_gain, g_shift, g_pos, g_surf = outs
    return (
        g_x.transpose(2, 0, 1, 3),
        g_wqkv,
        g_bqkv,
        g_wproj,
        g_bproj,
        g_gain,
        g_shift,
        g_pos.reshape(HEADS, 16, SLOTS).transpose(1, 0, 2),
        g_surf.transpose(2, 0, 1),
    )


def solution(mesh):
    in_specs = (P(None, "lat", "lon", None), P(None, "lat", "lon", None), P("lat", "lon")) + (P(),) * 8
    out_specs = (P(None, "lat", "lon", None),) + (P(),) * 8
    return jax.shard_map(on_device, mesh=mesh, in_specs=in_specs, out_specs=out_specs, check_vma=False)
```

```python
import functools

import jax
import jax.numpy as jnp
from jax import lax
from jax.experimental import pallas as pl
from jax.experimental.pallas import tpu as pltpu
from jax.sharding import PartitionSpec as P

F32 = jnp.float32
BF16 = jnp.bfloat16
MESH = pl.DeviceIdType.MESH
EPS = 1e-05
LOG2E = 1.4426950408889634
BIG = 2.0**33
HEADS = 12
SLOTS = 759
WIDTH = 384
WT = 144
PITCH = 23
KEYS = 256
SCALE = 32.0**-0.5
NT = (((1,), (1,)), ((), ()))
TN = (((0,), (0,)), ((), ()))
NN = (((1,), (0,)), ((), ()))
PX, PY, PZ = 4, 4, 8
PLANE = PX * PY
VMEM = pl.BlockSpec(memory_space=pltpu.VMEM)


def dot(a, b, dims=NN):
    return lax.dot_general(a, b, dims, preferred_element_type=F32)


class Place:
    def __init__(self):
        lat, lon = lax.axis_index("lat"), lax.axis_index("lon")
        n_lat, n_lon = lax.axis_size("lat"), lax.axis_size("lon")
        self.lat, self.n_lat = lat, n_lat
        self.core = lax.rem(lon, 2)
        self.z = lax.rem(lon // 2, PZ)
        self.x = lax.rem(lat, 2) * 2 + lon // (2 * PZ)
        self.y = lat // 2
        self.here = self.y * PX + self.x
        up, down = lax.rem(lat + 1, n_lat), lax.rem(lat + n_lat - 1, n_lat)
        right, left = lax.rem(lon + 1, n_lon), lax.rem(lon + n_lon - 1, n_lon)
        self.north, self.south = (up, lon), (down, lon)
        self.east, self.west = (lat, right), (lat, left)
        self.north_east, self.south_west = (up, right), (down, left)
        self.sibling = (lat, lon + 1 - 2 * self.core)
        self.x_pair = self.device(self.x + 1 - 2 * lax.rem(self.x, 2), self.y, self.z, self.core)

    def device(self, x, y, z, core):
        return (y * 2 + x // 2, (lax.rem(x, 2) * PZ + z) * 2 + core)

    def in_plane(self, step, sign):
        x = lax.rem(self.x + PX + sign * (step % PX), PX)
        y = lax.rem(self.y + PY + sign * (step // PX), PY)
        return x, y, y * PX + x

    def greet(self):
        others = [self.north, self.south, self.east, self.west, self.north_east, self.south_west, self.sibling]
        for step in range(1, PLANE):
            x, y, _ = self.in_plane(step, -1)
            others.append(self.device(x, y, self.z, self.core))
        for step in range(1, PZ):
            others.append(self.device(self.x, self.y, lax.rem(self.z + PZ - step, PZ), self.core))
        for other in others:
            pl.semaphore_signal(pltpu.get_barrier_semaphore(), inc=1, device_id=other, device_id_type=MESH)
        self.greeted = len(others)

    def meet(self):
        pl.semaphore_wait(pltpu.get_barrier_semaphore(), self.greeted)


def send(src, dst, sems, k, to):
    copy = pltpu.make_async_remote_copy(
        src_ref=src,
        dst_ref=dst,
        send_sem=sems.at[0, k],
        recv_sem=sems.at[1, k],
        device_id=to,
        device_id_type=MESH,
    )
    copy.start()
    return copy


def key_of(token):
    level, cell = token // 72, lax.rem(token, 72)
    return 128 * level + cell + (PITCH - 12) * (cell // 12)


def plain_rows():
    rows = lax.broadcasted_iota(jnp.int32, (72, 128), 0)
    return rows + (PITCH - 12) * (rows // 12)


def skew_parts(rows):
    lane = lax.broadcasted_iota(jnp.int32, (72, 128), 1)
    first = lane + rows >= PITCH * 5 + 11
    there = jnp.bitwise_and(lane - rows - 2, 127)
    back = jnp.bitwise_and(lane + rows + 2, 127)
    return first, there, back


def skew(table, first, there):
    mixed = jnp.where(first, table[:, :128], table[:, 128:])
    return jnp.take_along_axis(mixed, there, axis=1)


def split(values, count):
    pieces = []
    for _ in range(count):
        piece = values.astype(BF16)
        pieces.append(piece)
        values = values - piece.astype(F32)
    return pieces


def step_kernel(
    x_in, dy_in, land_in, rel_in, gain_in, shift_in, w_qkv_in, b_qkv_in, w_proj_in, pos_in, surf_in,
    full_b, full_c, gx_out,
    land, rel, gain, shift, w_qkv, b_qkv, w_proj, pos, surf, c_spread, c_back, w_qkv_t, w_proj_t, onehot_t,
    tok_x, tok_dy, cls_out, cls_in, side_in, tp, tp_low, gx,
    mixed, white, inv_std, normed, normed_t, dy_low, qkv, dctx, turned, k_cat, k_cat_t, v_cat, v_turned, q_feat,
    onehot, tables, d_tables, ctx_acc, dq_acc, f_acc, dkv_t, low, table_in,
    wp, c_recv, p_send, p_recv, tc_recv, t_send, t_recv, z_own, z_send, z_recv, z_full, z_cat,
    f_sems, h_sems, c_sems, t_sems, p_sems, z_sems, a_sems, bx_sems, by_sems, cx_sems, cy_sems, k_sems, local,
):
    place = Place()
    core, x, y, z, here = place.core, place.x, place.y, place.z, place.here
    place.greet()
    fetches = [
        pltpu.make_async_copy(a, b, local.at[4 + k])
        for k, (a, b) in enumerate(
            (
                (land_in, land), (pos_in, pos), (rel_in, rel), (w_qkv_in, w_qkv), (w_proj_in, w_proj),
                (gain_in, gain), (shift_in, shift), (b_qkv_in, b_qkv), (surf_in, surf),
            )
        )
    ]
    for copy in fetches:
        copy.start()

    cls_out[...] = jnp.zeros_like(cls_out)
    fetches[0].wait()
    for q in range(4):
        cls_out[q, :3, :6] = land[3 * (q // 2) : 3 * (q // 2) + 3, 6 * (q % 2) : 6 * (q % 2) + 6].astype(F32)

    def quadrant(ref, q):
        return ref.at[pl.ds(3 * (q // 2), 3), pl.ds(6 * (q % 2), 6)]

    place.meet()
    routes = ((0, place.south_west), (1, place.south), (2, place.west))
    halo_x = [send(quadrant(x_in, q), quadrant(tok_x, 3 - q), f_sems, q, to) for q, to in routes]
    halo_x += [send(cls_out.at[q], cls_in.at[3 - q], f_sems, 3 + q, to) for q, to in routes]
    halo_dy = [send(quadrant(dy_in, q), quadrant(tok_dy, 3 - q), f_sems, 6 + q, to) for q, to in routes]
    own_x = pltpu.make_async_copy(quadrant(x_in, 3), quadrant(tok_x, 0), local.at[0])
    own_dy = pltpu.make_async_copy(quadrant(dy_in, 3), quadrant(tok_dy, 0), local.at[1])
    own_cls = pltpu.make_async_copy(cls_out.at[3], cls_in.at[0], local.at[2])
    for copy in (own_x, own_dy, own_cls):
        copy.start()

    lat = place.lat
    last_band = lat == place.n_lat - 1
    for copy in fetches[1:]:
        copy.wait()
    key_at = lax.broadcasted_iota(jnp.int32, (KEYS, WT), 0)
    c_spread[...] = jnp.where(key_at == key_of(lax.broadcasted_iota(jnp.int32, (KEYS, WT), 1)), 1.0, 0.0).astype(BF16)
    key_at = lax.broadcasted_iota(jnp.int32, (WT, KEYS), 1)
    c_back[...] = jnp.where(key_at == key_of(lax.broadcasted_iota(jnp.int32, (WT, KEYS), 0)), 1.0, 0.0).astype(BF16)
    rel_now = rel[...]
    rel_low = jnp.bitwise_and(rel_now, 15)
    rel_wide = dot((rel_now - rel_low).astype(F32).astype(BF16), c_spread[...], NT) + dot(
        rel_low.astype(F32).astype(BF16), c_spread[...], NT
    )
    rel_lane = jnp.bitwise_and(lax.broadcasted_iota(jnp.int32, (WT, KEYS), 1), 127)
    rel_wide = jnp.where(lax.rem(rel_lane, PITCH) < 12, rel_wide, -1.0)
    first, _, back = skew_parts(plain_rows())
    slot = lax.broadcasted_iota(jnp.int32, (768, 128), 0).astype(F32)
    for b, block in enumerate((rel_wide[:72, :128], rel_wide[:72, 128:], rel_wide[72:, :128])):
        turned_back = jnp.take_along_axis(block, back, axis=1)
        for half in range(2):
            kept = jnp.where(first, turned_back, -1.0) if half == 0 else jnp.where(first, -1.0, turned_back)
            slots = jnp.max(kept, 0, keepdims=True)
            lanes = slice(b * 256 + half * 128, b * 256 + half * 128 + 128)
            onehot[:, lanes] = jnp.where(slot == slots, 1.0, 0.0).astype(BF16)
    table_in[...] = jnp.zeros_like(table_in)
    for w in range(2):
        for h in range(HEADS):
            table_in[w, h : h + 1, :SLOTS] = pos[pl.ds(16 * h + 2 * lat + w, 1), :] * LOG2E
        tables[w] = functools.reduce(jnp.add, [dot(part, onehot[...]) for part in split(table_in[w], 3)])

    onehot_t[...] = onehot[...].T
    w_qkv_t[...] = w_qkv[...].T
    w_proj_t[...] = w_proj[...].T

    eye = (
        lax.broadcasted_iota(jnp.int32, (WIDTH, WIDTH), 0) == lax.broadcasted_iota(jnp.int32, (WIDTH, WIDTH), 1)
    ).astype(F32).astype(BF16)
    strided = mixed.reshape(3 * 576, 128)

    def in_order(tok, first_row, out):
        for j in range(3):
            cols = slice(128 * j, 128 * j + 128)
            mixed[j, :, first_row : first_row + 4, :] = tok[:, :, :, cols].reshape(72, 4, 128).astype(F32)
        for k in range(4):
            level = (1, 2, 3, 0)[k]
            for j in range(3):
                out[72 * k : 72 * k + 72, 128 * j : 128 * j + 128] = strided[
                    pl.ds(576 * j + first_row + level, 72, stride=8), :
                ]

    for copy in halo_x + [own_x, own_cls]:
        copy.wait()
    in_order(tok_x, 0, white)
    tokens = white[...]
    centred = tokens - jnp.mean(tokens, -1, keepdims=True)
    inv = lax.rsqrt(jnp.mean(centred * centred, -1, keepdims=True) + EPS)
    inv_std[...] = inv
    whitened = centred * inv
    white[...] = whitened
    gain_row = gain[...].reshape(1, WIDTH)
    normed[...] = (whitened * gain_row + shift[...].reshape(1, WIDTH)).astype(BF16)
    qkv[...] = (dot(normed[...], w_qkv[...]) + b_qkv[...].reshape(1, 3 * WIDTH)).astype(BF16)
    normed_t[...] = dot(eye, normed[...], NT).astype(BF16)
    for w in range(2):
        rows = slice(w * WT, (w + 1) * WT)
        turned[w, 0] = dot(eye, qkv[rows, :WIDTH], NT).astype(BF16)
        padded = dot(c_spread[...], qkv[rows, WIDTH:]).astype(BF16)
        k_turned = dot(eye, padded[:, :WIDTH], NT).astype(BF16)
        v_turned[w] = dot(eye, padded[:, WIDTH:], NT).astype(BF16)
        for g in range(3):
            lanes = slice(128 * g, 128 * g + 128)
            k_cat[w, g, :, :128] = padded[:, lanes]
            k_cat_t[w, g, :128, :] = k_turned[lanes, :]
            v_cat[w, g, :, :128] = padded[:, WIDTH + 128 * g : WIDTH + 128 * g + 128]
            v_cat[w, g, :, 128:] = jnp.ones((KEYS, 128), BF16)

    lane = lax.broadcasted_iota(jnp.int32, (WT, 128), 1)
    token = lax.broadcasted_iota(jnp.int32, (WT, 128), 0)
    cell = lax.rem(token, 72)
    cell_row, cell_col = cell // 12, lax.rem(cell, 12)
    in_quad = 8 * (2 * (cell_row // 3) + cell_col // 6) + lax.rem(cell_row, 3)
    pick_row = jnp.where(lane == in_quad, 1.0, 0.0).astype(BF16)[:, :32]
    pick_col = jnp.where(lane == lax.rem(cell_col, 6), 1.0, 0.0)
    cells = dot(pick_row, cls_in[...].reshape(32, 128).astype(BF16)) * pick_col
    kind = dot(cells.astype(BF16), jnp.ones((128, 128), BF16)).astype(jnp.int32)
    turned_over = jnp.logical_and(lax.rem(token, 72) >= 36, last_band).astype(F32)
    of_key = jnp.where(kind == lax.rem(lane, 48) // 12, 1.0, 0.0)
    of_query = jnp.where(kind == lane, 1.0, 0.0).astype(BF16)
    side_in[...] = jnp.zeros_like(side_in)
    for a in range(4):
        for b in range(4):
            side_in[a : a + 1, 12 * b : 12 * b + 12] = surf[a, b : b + 1, :]
            side_in[a : a + 1, 48 + 12 * b : 60 + 12 * b] = surf[a, b : b + 1, :]
    surf_lane = lax.broadcasted_iota(jnp.int32, (128, 128), 1)
    surf_hi, surf_lo = split(side_in[...] * (1.0 / SCALE), 2)
    side = dot(of_query, jnp.where(surf_lane < 48, surf_hi.astype(F32), surf_lo.astype(F32)).astype(BF16))
    q_feat[...] = jnp.where(
        lane < 96, side, jnp.where(lane == 96, turned_over, jnp.where(lane == 97, 1.0 - turned_over, 0.0))
    ).astype(BF16)
    key_side = jnp.where(
        lane < 96,
        of_key,
        jnp.where(lane == 96, -BIG * (1.0 - turned_over), jnp.where(lane == 97, -BIG * turned_over, 0.0)),
    ).astype(BF16)
    key_lane = lax.broadcasted_iota(jnp.int32, (KEYS, 128), 1)
    key_row = jnp.bitwise_and(lax.broadcasted_iota(jnp.int32, (KEYS, 128), 0), 127)
    hidden = jnp.logical_and(lax.rem(key_row, PITCH) >= 12, jnp.logical_and(key_lane >= 96, key_lane < 98))
    k_feat = jnp.where(hidden, -BIG, dot(c_spread[...], key_side)).astype(BF16)
    k_feat_t = dot(eye[:128, :128], k_feat, NT).astype(BF16)
    for w in range(2):
        for g in range(3):
            k_cat[w, g, :, 128:] = k_feat
            k_cat_t[w, g, 128:, :] = k_feat_t

    for copy in halo_dy + [own_dy]:
        copy.wait()
    in_order(tok_dy, 4, dq_acc)
    dy_low[...] = dq_acc[...].astype(BF16)
    dctx[...] = dot(dy_low[...], w_proj_t[...]).astype(BF16)
    for w in range(2):
        turned[w, 1] = dot(eye, dctx[w * WT : (w + 1) * WT, :], NT).astype(BF16)

    zero = jnp.zeros((72, 128), F32)
    cat_lane = lax.broadcasted_iota(jnp.int32, (1, 256), 1)
    half_lane = lax.broadcasted_iota(jnp.int32, (1, 128), 1)
    block_row = jnp.bitwise_and(lax.broadcasted_iota(jnp.int32, (256, 512), 0), 127)
    block_lane = lax.broadcasted_iota(jnp.int32, (256, 512), 1)
    blocks_of_ones = jnp.where(block_row // 32 == block_lane // 128, 1.0, 0.0).astype(BF16)
    first, there, back = skew_parts(plain_rows())

    def own_level(a):
        return jnp.concatenate([a[:72, :128], a[72:, 128:]], 0)

    def both_levels(a):
        top = jnp.concatenate([a[:72], zero], 1)
        return jnp.concatenate([top, jnp.concatenate([zero, a[72:]], 1)], 0)

    def group_step(g, between=lambda: None):
        lanes = slice(g * 128, g * 128 + 128)
        for w in range(2):
            rows = slice(w * WT, (w + 1) * WT)
            part = [slice(WT * hh, WT * hh + WT) for hh in range(4)]
            q_cat = jnp.concatenate([qkv[rows, lanes], q_feat[...]], 1)
            dctx_now = dctx[rows, lanes]
            q_all, dctx_all = [], []
            for hh in range(4):
                mine = cat_lane // 32 == hh
                feat_mine = jnp.logical_and(
                    cat_lane >= 128, jnp.logical_or(cat_lane >= 224, lax.rem(cat_lane + 4, 12) == g * 4 + hh)
                )
                keep = jnp.logical_or(mine, feat_mine).astype(F32).astype(BF16)
                q_all.append(q_cat * keep)
                dctx_all.append(dctx_now * keep[:, :128])
            raw_all = dot(jnp.concatenate(q_all, 0), k_cat_t[w, g])
            d_raw_all = dot(jnp.concatenate(dctx_all, 0), v_turned[w, lanes, :])
            powers = []
            for hh in range(4):
                head = g * 4 + hh
                raw = raw_all[part[hh]]
                table = tables[w, head : head + 1, :]
                same = skew(table[:, :256], first, there)
                if w == 0:
                    upper = jnp.concatenate([same, skew(table[:, 256:512], first, there)], 1)
                    lower = jnp.concatenate([skew(table[:, 512:], first, there), same], 1)
                    bias = jnp.concatenate([upper, lower], 0)
                else:
                    raw = own_level(raw)
                    bias = jnp.concatenate([same, same], 0)
                score = raw * (SCALE * LOG2E) + bias
                powers.append(jnp.exp2(score - jnp.max(score, -1, keepdims=True)))
            wide = [a if w == 0 else both_levels(a) for a in powers]
            mixed_all = dot(jnp.concatenate([a.astype(BF16) for a in wide], 0), v_cat[w, g])
            inverse, context = [], jnp.zeros((WT, 128), F32)
            for hh in range(4):
                inverse.append(1.0 / mixed_all[part[hh], 128:])
                context = jnp.where(half_lane // 32 == hh, mixed_all[part[hh], :128] * inverse[hh], context)
            ctx_acc[rows, lanes] = context.astype(BF16)
            shares = jnp.concatenate(split(dctx_now.astype(F32) * context, 2), 1)
            deltas = dot(shares, blocks_of_ones)
            score_lows = []
            for hh in range(4):
                head = g * 4 + hh
                d_raw, delta = d_raw_all[part[hh]], deltas[:, 128 * hh : 128 * hh + 128]
                if w == 0:
                    double = lambda a: jnp.concatenate([a, a], 1)
                    probs = powers[hh] * double(inverse[hh])
                    d_score = probs * (d_raw - double(delta))
                    blocks = (d_score[:72, :128] + d_score[72:, 128:], d_score[:72, 128:], d_score[72:, :128])
                    probs_low, score_low = probs.astype(BF16), d_score.astype(BF16)
                else:
                    probs = powers[hh] * inverse[hh]
                    d_score = probs * (own_level(d_raw) - delta)
                    blocks = (d_score[:72] + d_score[72:],)
                    probs_low, score_low = both_levels(probs).astype(BF16), both_levels(d_score).astype(BF16)
                score_lows.append(score_low)
                head_rows = slice(head * 32, head * 32 + 32)
                dkv_t[w, 0, head_rows, :] = dot(turned[w, 0, head_rows, :], score_low) * SCALE
                dkv_t[w, 1, head_rows, :] = dot(turned[w, 1, head_rows, :], probs_low)
                for b, block in enumerate(blocks):
                    turned_back = jnp.take_along_axis(block, back, axis=1)
                    early = jnp.where(first, turned_back, 0.0)
                    late = turned_back - early
                    d_tables[w, head, :, b * 256 : b * 256 + 128] = jnp.sum(early.reshape(9, 8, 128), 0)
                    d_tables[w, head, :, b * 256 + 128 : b * 256 + 256] = jnp.sum(late.reshape(9, 8, 128), 0)
            both_all = dot(jnp.concatenate(score_lows, 0), k_cat[w, g])
            dq, feats = jnp.zeros((WT, 128), F32), f_acc[w]
            for hh in range(4):
                dq = jnp.where(half_lane // 32 == hh, both_all[part[hh], :128], dq)
                feats = jnp.where(lax.rem(half_lane, 12) == g * 4 + hh, both_all[part[hh], 128:], feats)
            dq_acc[rows, lanes] = dq * SCALE
            f_acc[w] = feats
            if w == 0:
                between()

    sums = {}

    def weight_grads(g):
        lanes = slice(128 * g, 128 * g + 128)
        dq = dq_acc[:, lanes]
        low[:, lanes] = dq.astype(BF16)
        sums[0, g] = jnp.sum(dq, 0, keepdims=True)
        for part in range(2):
            total = jnp.zeros((1, 128), F32)
            for w in range(2):
                rows_now = dot(c_back[...], dkv_t[w, part, lanes, :].astype(BF16), NT)
                total += jnp.sum(rows_now, 0, keepdims=True)
                at = WIDTH * (part + 1) + 128 * g
                low[w * WT : (w + 1) * WT, at : at + 128] = rows_now.astype(BF16)
            sums[part + 1, g] = total
        for part in range(3):
            at = WIDTH * part + 128 * g
            grad = dot(normed_t[...], low[:, at : at + 128])
            for i in range(8):
                n = 3 * i + part
                wp[g, n // PLANE, n % PLANE] = grad[48 * i : 48 * i + 48, :].astype(BF16)
        grad = dot(ctx_acc[:, lanes], dy_low[...], TN)
        for u in range(8):
            n = 24 + u
            for m in range(3):
                wp[g, n // PLANE, n % PLANE, 16 * m : 16 * m + 16, :] = grad[
                    16 * u : 16 * u + 16, 128 * m : 128 * m + 128
                ].astype(BF16)
        return send(wp.at[g, 1 - core], c_recv.at[g], c_sems, g, place.sibling)

    def plane_sends(g, core_copy):
        core_copy.wait()
        copies = []
        for step in range(1, PLANE):
            x_at, y_at, at = place.in_plane(step, 1)
            p_send[g, step] = (wp[g, core, at].astype(F32) + c_recv[g, at].astype(F32)).astype(BF16)
            copies.append(
                send(
                    p_send.at[g, step], p_recv.at[g, step], p_sems, g * PLANE + step, place.device(x_at, y_at, z, core)
                )
            )
        return copies

    d_tables[...] = jnp.zeros_like(d_tables)
    f_acc[...] = jnp.zeros_like(f_acc)
    plane_copies = []
    group_step(0)
    core_copies = [weight_grads(0)]
    group_step(1)
    plane_copies.append(plane_sends(0, core_copies[0]))
    core_copies.append(weight_grads(1))
    group_step(2)
    plane_copies.append(plane_sends(1, core_copies[1]))
    core_copies.append(weight_grads(2))

    d_normed = dot(low[...], w_qkv_t[...]).astype(BF16).astype(F32)

    for w in range(2):
        table = functools.reduce(jnp.add, [dot(part, onehot_t[...]) for part in split(jnp.sum(d_tables[w], 1), 2)])
        for half in range(2):
            for k in range(3):
                at = 128 * (3 * half + k)
                tp[w, half, 16 * k : 16 * k + 16, :] = table[:, at : at + 128]
    small = [sums[part, g] for part in range(3) for g in range(3)]
    for total in (
        jnp.sum(dy_low[...].astype(F32), 0, keepdims=True),
        jnp.sum(d_normed * white[...], 0, keepdims=True),
        jnp.sum(d_normed, 0, keepdims=True),
    ):
        small += [total[:, 128 * m : 128 * m + 128] for m in range(3)]
    d_surf = functools.reduce(jnp.add, [dot(of_query, part, TN) for part in split(f_acc[0] + f_acc[1], 2)])
    small += [d_surf[a : a + 1, :] for a in range(4)]
    for e, row in enumerate(small):
        w, half, at = small_row(e)
        tp[w, half, at : at + 1, :] = row
    tp_low[...] = tp[...].astype(BF16)
    t_copy = send(tp_low.at[1 - core], tc_recv, t_sems, 0, place.sibling)
    plane_copies.append(plane_sends(2, core_copies[2]))

    scaled = d_normed * gain_row
    first_mean = jnp.mean(scaled, -1, keepdims=True)
    second_mean = jnp.mean(scaled * white[...], -1, keepdims=True)
    dq_acc[...] = dy_low[...].astype(F32) + inv_std[...] * (scaled - first_mean - white[...] * second_mean)
    for j in range(3):
        cols = slice(128 * j, 128 * j + 128)
        for k in range(4):
            level = (1, 2, 3, 0)[k]
            strided[pl.ds(576 * j + level, 72, stride=8), :] = dq_acc[72 * k : 72 * k + 72, cols]
        gx[:, :, :, cols] = mixed[j, :, 0:4, :].astype(BF16).reshape(6, 12, 4, 128)

    def plane_total(g):
        total = wp[g, core, here].astype(F32) + c_recv[g, here].astype(F32)
        for step in range(1, PLANE):
            plane_copies[g][step - 1].wait()
            total = total + p_recv[g, step].astype(F32)
        return total

    def along_z(src, dst, sems, s):
        return [
            send(src(step), dst(step), sems, PZ * s + step, place.device(x, y, lax.rem(z + step, PZ), core))
            for step in (4, 3, 5, 2, 6, 1, 7)
        ]

    def z_sum(s, upper, lower):
        for k in range(PZ):
            piece = (upper, lower)[k // 4][12 * (k % 4) : 12 * (k % 4) + 12, :]
            z_own[s, k] = piece
            z_send[s, k] = piece.astype(BF16)
        return along_z(lambda step: z_send.at[s, lax.rem(z + step, PZ)], lambda step: z_recv.at[s, step], z_sems, s)

    def z_share(s, copies):
        for copy in copies:
            copy.wait()
        summed = z_own[s, z]
        for step in range(1, PZ):
            summed = summed + z_recv[s, step].astype(F32)
        z_full[s, z] = summed.astype(BF16)
        return along_z(lambda step: z_full.at[s, z], lambda step: z_full.at[s, z], a_sems, s)

    def z_join(s, copies):
        for copy in copies:
            copy.wait()
        for k in range(PZ):
            z_cat[12 * k : 12 * k + 12, :] = z_full[s, k].astype(F32)
        return z_cat[...].astype(BF16)

    t_mine = lax.rem(x, 2)
    total_0 = plane_total(0)
    t_copy.wait()
    t_send[...] = (tp[core, 1 - t_mine] + tc_recv[1 - t_mine].astype(F32)).astype(BF16)
    tx_copy = send(t_send, t_recv, t_sems, 1, place.x_pair)
    t_total = tp[core, t_mine] + tc_recv[t_mine].astype(F32)
    early = z_sum(0, total_0, plane_total(1))
    total_2 = plane_total(2)
    tx_copy.wait()
    late = z_sum(1, total_2, t_total + t_recv[...].astype(F32))
    early = z_share(0, early)
    home = [
        send(quadrant(gx, q), quadrant(gx_out, 3 - q), h_sems, q - 1, to)
        for q, to in ((1, place.east), (2, place.north), (3, place.north_east))
    ]
    own_gx = pltpu.make_async_copy(quadrant(gx, 0), quadrant(gx_out, 3), local.at[3])
    own_gx.start()
    late = z_share(1, late)

    def x_away(step):
        return place.device(lax.rem(x + step, PX), y, z, core)

    def y_away(step):
        return place.device(x, lax.rem(y + step, PY), z, core)

    b_first, c_first, b_then, c_then, last = {}, {}, {}, {}, []
    full_b[core, y, x] = z_join(0, early)
    for d in (2, 1, 3):
        b_first[d] = send(full_b.at[core, y, x], full_b.at[core, y, x], bx_sems, d, x_away(d))
    for d in (2, 1, 3):
        b_then[0, d] = send(full_b.at[core, y, x], full_b.at[core, y, x], by_sems, d, y_away(d))
    full_c[core, x, y] = z_join(1, late)
    for d in (2, 1, 3):
        c_first[d] = send(full_c.at[core, x, y], full_c.at[core, x, y], cy_sems, d, y_away(d))
    for d in (2, 1, 3):
        c_then[0, d] = send(full_c.at[core, x, y], full_c.at[core, x, y], cx_sems, d, x_away(d))
    for e in (1, 3, 2):
        x_from = lax.rem(x + PX - e, PX)
        b_first[e].wait()
        for d in (2, 1, 3):
            b_then[e, d] = send(full_b.at[core, y, x_from], full_b.at[core, y, x_from], by_sems, 4 * e + d, y_away(d))
    last.append(send(full_b.at[core, y], full_b.at[core, y], k_sems, 0, place.sibling))
    for e in (1, 3, 2):
        y_from = lax.rem(y + PY - e, PY)
        c_first[e].wait()
        for d in (2, 1, 3):
            c_then[e, d] = send(full_c.at[core, x, y_from], full_c.at[core, x, y_from], cx_sems, 4 * e + d, x_away(d))
    last.append(send(full_c.at[core, x], full_c.at[core, x], k_sems, 4, place.sibling))
    for d in (1, 3, 2):
        y_from = lax.rem(y + PY - d, PY)
        for e in range(4):
            b_then[e, d].wait()
        last.append(send(full_b.at[core, y_from], full_b.at[core, y_from], k_sems, d, place.sibling))
    for d in (1, 3, 2):
        x_from = lax.rem(x + PX - d, PX)
        for e in range(4):
            c_then[e, d].wait()
        last.append(send(full_c.at[core, x_from], full_c.at[core, x_from], k_sems, 4 + d, place.sibling))
    for copy in last + home:
        copy.wait()
    own_gx.wait()


def step(*operands):
    sems = pltpu.SemaphoreType.DMA
    anywhere = pl.BlockSpec(memory_space=pl.ANY)
    in_specs = [anywhere] * len(operands)
    return pl.pallas_call(
        step_kernel,
        out_shape=(
            pltpu.VMEM((2, PY, PX, 96, 128), BF16),
            pltpu.VMEM((2, PX, PY, 96, 128), BF16),
            pltpu.VMEM((6, 12, 4, WIDTH), BF16),
        ),
        in_specs=in_specs,
        out_specs=(VMEM, VMEM, VMEM),
        scratch_shapes=[
            pltpu.VMEM((6, 12), jnp.int32),
            pltpu.VMEM((WT, WT), jnp.int32),
            pltpu.VMEM((WIDTH,), F32),
            pltpu.VMEM((WIDTH,), F32),
            pltpu.VMEM((WIDTH, 3 * WIDTH), BF16),
            pltpu.VMEM((3 * WIDTH,), F32),
            pltpu.VMEM((WIDTH, WIDTH), BF16),
            pltpu.VMEM((HEADS * 16, SLOTS), F32),
            pltpu.VMEM((4, 4, HEADS), F32),
            pltpu.VMEM((KEYS, WT), BF16),
            pltpu.VMEM((WT, KEYS), BF16),
            pltpu.VMEM((3 * WIDTH, WIDTH), BF16),
            pltpu.VMEM((WIDTH, WIDTH), BF16),
            pltpu.VMEM((768, 768), BF16),
            pltpu.VMEM((6, 12, 4, WIDTH), BF16),
            pltpu.VMEM((6, 12, 4, WIDTH), BF16),
            pltpu.VMEM((4, 8, 128), F32),
            pltpu.VMEM((4, 8, 128), F32),
            pltpu.VMEM((128, 128), F32),
            pltpu.VMEM((2, 2, 48, 128), F32),
            pltpu.VMEM((2, 2, 48, 128), BF16),
            pltpu.VMEM((6, 12, 4, WIDTH), BF16),
            pltpu.VMEM((3, 72, 8, 128), F32),
            pltpu.VMEM((288, WIDTH), F32),
            pltpu.VMEM((288, 1), F32),
            pltpu.VMEM((288, WIDTH), BF16),
            pltpu.VMEM((WIDTH, 288), BF16),
            pltpu.VMEM((288, WIDTH), BF16),
            pltpu.VMEM((288, 3 * WIDTH), BF16),
            pltpu.VMEM((288, WIDTH), BF16),
            pltpu.VMEM((2, 2, WIDTH, WT), BF16),
            pltpu.VMEM((2, 3, KEYS, 256), BF16),
            pltpu.VMEM((2, 3, 256, KEYS), BF16),
            pltpu.VMEM((2, 3, KEYS, 256), BF16),
            pltpu.VMEM((2, WIDTH, KEYS), BF16),
            pltpu.VMEM((WT, 128), BF16),
            pltpu.VMEM((768, 768), BF16),
            pltpu.VMEM((2, 16, 768), F32),
            pltpu.VMEM((2, 16, 8, 768), F32),
            pltpu.VMEM((288, WIDTH), BF16),
            pltpu.VMEM((288, WIDTH), F32),
            pltpu.VMEM((2, WT, 128), F32),
            pltpu.VMEM((2, 2, WIDTH, KEYS), F32),
            pltpu.VMEM((288, 3 * WIDTH), BF16),
            pltpu.VMEM((2, 16, 768), F32),
            pltpu.VMEM((3, 2, PLANE, 48, 128), BF16),
            pltpu.VMEM((3, PLANE, 48, 128), BF16),
            pltpu.VMEM((3, PLANE, 48, 128), BF16),
            pltpu.VMEM((3, PLANE, 48, 128), BF16),
            pltpu.VMEM((2, 48, 128), BF16),
            pltpu.VMEM((48, 128), BF16),
            pltpu.VMEM((48, 128), BF16),
            pltpu.VMEM((2, PZ, 12, 128), F32),
            pltpu.VMEM((2, PZ, 12, 128), BF16),
            pltpu.VMEM((2, PZ, 12, 128), BF16),
            pltpu.VMEM((2, PZ, 12, 128), BF16),
            pltpu.VMEM((96, 128), F32),
            sems((2, 9)),
            sems((2, 3)),
            sems((2, 3)),
            sems((2, 2)),
            sems((2, 3 * PLANE)),
            sems((2, 2 * PZ)),
            sems((2, 2 * PZ)),
            sems((2, 4)),
            sems((2, 16)),
            sems((2, 16)),
            sems((2, 4)),
            sems((2, 8)),
            sems((13,)),
        ],
        compiler_params=pltpu.CompilerParams(
            collective_id=0, has_side_effects=True, vmem_limit_bytes=60 * 1024 * 1024
        ),
        name="step",
    )(*operands)


def small_row(e):
    quarter, k = e // 6, e % 6
    return quarter // 2, quarter % 2, 16 * (k // 4) + 12 + k % 4


def finish_kernel(
    grad_scale, full_b, full_c, gx, o_gx, o_wqkv, o_bqkv, o_wproj, o_bproj, o_gain, o_shift, o_pos, o_surf
):
    o_gx[...] = gx[...]

    def chunk(core, at):
        x, y = at % PX, at // PX
        return full_b.at[core, y, x], full_c.at[core, x, y]

    for n in range(2 * PLANE):
        b, c = chunk(n // PLANE, n % PLANE)
        for g in range(3):
            source = (b, b, c)[g]
            rows = (0, 48, 0)[g]
            part = source[rows : rows + 48, :].astype(F32) * grad_scale
            if n < 24:
                i, at = n // 3, WIDTH * (n % 3) + 128 * g
                o_wqkv[48 * i : 48 * i + 48, at : at + 128] = part
            else:
                at = 128 * g + 16 * (n - 24)
                for m in range(3):
                    o_wproj[at : at + 16, 128 * m : 128 * m + 128] = part[16 * m : 16 * m + 16, :]

    quarters = {}
    for core in range(2):
        for at in range(PLANE):
            x, y = at % PX, at // PX
            kind = (y * 2 + x // 2) * 2 + core
            rows = chunk(core, at)[1][48:96, :].astype(F32) * grad_scale
            key = core, x % 2
            quarters[key] = rows if key not in quarters else quarters[key] + rows
            for k in range(3):
                lo = 128 * (3 * (x % 2) + k)
                width = min(128, SLOTS - lo)
                for h in range(HEADS):
                    o_pos[16 * h + kind : 16 * h + kind + 1, lo : lo + width] = rows[
                        16 * k + h : 16 * k + h + 1, :width
                    ]

    def small(e):
        w, half, at = small_row(e)
        return quarters[w, half][at : at + 1, :]

    o_bqkv[...] = jnp.concatenate([small(n) for n in range(9)], 1).reshape(3 * WIDTH)
    for v, out in enumerate((o_bproj, o_gain, o_shift)):
        out[...] = jnp.concatenate([small(9 + 3 * v + m) for m in range(3)], 1).reshape(WIDTH)
    for a in range(4):
        side = small(18 + a)
        for b in range(4):
            o_surf[a, b : b + 1, :] = side[:, 12 * b : 12 * b + 12]


def finish(full_b, full_c, gx, grad_scale):
    one = lambda *shape: jax.ShapeDtypeStruct(shape, F32)
    return pl.pallas_call(
        functools.partial(finish_kernel, grad_scale),
        out_shape=(
            jax.ShapeDtypeStruct((6, 12, 4, WIDTH), BF16),
            one(WIDTH, 3 * WIDTH),
            one(3 * WIDTH),
            one(WIDTH, WIDTH),
            one(WIDTH),
            one(WIDTH),
            one(WIDTH),
            one(HEADS * 16, SLOTS),
            one(4, 4, HEADS),
        ),
        in_specs=[VMEM] * 3,
        out_specs=(VMEM,) * 9,
        compiler_params=pltpu.CompilerParams(vmem_limit_bytes=32 * 1024 * 1024),
        name="finish",
    )(full_b, full_c, gx)


def on_device(
    inputs, cotangent, land_sea, rel_index, norm_gain, norm_shift, w_qkv, b_qkv, w_proj, pos_bias, surf_bias
):
    levels, lat_rows, lon_cols, width = inputs.shape
    count = levels * lat_rows * lon_cols * lax.axis_size("lat") * lax.axis_size("lon")
    full_b, full_c, gx = step(
        inputs.transpose(1, 2, 0, 3),
        cotangent.transpose(1, 2, 0, 3),
        land_sea,
        rel_index,
        norm_gain,
        norm_shift,
        w_qkv,
        b_qkv,
        w_proj,
        pos_bias.transpose(1, 0, 2).reshape(-1, SLOTS),
        surf_bias.transpose(1, 2, 0),
    )
    outs = finish(full_b, full_c, gx, float(count) ** -0.5)
    g_x, g_wqkv, g_bqkv, g_wproj, g_bproj, g_gain, g_shift, g_pos, g_surf = outs
    return (
        g_x.transpose(2, 0, 1, 3),
        g_wqkv,
        g_bqkv,
        g_wproj,
        g_bproj,
        g_gain,
        g_shift,
        g_pos.reshape(HEADS, 16, SLOTS).transpose(1, 0, 2),
        g_surf.transpose(2, 0, 1),
    )


def solution(mesh):
    in_specs = (P(None, "lat", "lon", None), P(None, "lat", "lon", None), P("lat", "lon")) + (P(),) * 8
    out_specs = (P(None, "lat", "lon", None),) + (P(),) * 8
    return jax.shard_map(on_device, mesh=mesh, in_specs=in_specs, out_specs=out_specs, check_vma=False)
```

```python
import functools

import jax
import jax.numpy as jnp
from jax import lax
from jax.experimental import pallas as pl
from jax.experimental.pallas import tpu as pltpu
from jax.sharding import PartitionSpec as P

F32 = jnp.float32
BF16 = jnp.bfloat16
MESH = pl.DeviceIdType.MESH
EPS = 1e-05
LOG2E = 1.4426950408889634
BIG = 2.0**33
HEADS = 12
SLOTS = 759
WIDTH = 384
WT = 144
PITCH = 23
KEYS = 256
SCALE = 32.0**-0.5
NT = (((1,), (1,)), ((), ()))
TN = (((0,), (0,)), ((), ()))
NN = (((1,), (0,)), ((), ()))
PX, PY, PZ = 4, 4, 8
PLANE = PX * PY
VMEM = pl.BlockSpec(memory_space=pltpu.VMEM)


def dot(a, b, dims=NN):
    return lax.dot_general(a, b, dims, preferred_element_type=F32)


class Place:
    def __init__(self):
        lat, lon = lax.axis_index("lat"), lax.axis_index("lon")
        n_lat, n_lon = lax.axis_size("lat"), lax.axis_size("lon")
        self.lat, self.n_lat = lat, n_lat
        self.core = lax.rem(lon, 2)
        self.z = lax.rem(lon // 2, PZ)
        self.x = lax.rem(lat, 2) * 2 + lon // (2 * PZ)
        self.y = lat // 2
        self.here = self.y * PX + self.x
        up, down = lax.rem(lat + 1, n_lat), lax.rem(lat + n_lat - 1, n_lat)
        right, left = lax.rem(lon + 1, n_lon), lax.rem(lon + n_lon - 1, n_lon)
        self.north, self.south = (up, lon), (down, lon)
        self.east, self.west = (lat, right), (lat, left)
        self.north_east, self.south_west = (up, right), (down, left)
        self.sibling = (lat, lon + 1 - 2 * self.core)
        self.x_pair = self.device(self.x + 1 - 2 * lax.rem(self.x, 2), self.y, self.z, self.core)

    def device(self, x, y, z, core):
        return (y * 2 + x // 2, (lax.rem(x, 2) * PZ + z) * 2 + core)

    def in_plane(self, step, sign):
        x = lax.rem(self.x + PX + sign * (step % PX), PX)
        y = lax.rem(self.y + PY + sign * (step // PX), PY)
        return x, y, y * PX + x

    def greet(self):
        others = [self.north, self.south, self.east, self.west, self.north_east, self.south_west, self.sibling]
        for step in range(1, PLANE):
            x, y, _ = self.in_plane(step, -1)
            others.append(self.device(x, y, self.z, self.core))
        for step in range(1, PZ):
            others.append(self.device(self.x, self.y, lax.rem(self.z + PZ - step, PZ), self.core))
        for other in others:
            pl.semaphore_signal(pltpu.get_barrier_semaphore(), inc=1, device_id=other, device_id_type=MESH)
        self.greeted = len(others)

    def meet(self):
        pl.semaphore_wait(pltpu.get_barrier_semaphore(), self.greeted)


def send(src, dst, sems, k, to):
    copy = pltpu.make_async_remote_copy(
        src_ref=src,
        dst_ref=dst,
        send_sem=sems.at[0, k],
        recv_sem=sems.at[1, k],
        device_id=to,
        device_id_type=MESH,
    )
    copy.start()
    return copy


def key_of(token):
    level, cell = token // 72, lax.rem(token, 72)
    return 128 * level + cell + (PITCH - 12) * (cell // 12)


def plain_rows():
    rows = lax.broadcasted_iota(jnp.int32, (72, 128), 0)
    return rows + (PITCH - 12) * (rows // 12)


def skew_parts(rows):
    lane = lax.broadcasted_iota(jnp.int32, (72, 128), 1)
    first = lane + rows >= PITCH * 5 + 11
    there = jnp.bitwise_and(lane - rows - 2, 127)
    back = jnp.bitwise_and(lane + rows + 2, 127)
    return first, there, back


def skew(table, first, there):
    mixed = jnp.where(first, table[:, :128], table[:, 128:])
    return jnp.take_along_axis(mixed, there, axis=1)


def split(values, count):
    pieces = []
    for _ in range(count):
        piece = values.astype(BF16)
        pieces.append(piece)
        values = values - piece.astype(F32)
    return pieces


def step_kernel(
    x_in, dy_in, land_in, rel_in, gain_in, shift_in, w_qkv_in, b_qkv_in, w_proj_in, pos_in, surf_in,
    full_b, full_c, gx_out,
    land, rel, gain, shift, w_qkv, b_qkv, w_proj, pos, surf, c_spread, c_back, w_qkv_t, w_proj_t, onehot_t, bias_0, bias_1,
    tok_x, tok_dy, cls_out, cls_in, side_in, tp, tp_low, gx,
    mixed, white, inv_std, normed, normed_t, dy_low, qkv, dctx, turned, k_cat, k_cat_t, v_cat, v_turned, q_feat,
    onehot, tables, d_tables, ctx_acc, dq_acc, f_acc, dkv_t, low, table_in,
    wp, c_recv, p_send, p_recv, tc_recv, t_send, t_recv, z_own, z_send, z_recv, z_full, z_cat,
    f_sems, h_sems, c_sems, t_sems, p_sems, z_sems, a_sems, bx_sems, by_sems, cx_sems, cy_sems, k_sems, local,
):
    place = Place()
    core, x, y, z, here = place.core, place.x, place.y, place.z, place.here
    place.greet()
    fetches = [
        pltpu.make_async_copy(a, b, local.at[4 + k])
        for k, (a, b) in enumerate(
            (
                (land_in, land), (pos_in, pos), (rel_in, rel), (w_qkv_in, w_qkv), (w_proj_in, w_proj),
                (gain_in, gain), (shift_in, shift), (b_qkv_in, b_qkv), (surf_in, surf),
            )
        )
    ]
    for copy in fetches:
        copy.start()

    cls_out[...] = jnp.zeros_like(cls_out)
    fetches[0].wait()
    for q in range(4):
        cls_out[q, :3, :6] = land[3 * (q // 2) : 3 * (q // 2) + 3, 6 * (q % 2) : 6 * (q % 2) + 6].astype(F32)

    def quadrant(ref, q):
        return ref.at[pl.ds(3 * (q // 2), 3), pl.ds(6 * (q % 2), 6)]

    place.meet()
    routes = ((0, place.south_west), (1, place.south), (2, place.west))
    halo_x = [send(quadrant(x_in, q), quadrant(tok_x, 3 - q), f_sems, q, to) for q, to in routes]
    halo_x += [send(cls_out.at[q], cls_in.at[3 - q], f_sems, 3 + q, to) for q, to in routes]
    halo_dy = [send(quadrant(dy_in, q), quadrant(tok_dy, 3 - q), f_sems, 6 + q, to) for q, to in routes]
    own_x = pltpu.make_async_copy(quadrant(x_in, 3), quadrant(tok_x, 0), local.at[0])
    own_dy = pltpu.make_async_copy(quadrant(dy_in, 3), quadrant(tok_dy, 0), local.at[1])
    own_cls = pltpu.make_async_copy(cls_out.at[3], cls_in.at[0], local.at[2])
    for copy in (own_x, own_dy, own_cls):
        copy.start()

    lat = place.lat
    last_band = lat == place.n_lat - 1
    for copy in fetches[1:]:
        copy.wait()
    key_at = lax.broadcasted_iota(jnp.int32, (KEYS, WT), 0)
    c_spread[...] = jnp.where(key_at == key_of(lax.broadcasted_iota(jnp.int32, (KEYS, WT), 1)), 1.0, 0.0).astype(BF16)
    key_at = lax.broadcasted_iota(jnp.int32, (WT, KEYS), 1)
    c_back[...] = jnp.where(key_at == key_of(lax.broadcasted_iota(jnp.int32, (WT, KEYS), 0)), 1.0, 0.0).astype(BF16)
    rel_now = rel[...]
    rel_low = jnp.bitwise_and(rel_now, 15)
    rel_wide = dot((rel_now - rel_low).astype(F32).astype(BF16), c_spread[...], NT) + dot(
        rel_low.astype(F32).astype(BF16), c_spread[...], NT
    )
    rel_lane = jnp.bitwise_and(lax.broadcasted_iota(jnp.int32, (WT, KEYS), 1), 127)
    rel_wide = jnp.where(lax.rem(rel_lane, PITCH) < 12, rel_wide, -1.0)
    first, _, back = skew_parts(plain_rows())
    slot = lax.broadcasted_iota(jnp.int32, (768, 128), 0).astype(F32)
    for b, block in enumerate((rel_wide[:72, :128], rel_wide[:72, 128:], rel_wide[72:, :128])):
        turned_back = jnp.take_along_axis(block, back, axis=1)
        for half in range(2):
            kept = jnp.where(first, turned_back, -1.0) if half == 0 else jnp.where(first, -1.0, turned_back)
            slots = jnp.max(kept, 0, keepdims=True)
            lanes = slice(b * 256 + half * 128, b * 256 + half * 128 + 128)
            onehot[:, lanes] = jnp.where(slot == slots, 1.0, 0.0).astype(BF16)
    table_in[...] = jnp.zeros_like(table_in)
    for w in range(2):
        for h in range(HEADS):
            table_in[w, h : h + 1, :SLOTS] = pos[pl.ds(16 * h + 2 * lat + w, 1), :] * LOG2E
        tables[w] = functools.reduce(jnp.add, [dot(part, onehot[...]) for part in split(table_in[w], 3)])

    first, there, back = skew_parts(plain_rows())
    for h in range(HEADS):
        table = tables[0, h : h + 1, :]
        for b in range(3):
            block = skew(table[:, 256 * b : 256 * b + 256], first, there)
            if b == 0:
                bias_0[h, :72, :128] = block
                bias_0[h, 72:, 128:] = block
            elif b == 1:
                bias_0[h, :72, 128:] = block
            else:
                bias_0[h, 72:, :128] = block
        bias_1[h] = skew(tables[1, h : h + 1, :256], first, there)
    for w in range(2):
        for g in range(3):
            v_cat[w, g, :, 128:] = jnp.ones((KEYS, 128), BF16)
    d_tables[...] = jnp.zeros_like(d_tables)
    f_acc[...] = jnp.zeros_like(f_acc)
    side_in[...] = jnp.zeros_like(side_in)
    for a in range(4):
        for b in range(4):
            side_in[a : a + 1, 12 * b : 12 * b + 12] = surf[a, b : b + 1, :]
            side_in[a : a + 1, 48 + 12 * b : 60 + 12 * b] = surf[a, b : b + 1, :]
    block_row = jnp.bitwise_and(lax.broadcasted_iota(jnp.int32, (256, 512), 0), 127)
    block_lane = lax.broadcasted_iota(jnp.int32, (256, 512), 1)
    blocks_of_ones = jnp.where(block_row // 32 == block_lane // 128, 1.0, 0.0).astype(BF16)
    onehot_t[...] = onehot[...].T
    w_qkv_t[...] = w_qkv[...].T
    w_proj_t[...] = w_proj[...].T

    eye = (
        lax.broadcasted_iota(jnp.int32, (WIDTH, WIDTH), 0) == lax.broadcasted_iota(jnp.int32, (WIDTH, WIDTH), 1)
    ).astype(F32).astype(BF16)
    strided = mixed.reshape(3 * 576, 128)

    def in_order(tok, first_row, out):
        for j in range(3):
            cols = slice(128 * j, 128 * j + 128)
            mixed[j, :, first_row : first_row + 4, :] = tok[:, :, :, cols].reshape(72, 4, 128).astype(F32)
        for k in range(4):
            level = (1, 2, 3, 0)[k]
            for j in range(3):
                out[72 * k : 72 * k + 72, 128 * j : 128 * j + 128] = strided[
                    pl.ds(576 * j + first_row + level, 72, stride=8), :
                ]

    for copy in halo_x + [own_x, own_cls]:
        copy.wait()
    in_order(tok_x, 0, white)
    tokens = white[...]
    centred = tokens - jnp.mean(tokens, -1, keepdims=True)
    inv = lax.rsqrt(jnp.mean(centred * centred, -1, keepdims=True) + EPS)
    inv_std[...] = inv
    whitened = centred * inv
    white[...] = whitened
    gain_row = gain[...].reshape(1, WIDTH)
    normed[...] = (whitened * gain_row + shift[...].reshape(1, WIDTH)).astype(BF16)
    qkv[...] = (dot(normed[...], w_qkv[...]) + b_qkv[...].reshape(1, 3 * WIDTH)).astype(BF16)
    normed_t[...] = dot(eye, normed[...], NT).astype(BF16)
    for w in range(2):
        rows = slice(w * WT, (w + 1) * WT)
        turned[w, 0] = dot(eye, qkv[rows, :WIDTH], NT).astype(BF16)
        padded = dot(c_spread[...], qkv[rows, WIDTH:]).astype(BF16)
        k_turned = dot(eye, padded[:, :WIDTH], NT).astype(BF16)
        v_turned[w] = dot(eye, padded[:, WIDTH:], NT).astype(BF16)
        for g in range(3):
            lanes = slice(128 * g, 128 * g + 128)
            k_cat[w, g, :, :128] = padded[:, lanes]
            k_cat_t[w, g, :128, :] = k_turned[lanes, :]
            v_cat[w, g, :, :128] = padded[:, WIDTH + 128 * g : WIDTH + 128 * g + 128]

    lane = lax.broadcasted_iota(jnp.int32, (WT, 128), 1)
    token = lax.broadcasted_iota(jnp.int32, (WT, 128), 0)
    cell = lax.rem(token, 72)
    cell_row, cell_col = cell // 12, lax.rem(cell, 12)
    in_quad = 8 * (2 * (cell_row // 3) + cell_col // 6) + lax.rem(cell_row, 3)
    pick_row = jnp.where(lane == in_quad, 1.0, 0.0).astype(BF16)[:, :32]
    pick_col = jnp.where(lane == lax.rem(cell_col, 6), 1.0, 0.0)
    cells = dot(pick_row, cls_in[...].reshape(32, 128).astype(BF16)) * pick_col
    kind = dot(cells.astype(BF16), jnp.ones((128, 128), BF16)).astype(jnp.int32)
    turned_over = jnp.logical_and(lax.rem(token, 72) >= 36, last_band).astype(F32)
    of_key = jnp.where(kind == lax.rem(lane, 48) // 12, 1.0, 0.0)
    of_query = jnp.where(kind == lane, 1.0, 0.0).astype(BF16)
    surf_lane = lax.broadcasted_iota(jnp.int32, (128, 128), 1)
    surf_hi, surf_lo = split(side_in[...] * (1.0 / SCALE), 2)
    side = dot(of_query, jnp.where(surf_lane < 48, surf_hi.astype(F32), surf_lo.astype(F32)).astype(BF16))
    q_feat[...] = jnp.where(
        lane < 96, side, jnp.where(lane == 96, turned_over, jnp.where(lane == 97, 1.0 - turned_over, 0.0))
    ).astype(BF16)
    key_side = jnp.where(
        lane < 96,
        of_key,
        jnp.where(lane == 96, -BIG * (1.0 - turned_over), jnp.where(lane == 97, -BIG * turned_over, 0.0)),
    ).astype(BF16)
    key_lane = lax.broadcasted_iota(jnp.int32, (KEYS, 128), 1)
    key_row = jnp.bitwise_and(lax.broadcasted_iota(jnp.int32, (KEYS, 128), 0), 127)
    hidden = jnp.logical_and(lax.rem(key_row, PITCH) >= 12, jnp.logical_and(key_lane >= 96, key_lane < 98))
    k_feat = jnp.where(hidden, -BIG, dot(c_spread[...], key_side)).astype(BF16)
    k_feat_t = dot(eye[:128, :128], k_feat, NT).astype(BF16)
    for w in range(2):
        for g in range(3):
            k_cat[w, g, :, 128:] = k_feat
            k_cat_t[w, g, 128:, :] = k_feat_t

    for copy in halo_dy + [own_dy]:
        copy.wait()
    in_order(tok_dy, 4, dq_acc)
    dy_low[...] = dq_acc[...].astype(BF16)
    dctx[...] = dot(dy_low[...], w_proj_t[...]).astype(BF16)
    for w in range(2):
        turned[w, 1] = dot(eye, dctx[w * WT : (w + 1) * WT, :], NT).astype(BF16)

    zero = jnp.zeros((72, 128), F32)
    cat_lane = lax.broadcasted_iota(jnp.int32, (1, 256), 1)
    half_lane = lax.broadcasted_iota(jnp.int32, (1, 128), 1)
    def own_level(a):
        return jnp.concatenate([a[:72, :128], a[72:, 128:]], 0)

    def both_levels(a):
        top = jnp.concatenate([a[:72], zero], 1)
        return jnp.concatenate([top, jnp.concatenate([zero, a[72:]], 1)], 0)

    def group_step(g, between=lambda: None):
        lanes = slice(g * 128, g * 128 + 128)
        for w in range(2):
            rows = slice(w * WT, (w + 1) * WT)
            part = [slice(WT * hh, WT * hh + WT) for hh in range(4)]
            q_cat = jnp.concatenate([qkv[rows, lanes], q_feat[...]], 1)
            dctx_now = dctx[rows, lanes]
            q_all, dctx_all = [], []
            for hh in range(4):
                mine = cat_lane // 32 == hh
                feat_mine = jnp.logical_and(
                    cat_lane >= 128, jnp.logical_or(cat_lane >= 224, lax.rem(cat_lane + 4, 12) == g * 4 + hh)
                )
                keep = jnp.logical_or(mine, feat_mine).astype(F32).astype(BF16)
                q_all.append(q_cat * keep)
                dctx_all.append(dctx_now * keep[:, :128])
            raw_all = dot(jnp.concatenate(q_all, 0), k_cat_t[w, g])
            d_raw_all = dot(jnp.concatenate(dctx_all, 0), v_turned[w, lanes, :])
            powers = []
            for hh in range(4):
                head = g * 4 + hh
                raw = raw_all[part[hh]]
                if w == 0:
                    bias = bias_0[head]
                else:
                    raw = own_level(raw)
                    bias = jnp.concatenate([bias_1[head], bias_1[head]], 0)
                score = raw * (SCALE * LOG2E) + bias
                powers.append(jnp.exp2(score - jnp.max(score, -1, keepdims=True)))
            wide = [a if w == 0 else both_levels(a) for a in powers]
            mixed_all = dot(jnp.concatenate([a.astype(BF16) for a in wide], 0), v_cat[w, g])
            inverse, context = [], jnp.zeros((WT, 128), F32)
            for hh in range(4):
                inverse.append(1.0 / mixed_all[part[hh], 128:])
                context = jnp.where(half_lane // 32 == hh, mixed_all[part[hh], :128] * inverse[hh], context)
            ctx_acc[rows, lanes] = context.astype(BF16)
            shares = jnp.concatenate(split(dctx_now.astype(F32) * context, 2), 1)
            deltas = dot(shares, blocks_of_ones)
            score_lows = []
            for hh in range(4):
                head = g * 4 + hh
                d_raw, delta = d_raw_all[part[hh]], deltas[:, 128 * hh : 128 * hh + 128]
                if w == 0:
                    double = lambda a: jnp.concatenate([a, a], 1)
                    probs = powers[hh] * double(inverse[hh])
                    d_score = probs * (d_raw - double(delta))
                    blocks = (d_score[:72, :128] + d_score[72:, 128:], d_score[:72, 128:], d_score[72:, :128])
                    probs_low, score_low = probs.astype(BF16), d_score.astype(BF16)
                else:
                    probs = powers[hh] * inverse[hh]
                    d_score = probs * (own_level(d_raw) - delta)
                    blocks = (d_score[:72] + d_score[72:],)
                    probs_low, score_low = both_levels(probs).astype(BF16), both_levels(d_score).astype(BF16)
                score_lows.append(score_low)
                head_rows = slice(head * 32, head * 32 + 32)
                dkv_t[w, 0, head_rows, :] = dot(turned[w, 0, head_rows, :], score_low) * SCALE
                dkv_t[w, 1, head_rows, :] = dot(turned[w, 1, head_rows, :], probs_low)
                for b, block in enumerate(blocks):
                    turned_back = jnp.take_along_axis(block, back, axis=1)
                    early = jnp.where(first, turned_back, 0.0)
                    late = turned_back - early
                    d_tables[w, head, :, b * 256 : b * 256 + 128] = jnp.sum(early.reshape(9, 8, 128), 0)
                    d_tables[w, head, :, b * 256 + 128 : b * 256 + 256] = jnp.sum(late.reshape(9, 8, 128), 0)
            both_all = dot(jnp.concatenate(score_lows, 0), k_cat[w, g])
            dq, feats = jnp.zeros((WT, 128), F32), f_acc[w]
            for hh in range(4):
                dq = jnp.where(half_lane // 32 == hh, both_all[part[hh], :128], dq)
                feats = jnp.where(lax.rem(half_lane, 12) == g * 4 + hh, both_all[part[hh], 128:], feats)
            dq_acc[rows, lanes] = dq * SCALE
            f_acc[w] = feats
            if w == 0:
                between()

    sums = {}

    def weight_grads(g):
        lanes = slice(128 * g, 128 * g + 128)
        dq = dq_acc[:, lanes]
        low[:, lanes] = dq.astype(BF16)
        sums[0, g] = jnp.sum(dq, 0, keepdims=True)
        for part in range(2):
            total = jnp.zeros((1, 128), F32)
            for w in range(2):
                rows_now = dot(c_back[...], dkv_t[w, part, lanes, :].astype(BF16), NT)
                total += jnp.sum(rows_now, 0, keepdims=True)
                at = WIDTH * (part + 1) + 128 * g
                low[w * WT : (w + 1) * WT, at : at + 128] = rows_now.astype(BF16)
            sums[part + 1, g] = total
        for part in range(3):
            at = WIDTH * part + 128 * g
            grad = dot(normed_t[...], low[:, at : at + 128])
            for i in range(8):
                n = 3 * i + part
                wp[g, n // PLANE, n % PLANE] = grad[48 * i : 48 * i + 48, :].astype(BF16)
        grad = dot(ctx_acc[:, lanes], dy_low[...], TN)
        for u in range(8):
            n = 24 + u
            for m in range(3):
                wp[g, n // PLANE, n % PLANE, 16 * m : 16 * m + 16, :] = grad[
                    16 * u : 16 * u + 16, 128 * m : 128 * m + 128
                ].astype(BF16)
        return send(wp.at[g, 1 - core], c_recv.at[g], c_sems, g, place.sibling)

    def plane_sends(g, core_copy):
        core_copy.wait()
        copies = []
        for step in range(1, PLANE):
            x_at, y_at, at = place.in_plane(step, 1)
            p_send[g, step] = (wp[g, core, at].astype(F32) + c_recv[g, at].astype(F32)).astype(BF16)
            copies.append(
                send(
                    p_send.at[g, step], p_recv.at[g, step], p_sems, g * PLANE + step, place.device(x_at, y_at, z, core)
                )
            )
        return copies

    plane_copies = []
    group_step(0)
    core_copies = [weight_grads(0)]
    group_step(1)
    plane_copies.append(plane_sends(0, core_copies[0]))
    core_copies.append(weight_grads(1))
    group_step(2)
    plane_copies.append(plane_sends(1, core_copies[1]))
    core_copies.append(weight_grads(2))

    d_normed = dot(low[...], w_qkv_t[...]).astype(BF16).astype(F32)

    plane_copies.append(plane_sends(2, core_copies[2]))

    stacked = [part for w in range(2) for part in split(jnp.sum(d_tables[w], 1), 2)]
    by_slot = dot(jnp.concatenate(stacked, 0), onehot_t[...])
    for w in range(2):
        table = by_slot[32 * w : 32 * w + 16] + by_slot[32 * w + 16 : 32 * w + 32]
        for half in range(2):
            for k in range(3):
                at = 128 * (3 * half + k)
                tp[w, half, 16 * k : 16 * k + 16, :] = table[:, at : at + 128]
    small = [sums[part, g] for part in range(3) for g in range(3)]
    for total in (
        jnp.sum(dy_low[...].astype(F32), 0, keepdims=True),
        jnp.sum(d_normed * white[...], 0, keepdims=True),
        jnp.sum(d_normed, 0, keepdims=True),
    ):
        small += [total[:, 128 * m : 128 * m + 128] for m in range(3)]
    d_surf = functools.reduce(jnp.add, [dot(of_query, part, TN) for part in split(f_acc[0] + f_acc[1], 2)])
    small += [d_surf[a : a + 1, :] for a in range(4)]
    for e, row in enumerate(small):
        w, half, at = small_row(e)
        tp[w, half, at : at + 1, :] = row
    tp_low[...] = tp[...].astype(BF16)
    t_copy = send(tp_low.at[1 - core], tc_recv, t_sems, 0, place.sibling)

    scaled = d_normed * gain_row
    first_mean = jnp.mean(scaled, -1, keepdims=True)
    second_mean = jnp.mean(scaled * white[...], -1, keepdims=True)
    dq_acc[...] = dy_low[...].astype(F32) + inv_std[...] * (scaled - first_mean - white[...] * second_mean)
    for j in range(3):
        cols = slice(128 * j, 128 * j + 128)
        for k in range(4):
            level = (1, 2, 3, 0)[k]
            strided[pl.ds(576 * j + level, 72, stride=8), :] = dq_acc[72 * k : 72 * k + 72, cols]
        gx[:, :, :, cols] = mixed[j, :, 0:4, :].astype(BF16).reshape(6, 12, 4, 128)

    def plane_total(g):
        total = wp[g, core, here].astype(F32) + c_recv[g, here].astype(F32)
        for step in range(1, PLANE):
            plane_copies[g][step - 1].wait()
            total = total + p_recv[g, step].astype(F32)
        return total

    def along_z(src, dst, sems, s):
        return [
            send(src(step), dst(step), sems, PZ * s + step, place.device(x, y, lax.rem(z + step, PZ), core))
            for step in (4, 3, 5, 2, 6, 1, 7)
        ]

    def z_sum(s, upper, lower):
        for k in range(PZ):
            piece = (upper, lower)[k // 4][12 * (k % 4) : 12 * (k % 4) + 12, :]
            z_own[s, k] = piece
            z_send[s, k] = piece.astype(BF16)
        return along_z(lambda step: z_send.at[s, lax.rem(z + step, PZ)], lambda step: z_recv.at[s, step], z_sems, s)

    def z_share(s, copies):
        for copy in copies:
            copy.wait()
        summed = z_own[s, z]
        for step in range(1, PZ):
            summed = summed + z_recv[s, step].astype(F32)
        z_full[s, z] = summed.astype(BF16)
        return along_z(lambda step: z_full.at[s, z], lambda step: z_full.at[s, z], a_sems, s)

    def z_join(s, copies):
        for copy in copies:
            copy.wait()
        for k in range(PZ):
            z_cat[12 * k : 12 * k + 12, :] = z_full[s, k].astype(F32)
        return z_cat[...].astype(BF16)

    t_mine = lax.rem(x, 2)
    total_0 = plane_total(0)
    t_copy.wait()
    t_send[...] = (tp[core, 1 - t_mine] + tc_recv[1 - t_mine].astype(F32)).astype(BF16)
    tx_copy = send(t_send, t_recv, t_sems, 1, place.x_pair)
    t_total = tp[core, t_mine] + tc_recv[t_mine].astype(F32)
    early = z_sum(0, total_0, plane_total(1))
    total_2 = plane_total(2)
    tx_copy.wait()
    late = z_sum(1, total_2, t_total + t_recv[...].astype(F32))
    early = z_share(0, early)
    home = [
        send(quadrant(gx, q), quadrant(gx_out, 3 - q), h_sems, q - 1, to)
        for q, to in ((1, place.east), (2, place.north), (3, place.north_east))
    ]
    own_gx = pltpu.make_async_copy(quadrant(gx, 0), quadrant(gx_out, 3), local.at[3])
    own_gx.start()
    late = z_share(1, late)

    def x_away(step):
        return place.device(lax.rem(x + step, PX), y, z, core)

    def y_away(step):
        return place.device(x, lax.rem(y + step, PY), z, core)

    b_first, c_first, b_then, c_then, last = {}, {}, {}, {}, []
    full_b[core, y, x] = z_join(0, early)
    for d in (2, 1, 3):
        b_first[d] = send(full_b.at[core, y, x], full_b.at[core, y, x], bx_sems, d, x_away(d))
    for d in (2, 1, 3):
        b_then[0, d] = send(full_b.at[core, y, x], full_b.at[core, y, x], by_sems, d, y_away(d))
    full_c[core, x, y] = z_join(1, late)
    for d in (2, 1, 3):
        c_first[d] = send(full_c.at[core, x, y], full_c.at[core, x, y], cy_sems, d, y_away(d))
    for d in (2, 1, 3):
        c_then[0, d] = send(full_c.at[core, x, y], full_c.at[core, x, y], cx_sems, d, x_away(d))
    for e in (1, 3, 2):
        x_from = lax.rem(x + PX - e, PX)
        b_first[e].wait()
        for d in (2, 1, 3):
            b_then[e, d] = send(full_b.at[core, y, x_from], full_b.at[core, y, x_from], by_sems, 4 * e + d, y_away(d))
    last.append(send(full_b.at[core, y], full_b.at[core, y], k_sems, 0, place.sibling))
    for e in (1, 3, 2):
        y_from = lax.rem(y + PY - e, PY)
        c_first[e].wait()
        for d in (2, 1, 3):
            c_then[e, d] = send(full_c.at[core, x, y_from], full_c.at[core, x, y_from], cx_sems, 4 * e + d, x_away(d))
    last.append(send(full_c.at[core, x], full_c.at[core, x], k_sems, 4, place.sibling))
    for d in (1, 3, 2):
        y_from = lax.rem(y + PY - d, PY)
        for e in range(4):
            b_then[e, d].wait()
        last.append(send(full_b.at[core, y_from], full_b.at[core, y_from], k_sems, d, place.sibling))
    for d in (1, 3, 2):
        x_from = lax.rem(x + PX - d, PX)
        for e in range(4):
            c_then[e, d].wait()
        last.append(send(full_c.at[core, x_from], full_c.at[core, x_from], k_sems, 4 + d, place.sibling))
    for copy in last + home:
        copy.wait()
    own_gx.wait()


def step(*operands):
    sems = pltpu.SemaphoreType.DMA
    anywhere = pl.BlockSpec(memory_space=pl.ANY)
    in_specs = [anywhere] * len(operands)
    return pl.pallas_call(
        step_kernel,
        out_shape=(
            pltpu.VMEM((2, PY, PX, 96, 128), BF16),
            pltpu.VMEM((2, PX, PY, 96, 128), BF16),
            pltpu.VMEM((6, 12, 4, WIDTH), BF16),
        ),
        in_specs=in_specs,
        out_specs=(VMEM, VMEM, VMEM),
        scratch_shapes=[
            pltpu.VMEM((6, 12), jnp.int32),
            pltpu.VMEM((WT, WT), jnp.int32),
            pltpu.VMEM((WIDTH,), F32),
            pltpu.VMEM((WIDTH,), F32),
            pltpu.VMEM((WIDTH, 3 * WIDTH), BF16),
            pltpu.VMEM((3 * WIDTH,), F32),
            pltpu.VMEM((WIDTH, WIDTH), BF16),
            pltpu.VMEM((HEADS * 16, SLOTS), F32),
            pltpu.VMEM((4, 4, HEADS), F32),
            pltpu.VMEM((KEYS, WT), BF16),
            pltpu.VMEM((WT, KEYS), BF16),
            pltpu.VMEM((3 * WIDTH, WIDTH), BF16),
            pltpu.VMEM((WIDTH, WIDTH), BF16),
            pltpu.VMEM((768, 768), BF16),
            pltpu.VMEM((HEADS, WT, KEYS), F32),
            pltpu.VMEM((HEADS, 72, 128), F32),
            pltpu.VMEM((6, 12, 4, WIDTH), BF16),
            pltpu.VMEM((6, 12, 4, WIDTH), BF16),
            pltpu.VMEM((4, 8, 128), F32),
            pltpu.VMEM((4, 8, 128), F32),
            pltpu.VMEM((128, 128), F32),
            pltpu.VMEM((2, 2, 48, 128), F32),
            pltpu.VMEM((2, 2, 48, 128), BF16),
            pltpu.VMEM((6, 12, 4, WIDTH), BF16),
            pltpu.VMEM((3, 72, 8, 128), F32),
            pltpu.VMEM((288, WIDTH), F32),
            pltpu.VMEM((288, 1), F32),
            pltpu.VMEM((288, WIDTH), BF16),
            pltpu.VMEM((WIDTH, 288), BF16),
            pltpu.VMEM((288, WIDTH), BF16),
            pltpu.VMEM((288, 3 * WIDTH), BF16),
            pltpu.VMEM((288, WIDTH), BF16),
            pltpu.VMEM((2, 2, WIDTH, WT), BF16),
            pltpu.VMEM((2, 3, KEYS, 256), BF16),
            pltpu.VMEM((2, 3, 256, KEYS), BF16),
            pltpu.VMEM((2, 3, KEYS, 256), BF16),
            pltpu.VMEM((2, WIDTH, KEYS), BF16),
            pltpu.VMEM((WT, 128), BF16),
            pltpu.VMEM((768, 768), BF16),
            pltpu.VMEM((2, 16, 768), F32),
            pltpu.VMEM((2, 16, 8, 768), F32),
            pltpu.VMEM((288, WIDTH), BF16),
            pltpu.VMEM((288, WIDTH), F32),
            pltpu.VMEM((2, WT, 128), F32),
            pltpu.VMEM((2, 2, WIDTH, KEYS), F32),
            pltpu.VMEM((288, 3 * WIDTH), BF16),
            pltpu.VMEM((2, 16, 768), F32),
            pltpu.VMEM((3, 2, PLANE, 48, 128), BF16),
            pltpu.VMEM((3, PLANE, 48, 128), BF16),
            pltpu.VMEM((3, PLANE, 48, 128), BF16),
            pltpu.VMEM((3, PLANE, 48, 128), BF16),
            pltpu.VMEM((2, 48, 128), BF16),
            pltpu.VMEM((48, 128), BF16),
            pltpu.VMEM((48, 128), BF16),
            pltpu.VMEM((2, PZ, 12, 128), F32),
            pltpu.VMEM((2, PZ, 12, 128), BF16),
            pltpu.VMEM((2, PZ, 12, 128), BF16),
            pltpu.VMEM((2, PZ, 12, 128), BF16),
            pltpu.VMEM((96, 128), F32),
            sems((2, 9)),
            sems((2, 3)),
            sems((2, 3)),
            sems((2, 2)),
            sems((2, 3 * PLANE)),
            sems((2, 2 * PZ)),
            sems((2, 2 * PZ)),
            sems((2, 4)),
            sems((2, 16)),
            sems((2, 16)),
            sems((2, 4)),
            sems((2, 8)),
            sems((13,)),
        ],
        compiler_params=pltpu.CompilerParams(
            collective_id=0, has_side_effects=True, vmem_limit_bytes=60 * 1024 * 1024
        ),
        name="step",
    )(*operands)


def small_row(e):
    quarter, k = e // 6, e % 6
    return quarter // 2, quarter % 2, 16 * (k // 4) + 12 + k % 4


def finish_kernel(
    grad_scale, full_b, full_c, gx, o_gx, o_wqkv, o_bqkv, o_wproj, o_bproj, o_gain, o_shift, o_pos, o_surf
):
    o_gx[...] = gx[...]

    def chunk(core, at):
        x, y = at % PX, at // PX
        return full_b.at[core, y, x], full_c.at[core, x, y]

    for n in range(2 * PLANE):
        b, c = chunk(n // PLANE, n % PLANE)
        for g in range(3):
            source = (b, b, c)[g]
            rows = (0, 48, 0)[g]
            part = source[rows : rows + 48, :].astype(F32) * grad_scale
            if n < 24:
                i, at = n // 3, WIDTH * (n % 3) + 128 * g
                o_wqkv[48 * i : 48 * i + 48, at : at + 128] = part
            else:
                at = 128 * g + 16 * (n - 24)
                for m in range(3):
                    o_wproj[at : at + 16, 128 * m : 128 * m + 128] = part[16 * m : 16 * m + 16, :]

    quarters = {}
    for core in range(2):
        for at in range(PLANE):
            x, y = at % PX, at // PX
            kind = (y * 2 + x // 2) * 2 + core
            rows = chunk(core, at)[1][48:96, :].astype(F32) * grad_scale
            key = core, x % 2
            quarters[key] = rows if key not in quarters else quarters[key] + rows
            for k in range(3):
                lo = 128 * (3 * (x % 2) + k)
                width = min(128, SLOTS - lo)
                for h in range(HEADS):
                    o_pos[16 * h + kind : 16 * h + kind + 1, lo : lo + width] = rows[
                        16 * k + h : 16 * k + h + 1, :width
                    ]

    def small(e):
        w, half, at = small_row(e)
        return quarters[w, half][at : at + 1, :]

    o_bqkv[...] = jnp.concatenate([small(n) for n in range(9)], 1).reshape(3 * WIDTH)
    for v, out in enumerate((o_bproj, o_gain, o_shift)):
        out[...] = jnp.concatenate([small(9 + 3 * v + m) for m in range(3)], 1).reshape(WIDTH)
    for a in range(4):
        side = small(18 + a)
        for b in range(4):
            o_surf[a, b : b + 1, :] = side[:, 12 * b : 12 * b + 12]


def finish(full_b, full_c, gx, grad_scale):
    one = lambda *shape: jax.ShapeDtypeStruct(shape, F32)
    return pl.pallas_call(
        functools.partial(finish_kernel, grad_scale),
        out_shape=(
            jax.ShapeDtypeStruct((6, 12, 4, WIDTH), BF16),
            one(WIDTH, 3 * WIDTH),
            one(3 * WIDTH),
            one(WIDTH, WIDTH),
            one(WIDTH),
            one(WIDTH),
            one(WIDTH),
            one(HEADS * 16, SLOTS),
            one(4, 4, HEADS),
        ),
        in_specs=[VMEM] * 3,
        out_specs=(VMEM,) * 9,
        compiler_params=pltpu.CompilerParams(vmem_limit_bytes=32 * 1024 * 1024),
        name="finish",
    )(full_b, full_c, gx)


def on_device(
    inputs, cotangent, land_sea, rel_index, norm_gain, norm_shift, w_qkv, b_qkv, w_proj, pos_bias, surf_bias
):
    levels, lat_rows, lon_cols, width = inputs.shape
    count = levels * lat_rows * lon_cols * lax.axis_size("lat") * lax.axis_size("lon")
    full_b, full_c, gx = step(
        inputs.transpose(1, 2, 0, 3),
        cotangent.transpose(1, 2, 0, 3),
        land_sea,
        rel_index,
        norm_gain,
        norm_shift,
        w_qkv,
        b_qkv,
        w_proj,
        pos_bias.transpose(1, 0, 2).reshape(-1, SLOTS),
        surf_bias.transpose(1, 2, 0),
    )
    outs = finish(full_b, full_c, gx, float(count) ** -0.5)
    g_x, g_wqkv, g_bqkv, g_wproj, g_bproj, g_gain, g_shift, g_pos, g_surf = outs
    return (
        g_x.transpose(2, 0, 1, 3),
        g_wqkv,
        g_bqkv,
        g_wproj,
        g_bproj,
        g_gain,
        g_shift,
        g_pos.reshape(HEADS, 16, SLOTS).transpose(1, 0, 2),
        g_surf.transpose(2, 0, 1),
    )


def solution(mesh):
    in_specs = (P(None, "lat", "lon", None), P(None, "lat", "lon", None), P("lat", "lon")) + (P(),) * 8
    out_specs = (P(None, "lat", "lon", None),) + (P(),) * 8
    return jax.shard_map(on_device, mesh=mesh, in_specs=in_specs, out_specs=out_specs, check_vma=False)
```
